128 devices in a mesh: seq: 16 (over y, x), ret: 8 (over z, core).
Axes of the slice: x: 4, y: 4, z: 4, core: 2. Of those that a mesh axis runs over, the one named last changes fastest.
Arguments:
- queries: bfloat16 [12288, 4096], P('seq', 'ret'), may hold values from -4 to 4
- grad_ctx: bfloat16 [12288, 4096], P('seq', 'ret'), may hold values from -6 to 6
- neighbours: bfloat16 [256, 128, 896], P(('seq', 'ret')), may hold values from -6 to 6
- up_weight: bfloat16 [896, 3584], replicated, may hold values from -0.1875 to 0.1875
- down_weight: bfloat16 [3584, 896], replicated, may hold values from -0.09375 to 0.09375
- key_weight: bfloat16 [896, 4096], P(None, 'ret'), may hold values from -0.1875 to 0.1875
- value_weight: bfloat16 [896, 4096], P(None, 'ret'), may hold values from -0.1875 to 0.1875
- group_ids: int32 [192, 2], P('seq'), may hold values from 0 to 15, all different within a row; in each aligned block of 12 rows (0 to 11, 12 to 23, ...) at most 3 rows name the same one
- slot_ids: int32 [192, 2], P('seq'), may hold values from 0 to 15
Outputs:
- context: bfloat16 [12288, 4096], P('seq', 'ret')
- grad_queries: bfloat16 [12288, 4096], P('seq', 'ret')
- grad_encoded: bfloat16 [256, 128, 896], P(('seq', 'ret'))
- grad_key_weight: float32 [896, 4096], P('seq', 'ret')
- grad_value_weight: float32 [896, 4096], P('seq', 'ret')
The draws below stay inside these ranges and needn't reach their ends.
Inputs may be any that keep to these rules, and one draw needn't show every extreme that they name: `group_ids`: the two neighbours of a span lie on different indices of seq. Among the spans of one index of seq no index of seq is named more than 3 times, and in every draw some index of seq is named exactly 3 times by the spans of some index of seq.
All inputs are finite; a program needn't handle non-finite values.
Results may differ from the reference program's by a relative error of at most 0.018.
Values may be sent and summed in bfloat16 or wider, within the bound.
A program may use at most 192 MiB of HBM per device.

```python
import math
import jax
import jax.numpy as jnp
import numpy as np
from jax import lax

HEADS = 32
HD = 128
DE = 896
FFE = 3584
SPAN = 64
RLEN = 128
TOK_SEQ = 768
NB_DEV = 2
TOKENS = 12288
CH_G = 12
SPANS = 192
CAP = 3
NB_SEQ = 16
NEIGH = 256
HB = 4
N_SEQ = 16
N_RET = 8


def set_ends(values, key, smallest, high):
    longest = values.shape.index(max(values.shape))
    spots = []
    for shift in (0, 1):
        where = [jax.random.randint(jax.random.fold_in(key, axis), (), 0, length) for axis, length in enumerate(values.shape)]
        where[longest] = (where[longest] + shift) % values.shape[longest]
        spots.append(tuple(where))
    return values.at[spots[0]].set(smallest).at[spots[1]].set(high)


def block_scale(own_key, extent, pieces, least, largest):
    def one(dim, shards_of):
        steps = jax.random.uniform(jax.random.fold_in(jax.random.fold_in(own_key, 6), dim), (shards_of,), jnp.float32, least / len(pieces), largest / len(pieces))
        return jnp.repeat(jnp.exp(steps), extent[dim] // shards_of).reshape((-1,) + (1,) * (len(extent) - dim - 1))

    gain = one(*pieces[0])
    for cut in pieces[1:]:
        gain = gain * one(*cut)
    return gain


def shared_out(key, own, number, rows, count, top, limit, skew):
    sequence = jax.random.permutation(key, count)
    heavy_load, ordinary = load_shares(count, rows * top, limit, skew, True), load_shares(count, rows * top, limit, skew, False)
    places = jnp.arange(count)

    def named(lengths, rotation):
        used = int((lengths > 0).sum())
        fixed = max(1, used // 4)
        passed = fixed + (places - fixed + rotation * (used - fixed)) % max(1, count - fixed)
        return jnp.zeros((count,), jnp.int32).at[sequence[jnp.where(places < fixed, places, passed)]].set(jnp.asarray(lengths, jnp.int32))

    lengths = jnp.where(number % 4 == 0, named(heavy_load, number // 4), named(ordinary, number - number // 4 - 1))
    mixed = jax.random.permutation(jax.random.fold_in(own, 3), count)
    giver, receiver = mixed[0:count // 2 * 2:2], mixed[1:count // 2 * 2:2]
    slack = jnp.minimum(lengths[giver] - 1, limit - lengths[receiver]) // 2
    slack = jnp.where((giver == sequence[0]) | (receiver == sequence[0]) | (lengths[receiver] == 0), 0, jnp.maximum(slack, 0))
    passed = jax.random.randint(jax.random.fold_in(own, 4), (count // 2,), 0, 1 << 20) % (slack + 1)
    lengths = lengths.at[giver].add(-passed).at[receiver].add(passed)
    members = jnp.searchsorted(jnp.cumsum(lengths), jnp.arange(rows * top), side="right").astype(jnp.int32)
    table = members.reshape(top, rows).T
    table = table[jax.random.permutation(jax.random.fold_in(own, 1), rows)]
    rotation = jax.random.randint(jax.random.fold_in(own, 2), (rows, 1), 0, top)
    return jnp.take_along_axis(table, (jnp.arange(top)[None, :] + rotation) % top, axis=1)


def load_shares(count, total, reach, slope, full):
    weights = [(1 << 20) // math.isqrt(grade ** slope) + 1 for grade in range(1, count + 1)]
    largest = reach if full else min(reach, max(-(-total // count), total * weights[0] // sum(weights)))
    least = 1 if total - largest >= count - 1 else 0
    given, spare = [largest] + [least] * (count - 1), total - largest - least * (count - 1)
    while spare > 0:
        movable = [i for i in range(1, count) if given[i] < largest] or [i for i in range(1, count) if given[i] < reach]
        pool, budget = sum([weights[i] for i in movable]), spare
        for i in movable:
            addition = min(reach - given[i], max(1, budget * weights[i] // pool), spare)
            given[i] = given[i] + addition
            spare = spare - addition
    return np.array(given)


def normal_values(key, shape, width, reach, pieces=(), held_as=jnp.bfloat16):
    factor_of = block_scale(key, shape, pieces, -0.22, 0.18) if pieces else 1.0
    drawn = jax.random.normal(key, shape, jnp.float32) * width * factor_of
    return jnp.minimum(jnp.maximum(drawn, -reach), reach).astype(held_as)


def setup_inputs(seed: int = 0) -> dict:
    seeds = jax.random.split(jax.random.key(seed), 10)
    queries = normal_values(seeds[0], (TOKENS, HEADS * HD), 1.0, 4.0, ((0, 16), (1, 8)))
    grad_ctx = normal_values(seeds[1], (TOKENS, HEADS * HD), 1.0, 6.0, ((0, 16), (1, 8)))
    neighbours = normal_values(seeds[2], (NEIGH, RLEN, DE), 1.0, 6.0, ((0, 128),))
    up_weight = normal_values(seeds[3], (DE, FFE), DE ** -0.5, 0.1875)
    down_weight = normal_values(seeds[4], (FFE, DE), FFE ** -0.5, 0.09375)
    key_weight = normal_values(seeds[5], (DE, HEADS * HD), DE ** -0.5, 0.1875, ((1, 8),))
    value_weight = normal_values(seeds[6], (DE, HEADS * HD), DE ** -0.5, 0.1875, ((1, 8),))
    group_ids_keys = jax.random.split(jax.random.fold_in(seeds[7], 1), SPANS // CH_G)
    group_ids_turns = jax.random.permutation(jax.random.fold_in(seeds[7], 3), SPANS // CH_G)
    group_ids = jax.vmap(lambda own, number: shared_out(jax.random.fold_in(seeds[7], 2), own, number, CH_G, N_SEQ, 2, CAP, 2))(group_ids_keys, group_ids_turns).reshape((SPANS, 2))
    slot_ids = set_ends(jax.random.randint(seeds[8], (SPANS, 2), 0, NB_SEQ), jax.random.fold_in(seeds[8], 1), 0, NB_SEQ - 1).astype(jnp.int32)
    return dict(queries=queries, grad_ctx=grad_ctx, neighbours=neighbours, up_weight=up_weight, down_weight=down_weight, key_weight=key_weight, value_weight=value_weight, group_ids=group_ids, slot_ids=slot_ids)


def encode(raw_block, up_weight, down_weight):
    amount, row_len, feat_width = raw_block.shape
    inputs = raw_block.reshape(-1, feat_width).astype(jnp.float32)
    normed = (inputs * lax.rsqrt(lax.optimization_barrier(jnp.mean(inputs * inputs, axis=-1, keepdims=True)) + 1e-06)).astype(jnp.bfloat16)
    hidden = jax.nn.gelu(jnp.dot(normed, up_weight, preferred_element_type=jnp.float32)).astype(jnp.bfloat16)
    output = inputs + jnp.dot(hidden, down_weight, preferred_element_type=jnp.float32)
    return output.astype(jnp.bfloat16).reshape(amount, row_len, feat_width)

def attend(queries, key_req, value_req, grad_out):
    score_scale = 1.0 / math.sqrt(queries.shape[-1])
    query_f = queries.astype(jnp.float32)
    key_f = key_req.astype(jnp.float32)
    value_f = value_req.astype(jnp.float32)
    grad_f = grad_out.astype(jnp.float32)
    scores = jnp.einsum('cqhd,ckhd->chqk', query_f, key_f) * score_scale
    weights = jnp.exp(scores)
    weights = weights / lax.optimization_barrier(jnp.sum(weights, axis=-1, keepdims=True))
    probs = weights.astype(jnp.bfloat16)
    probs_f = probs.astype(jnp.float32)
    context = jnp.einsum('chqk,ckhd->cqhd', probs_f, value_f).astype(jnp.bfloat16)
    grad_probs = jnp.einsum('cqhd,ckhd->chqk', grad_f, value_f)
    mixed = (weights * (grad_probs - lax.optimization_barrier(jnp.sum(weights * grad_probs, axis=-1, keepdims=True))) * score_scale).astype(jnp.bfloat16)
    mixed_f = mixed.astype(jnp.float32)
    grad_queries = jnp.einsum('chqk,ckhd->cqhd', mixed_f, key_f).astype(jnp.bfloat16)
    grad_keys = jnp.einsum('chqk,cqhd->ckhd', mixed_f, query_f).astype(jnp.bfloat16)
    grad_values = jnp.einsum('chqk,cqhd->ckhd', probs_f, grad_f).astype(jnp.bfloat16)
    return (context, grad_queries, grad_keys, grad_values)

def reference(queries, grad_ctx, neighbours, up_weight, down_weight, key_weight, value_weight, group_ids, slot_ids):
    encoded = lax.map(lambda raw_block: encode(raw_block, up_weight, down_weight), neighbours.reshape(N_SEQ * N_RET, NB_DEV, RLEN, DE)).reshape(NEIGH, RLEN, DE)
    request_rows = (group_ids * NB_SEQ + slot_ids).astype(jnp.int32).reshape(-1)
    head_width = HB * HD
    requests = 2 * CH_G
    shape_q = (CH_G, SPAN, HB, HD)
    shape_kv = (CH_G, 2 * RLEN, HB, HD)
    grad_total = jnp.zeros((NEIGH, RLEN, DE), jnp.float32)
    contexts = []
    grad_qs = []
    key_grads = []
    value_grads = []
    for block_idx in range(N_RET):
        columns = slice(block_idx * head_width, (block_idx + 1) * head_width)
        key_block = key_weight[:, columns]
        value_block = value_weight[:, columns]
        query_block = queries[:, columns]
        grad_block = grad_ctx[:, columns]

        def one_group(carry, group_idx):
            grad_table, key_acc, value_acc = carry
            row_start = (group_idx * TOK_SEQ).astype(jnp.int32)
            query_rows = lax.dynamic_slice_in_dim(query_block, row_start, TOK_SEQ, 0)
            grad_rows = lax.dynamic_slice_in_dim(grad_block, row_start, TOK_SEQ, 0)
            wanted = lax.dynamic_slice_in_dim(request_rows, (group_idx * requests).astype(jnp.int32), requests, 0)
            picked = jnp.take(encoded, wanted, axis=0).reshape(-1, DE)
            key_flat = jnp.dot(picked, key_block, preferred_element_type=jnp.float32).astype(jnp.bfloat16)
            value_flat = jnp.dot(picked, value_block, preferred_element_type=jnp.float32).astype(jnp.bfloat16)
            context, grad_query, grad_keys, grad_values = attend(query_rows.reshape(shape_q), key_flat.reshape(shape_kv), value_flat.reshape(shape_kv), grad_rows.reshape(shape_q))
            grad_keys = grad_keys.reshape(-1, head_width)
            grad_values = grad_values.reshape(-1, head_width)
            key_acc = key_acc + jnp.dot(picked.astype(jnp.float32).T, grad_keys.astype(jnp.float32))
            value_acc = value_acc + jnp.dot(picked.astype(jnp.float32).T, grad_values.astype(jnp.float32))
            grad_part = (jnp.dot(grad_keys, key_block.T, preferred_element_type=jnp.float32) + jnp.dot(grad_values, value_block.T, preferred_element_type=jnp.float32)).astype(jnp.bfloat16)
            grad_table = grad_table.at[wanted].add(grad_part.reshape(requests, RLEN, DE).astype(jnp.float32))
            return ((grad_table, key_acc, value_acc), (context.reshape(TOK_SEQ, head_width), grad_query.reshape(TOK_SEQ, head_width)))
        start = (grad_total, jnp.zeros((DE, head_width), jnp.float32), jnp.zeros((DE, head_width), jnp.float32))
        (grad_total, key_acc, value_acc), (context, grad_query) = lax.scan(one_group, start, jnp.arange(N_SEQ, dtype=jnp.int32))
        contexts.append(context)
        grad_qs.append(grad_query)
        key_grads.append(key_acc)
        value_grads.append(value_acc)
    context_all = jnp.stack(contexts, axis=2).reshape(TOKENS, HEADS * HD)
    grad_q_all = jnp.stack(grad_qs, axis=2).reshape(TOKENS, HEADS * HD)
    return (context_all, grad_q_all, grad_total.astype(jnp.bfloat16), jnp.concatenate(key_grads, axis=1), jnp.concatenate(value_grads, axis=1))
```

```python
import functools
import math

import jax
import jax.numpy as jnp
from jax import lax
from jax.experimental import pallas as pl
from jax.experimental.pallas import tpu as pltpu
from jax.sharding import PartitionSpec as P

HD = 128
CAP = 3
MESH = pl.DeviceIdType.MESH
SIDE = 4
GROUPS = 16
RETS = 8
PIECES = 6
MIB = 1024 * 1024


def encode(raw_block, up_weight, down_weight):
    amount, row_len, feat_width = raw_block.shape
    inputs = raw_block.reshape(-1, feat_width).astype(jnp.float32)
    normed = (inputs * lax.rsqrt(jnp.mean(inputs * inputs, axis=-1, keepdims=True) + 1e-06)).astype(
        jnp.bfloat16
    )
    hidden = jax.nn.gelu(jnp.dot(normed, up_weight, preferred_element_type=jnp.float32)).astype(
        jnp.bfloat16
    )
    output = inputs + jnp.dot(hidden, down_weight, preferred_element_type=jnp.float32)
    return output.astype(jnp.bfloat16).reshape(amount, row_len, feat_width)


def ahead(seq, d):
    y, x = seq // SIDE, seq % SIDE
    return ((y + d // SIDE) % SIDE) * SIDE + (x + d % SIDE) % SIDE


def behind(seq, d):
    y, x = seq // SIDE, seq % SIDE
    return ((y + SIDE - d // SIDE) % SIDE) * SIDE + (x + SIDE - d % SIDE) % SIDE


def loop(low, high, step):
    def run(i, carry):
        step(i)
        return carry

    lax.fori_loop(low, high, run, 0)


def greet(seq, ret):
    barrier = pltpu.get_barrier_semaphore()

    def to_seq(d):
        pl.semaphore_signal(barrier, inc=1, device_id=(ahead(seq, d), ret), device_id_type=MESH)

    def to_ret(d):
        pl.semaphore_signal(barrier, inc=1, device_id=(seq, (ret + d) % RETS), device_id_type=MESH)

    loop(1, GROUPS, to_seq)
    loop(1, RETS, to_ret)
    pl.semaphore_wait(barrier, GROUPS + RETS - 2)


def remote(src, dst, send, recv, to):
    return pltpu.make_async_remote_copy(
        src_ref=src,
        dst_ref=dst,
        send_sem=send,
        recv_sem=recv,
        device_id=to,
        device_id_type=MESH,
    )


def fetch_kernel(
    enc,
    wanted,
    position,
    picked,
    served,
    table,
    arrived,
    leaving,
    own,
    served_s,
    id_send,
    id_recv,
    tab_send,
    tab_recv,
    seq_send,
    seq_recv,
    up_send,
    down_send,
    up_recv,
    down_recv,
    far_send,
    far_recv,
    sib_send,
    sib_recv,
    local,
):
    seq, ret = lax.axis_index("seq"), lax.axis_index("ret")
    z, core = ret // 2, ret % 2
    greet(seq, ret)

    def id_copy(d, dest, slot):
        return remote(wanted.at[dest], served.at[slot], id_send.at[d], id_recv.at[d], (dest, ret))

    def tab_copy(d, dest, slot):
        return remote(
            enc.at[:, dest],
            table.at[pl.ds(2 * slot, 2)],
            tab_send.at[d],
            tab_recv.at[d],
            (seq, dest),
        )

    loop(1, GROUPS, lambda d: id_copy(d, ahead(seq, d), seq).start())
    loop(1, RETS, lambda d: tab_copy(d, (ret + d) % RETS, ret).start())
    served[seq] = wanted[seq]
    table[2 * ret] = enc[0, ret]
    table[2 * ret + 1] = enc[1, ret]
    loop(1, GROUPS, lambda d: id_copy(d, ahead(seq, d), behind(seq, d)).wait())
    to_scalar = pltpu.make_async_copy(served, served_s, local.at[0])
    to_scalar.start()
    to_scalar.wait()
    loop(1, RETS, lambda d: tab_copy(d, (ret + d) % RETS, (ret + RETS - d) % RETS).wait())

    def seq_copy(d, dest, slot):
        return remote(
            leaving.at[dest], arrived.at[slot], seq_send.at[d], seq_recv.at[d], (dest, ret)
        )

    def serve(d):
        dest = ahead(seq, d)
        for k in range(CAP):
            leaving[dest, k] = table[jnp.maximum(served_s[dest, 0, k], 0)]
        seq_copy(d, dest, seq).start()

    loop(1, GROUPS, serve)
    for k in range(CAP):
        arrived[seq, k] = table[jnp.maximum(served_s[seq, 0, k], 0)]
    loop(1, GROUPS, lambda d: seq_copy(d, ahead(seq, d), behind(seq, d)).wait())

    requests = own.shape[0]

    def compact(i):
        at = position[i]
        own[i] = arrived[at // CAP, at % CAP]

    loop(0, requests, compact)

    size = requests // PIECES
    half = PIECES // 2
    above, below, facing = (z + 1) % SIDE, (z + SIDE - 1) % SIDE, (z + 2) % SIDE
    sibling = (seq, 2 * z + 1 - core)

    def rows(p):
        return pl.ds(p * size, size)

    def own_up(p, held):
        return remote(
            own.at[rows(p)],
            picked.at[rows(p), 2 * held + core],
            up_send.at[p],
            up_recv.at[p],
            (seq, 2 * above + core),
        )

    def own_down(p, held):
        return remote(
            own.at[rows(p)],
            picked.at[rows(p), 2 * held + core],
            down_send.at[p],
            down_recv.at[p],
            (seq, 2 * below + core),
        )

    def relay(p, held, to):
        return remote(
            picked.at[rows(p), 2 * held + core],
            picked.at[rows(p), 2 * held + core],
            far_send.at[p],
            far_recv.at[p],
            (seq, 2 * to + core),
        )

    def across(p, o, held, side):
        return remote(
            picked.at[rows(p), 2 * held + side],
            picked.at[rows(p), 2 * held + side],
            sib_send.at[o, p],
            sib_recv.at[o, p],
            sibling,
        )

    def own_across(p, side):
        return remote(
            own.at[rows(p)],
            picked.at[rows(p), 2 * z + side],
            sib_send.at[0, p],
            sib_recv.at[0, p],
            sibling,
        )

    for p in range(half):
        own_up(p, z).start()
        own_down(p + half, z).start()
    for p in range(half):
        own_up(p + half, z).start()
        own_down(p, z).start()
    for p in range(PIECES):
        own_across(p, core).start()
    keep = pltpu.make_async_copy(own, picked.at[:, ret], local.at[1])
    keep.start()
    for p in range(half):
        own_up(p, below).wait_recv()
        relay(p, below, above).start()
        across(p, 1, below, core).start()
        own_down(p + half, above).wait_recv()
        relay(p + half, above, below).start()
        across(p + half, 2, above, core).start()
    for p in range(half):
        own_up(p + half, below).wait_recv()
        across(p + half, 1, below, core).start()
        own_down(p, above).wait_recv()
        across(p, 2, above, core).start()
    for p in range(half):
        relay(p, facing, above).wait_recv()
        across(p, 3, facing, core).start()
        relay(p + half, facing, below).wait_recv()
        across(p + half, 3, facing, core).start()
    keep.wait()
    for p in range(PIECES):
        own_up(p, z).wait_send()
        own_down(p, z).wait_send()
        relay(p, below if p < half else above, above if p < half else below).wait_send()
        own_across(p, 1 - core).wait()
        across(p, 1, below, 1 - core).wait()
        across(p, 2, above, 1 - core).wait()
        across(p, 3, facing, 1 - core).wait()


def fetch(enc, wanted, position):
    requests = position.shape[0]
    feat = enc.shape[-1]
    enc = enc.reshape(2, RETS, 16, feat)
    dma = pltpu.SemaphoreType.DMA
    return pl.pallas_call(
        fetch_kernel,
        out_shape=(
            jax.ShapeDtypeStruct((requests, RETS, 16, feat), jnp.bfloat16),
            jax.ShapeDtypeStruct(wanted.shape, jnp.int32),
        ),
        in_specs=[
            pl.BlockSpec(memory_space=pltpu.VMEM),
            pl.BlockSpec(memory_space=pltpu.VMEM),
            pl.BlockSpec(memory_space=pltpu.SMEM),
        ],
        out_specs=(pl.BlockSpec(memory_space=pl.ANY), pl.BlockSpec(memory_space=pltpu.VMEM)),
        scratch_shapes=[
            pltpu.VMEM((2 * RETS, 16, feat), jnp.bfloat16),
            pltpu.VMEM((GROUPS, CAP, 16, feat), jnp.bfloat16),
            pltpu.VMEM((GROUPS, CAP, 16, feat), jnp.bfloat16),
            pltpu.VMEM((requests, 16, feat), jnp.bfloat16),
            pltpu.SMEM(wanted.shape, jnp.int32),
            dma((GROUPS,)),
            dma((GROUPS,)),
            dma((RETS,)),
            dma((RETS,)),
            dma((GROUPS,)),
            dma((GROUPS,)),
            dma((PIECES,)),
            dma((PIECES,)),
            dma((PIECES,)),
            dma((PIECES,)),
            dma((PIECES,)),
            dma((PIECES,)),
            dma((4, PIECES)),
            dma((4, PIECES)),
            dma((2,)),
        ],
        compiler_params=pltpu.CompilerParams(
            collective_id=0, has_side_effects=True, vmem_limit_bytes=32 * MIB
        ),
        name="fetch",
    )(enc, wanted, position)


NT = (((1,), (1,)), ((), ()))
TN = (((0,), (0,)), ((), ()))


def dot(a, b, dims=(((1,), (0,)), ((), ()))):
    return lax.dot_general(a, b, dims, preferred_element_type=jnp.float32)


def attend_kernel(
    picked, wk, wv, q, go, ctx, gq, part, gw, keys, values, gkeys, gvalues, acc_k, acc_v
):
    step = pl.program_id(0)
    spans = q.shape[0] // 64
    heads = q.shape[1] // HD
    scale = 1.0 / math.sqrt(HD)
    rows = picked[...]
    keys[...] = dot(rows, wk[...]).astype(jnp.bfloat16)
    values[...] = dot(rows, wv[...]).astype(jnp.bfloat16)
    for c in range(spans):
        tok = slice(64 * c, 64 * c + 64)
        row = slice(256 * c, 256 * c + 256)
        for h in range(heads):
            col = slice(HD * h, HD * h + HD)
            qh, gh = q[tok, col], go[tok, col]
            kh, vh = keys[row, col], values[row, col]
            weights = jnp.exp(dot(qh, kh, NT) * scale)
            weights = weights / jnp.sum(weights, axis=-1, keepdims=True)
            probs = weights.astype(jnp.bfloat16)
            ctx[tok, col] = dot(probs, vh).astype(jnp.bfloat16)
            gp = dot(gh, vh, NT)
            mixed = (
                weights * (gp - jnp.sum(weights * gp, axis=-1, keepdims=True)) * scale
            ).astype(jnp.bfloat16)
            gq[tok, col] = dot(mixed, kh).astype(jnp.bfloat16)
            gkeys[row, col] = dot(mixed, qh, TN).astype(jnp.bfloat16)
            gvalues[row, col] = dot(probs, gh, TN).astype(jnp.bfloat16)
    part[...] = (dot(gkeys[...], wk[...], NT) + dot(gvalues[...], wv[...], NT)).astype(jnp.bfloat16)
    add_k = dot(rows, gkeys[...], TN)
    add_v = dot(rows, gvalues[...], TN)

    @pl.when(step == 0)
    def _():
        acc_k[...] = add_k
        acc_v[...] = add_v

    @pl.when(step > 0)
    def _():
        acc_k[...] += add_k
        acc_v[...] += add_v

    @pl.when(step == pl.num_programs(0) - 1)
    def _():
        size = acc_k.shape[0] // GROUPS
        for j in range(GROUPS):
            own = slice(size * j, size * j + size)
            gw[j] = jnp.concatenate([acc_k[own], acc_v[own]], axis=0).astype(jnp.bfloat16)


def attend(picked, wk, wv, q, go, together=2):
    feat, width = wk.shape
    span_count = q.shape[0] // 64
    steps = span_count // together
    rows, toks = 256 * together, 64 * together
    whole = lambda i: (0, 0)
    along = lambda i: (i, 0)
    return pl.pallas_call(
        attend_kernel,
        grid=(steps,),
        out_shape=(
            jax.ShapeDtypeStruct(q.shape, jnp.bfloat16),
            jax.ShapeDtypeStruct(q.shape, jnp.bfloat16),
            jax.ShapeDtypeStruct(picked.shape, jnp.bfloat16),
            jax.ShapeDtypeStruct((GROUPS, 2 * feat // GROUPS, width), jnp.bfloat16),
        ),
        in_specs=[
            pl.BlockSpec((rows, feat), along),
            pl.BlockSpec((feat, width), whole),
            pl.BlockSpec((feat, width), whole),
            pl.BlockSpec((toks, width), along),
            pl.BlockSpec((toks, width), along),
        ],
        out_specs=(
            pl.BlockSpec((toks, width), along),
            pl.BlockSpec((toks, width), along),
            pl.BlockSpec((rows, feat), along),
            pl.BlockSpec((GROUPS, 2 * feat // GROUPS, width), lambda i: (0, 0, 0)),
        ),
        scratch_shapes=[
            pltpu.VMEM((rows, width), jnp.bfloat16),
            pltpu.VMEM((rows, width), jnp.bfloat16),
            pltpu.VMEM((rows, width), jnp.bfloat16),
            pltpu.VMEM((rows, width), jnp.bfloat16),
            pltpu.VMEM((feat, width), jnp.float32),
            pltpu.VMEM((feat, width), jnp.float32),
        ],
        compiler_params=pltpu.CompilerParams(
            dimension_semantics=("arbitrary",), vmem_limit_bytes=48 * MIB
        ),
        name="attend",
    )(picked, wk, wv, q, go)


def give_kernel(
    part,
    gw,
    served,
    source,
    home,
    gk_out,
    gv_out,
    acc,
    sib,
    near_up,
    near_down,
    far,
    total,
    leaving,
    arrived,
    table,
    wsum,
    w_send,
    w_recv,
    own_sem,
    sib_send,
    sib_recv,
    up_send,
    up_recv,
    down_send,
    down_recv,
    far_send,
    far_recv,
    seq_send,
    seq_recv,
    tab_send,
    tab_recv,
    keep,
):
    seq, ret = lax.axis_index("seq"), lax.axis_index("ret")
    z, core = ret // 2, ret % 2
    requests = total.shape[0]
    size = requests // PIECES
    half = PIECES // 2
    above, below = (z + 1) % SIDE, (z + SIDE - 1) % SIDE
    greet(seq, ret)

    def own_copy(o):
        return pltpu.make_async_copy(part.at[:, (z + o) % SIDE, core], acc.at[o], own_sem.at[o])

    def sib_copy(o):
        return remote(
            part.at[:, (z + o) % SIDE, 1 - core],
            sib.at[o],
            sib_send.at[o],
            sib_recv.at[o],
            (seq, 2 * z + 1 - core),
        )

    def w_copy(d, dest):
        return remote(gw.at[dest], wsum.at[d], w_send.at[d], w_recv.at[d], (dest, ret))

    for o in (2, 1, 3, 0):
        own_copy(o).start()
        sib_copy(o).start()
    loop(1, GROUPS, lambda d: w_copy(d, ahead(seq, d)).start())
    own_w = pltpu.make_async_copy(gw.at[seq], wsum.at[0], w_send.at[0])
    own_w.start()

    def rows(p):
        return pl.ds(p * size, size)

    def merge(o):
        own_copy(o).wait()
        sib_copy(o).wait_recv()

        def one(i):
            acc[o, i] = (acc[o, i].astype(jnp.float32) + sib[o, i].astype(jnp.float32)).astype(
                jnp.bfloat16
            )

        loop(0, requests, one)

    def add_far(o, p):
        def one(i):
            acc[o, i] = (acc[o, i].astype(jnp.float32) + far[i].astype(jnp.float32)).astype(
                jnp.bfloat16
            )

        loop(p * size, p * size + size, one)

    up_to, down_to = (seq, 2 * above + core), (seq, 2 * below + core)

    def far_copy(p):
        return remote(
            acc.at[2, rows(p)],
            far.at[rows(p)],
            far_send.at[p],
            far_recv.at[p],
            up_to if p < half else down_to,
        )

    def up_copy(p):
        return remote(acc.at[1, rows(p)], near_up.at[rows(p)], up_send.at[p], up_recv.at[p], up_to)

    def down_copy(p):
        return remote(
            acc.at[3, rows(p)], near_down.at[rows(p)], down_send.at[p], down_recv.at[p], down_to
        )

    merge(2)
    for p in range(half):
        far_copy(p).start()
        far_copy(p + half).start()
    merge(1)
    for p in range(half):
        up_copy(p + half).start()
    merge(3)
    for p in range(half):
        down_copy(p).start()
    merge(0)
    for p in range(half):
        far_copy(p).wait_recv()
        add_far(1, p)
        up_copy(p).start()
        far_copy(p + half).wait_recv()
        add_far(3, p + half)
        down_copy(p + half).start()
    for p in range(half):
        up_copy(p + half).wait_recv()
        down_copy(p).wait_recv()
    for p in range(half):
        up_copy(p).wait_recv()
        down_copy(p + half).wait_recv()

    def finish(i):
        total[i] = (
            acc[0, i].astype(jnp.float32)
            + near_up[i].astype(jnp.float32)
            + near_down[i].astype(jnp.float32)
        ).astype(jnp.bfloat16)

    loop(0, requests, finish)

    def seq_copy(d, dest, slot):
        return remote(
            leaving.at[dest], arrived.at[slot], seq_send.at[d], seq_recv.at[d], (dest, ret)
        )

    def give_back(d):
        dest = ahead(seq, d)
        for k in range(CAP):
            leaving[dest, k] = total[source[dest * CAP + k]]
        seq_copy(d, dest, seq).start()

    loop(1, GROUPS, give_back)
    for k in range(CAP):
        arrived[seq, k] = total[source[seq * CAP + k]]

    own_w.wait()
    loop(1, GROUPS, lambda d: w_copy(d, ahead(seq, d)).wait())
    rows_w = gk_out.shape[0]
    for c in range(0, gk_out.shape[1], 128):
        col = pl.ds(c, 128)
        w_total = wsum[0, :, col].astype(jnp.float32)
        for d in range(1, GROUPS):
            w_total = w_total + wsum[d, :, col].astype(jnp.float32)
        gk_out[:, col] = w_total[:rows_w]
        gv_out[:, col] = w_total[rows_w:]

    loop(1, GROUPS, lambda d: seq_copy(d, ahead(seq, d), behind(seq, d)).wait())

    def tab_copy(d, dest, slot):
        return remote(
            table.at[pl.ds(2 * dest, 2)],
            home.at[:, slot],
            tab_send.at[d],
            tab_recv.at[d],
            (seq, dest),
        )

    feat = total.shape[-1]

    def sum_slot(slot):
        def add(s, carry):
            for k in range(CAP):
                here = served[s, 0, k] == slot
                carry = carry + jnp.where(here, arrived[s, k].astype(jnp.float32), 0.0)
            return carry

        table[slot] = lax.fori_loop(0, GROUPS, add, jnp.zeros((16, feat), jnp.float32)).astype(
            jnp.bfloat16
        )

    def send_home(d):
        dest = (ret + d) % RETS
        sum_slot(2 * dest)
        sum_slot(2 * dest + 1)
        tab_copy(d, dest, ret).start()

    loop(1, RETS, send_home)
    sum_slot(2 * ret)
    sum_slot(2 * ret + 1)
    kept = pltpu.make_async_copy(table.at[pl.ds(2 * ret, 2)], home.at[:, ret], keep)
    kept.start()
    kept.wait()
    loop(1, RETS, lambda d: tab_copy(d, (ret + d) % RETS, (ret + RETS - d) % RETS).wait())
    for o in range(4):
        sib_copy(o).wait_send()
    for p in range(PIECES):
        far_copy(p).wait_send()
        up_copy(p).wait_send()
        down_copy(p).wait_send()


def give(part, gw, served, source):
    requests, feat = part.shape[0] // 128, part.shape[1]
    part = part.reshape(requests, SIDE, 2, 16, feat)
    _, rows_w, width = gw.shape
    dma = pltpu.SemaphoreType.DMA
    chunk = (requests, 16, feat)
    vmem = pl.BlockSpec(memory_space=pltpu.VMEM)
    home, gk, gv = pl.pallas_call(
        give_kernel,
        out_shape=(
            jax.ShapeDtypeStruct((2, RETS, 16, feat), jnp.bfloat16),
            jax.ShapeDtypeStruct((rows_w // 2, width), jnp.float32),
            jax.ShapeDtypeStruct((rows_w // 2, width), jnp.float32),
        ),
        in_specs=[
            pl.BlockSpec(memory_space=pl.ANY),
            pl.BlockSpec(memory_space=pl.ANY),
            pl.BlockSpec(memory_space=pltpu.SMEM),
            pl.BlockSpec(memory_space=pltpu.SMEM),
        ],
        out_specs=(vmem, vmem, vmem),
        scratch_shapes=[
            pltpu.VMEM((4,) + chunk, jnp.bfloat16),
            pltpu.VMEM((4,) + chunk, jnp.bfloat16),
            pltpu.VMEM(chunk, jnp.bfloat16),
            pltpu.VMEM(chunk, jnp.bfloat16),
            pltpu.VMEM(chunk, jnp.bfloat16),
            pltpu.VMEM(chunk, jnp.bfloat16),
            pltpu.VMEM((GROUPS, CAP, 16, feat), jnp.bfloat16),
            pltpu.VMEM((GROUPS, CAP, 16, feat), jnp.bfloat16),
            pltpu.VMEM((2 * RETS, 16, feat), jnp.bfloat16),
            pltpu.VMEM(gw.shape, jnp.bfloat16),
            dma((GROUPS,)),
            dma((GROUPS,)),
            dma((4,)),
            dma((4,)),
            dma((4,)),
            dma((PIECES,)),
            dma((PIECES,)),
            dma((PIECES,)),
            dma((PIECES,)),
            dma((PIECES,)),
            dma((PIECES,)),
            dma((GROUPS,)),
            dma((GROUPS,)),
            dma((RETS,)),
            dma((RETS,)),
            dma,
        ],
        compiler_params=pltpu.CompilerParams(
            collective_id=1, has_side_effects=True, vmem_limit_bytes=32 * MIB
        ),
        name="give",
    )(part, gw, served, source)
    return home.reshape(2, 128, feat), gk, gv


def body(
    queries,
    grad_ctx,
    neighbours,
    up_weight,
    down_weight,
    key_weight,
    value_weight,
    group_ids,
    slot_ids,
):
    targets, slots = group_ids.reshape(-1), slot_ids.reshape(-1)
    requests = targets.shape[0]
    order = jnp.arange(requests, dtype=jnp.int32)
    earlier = (targets[:, None] == targets[None, :]) & (order[None, :] < order[:, None])
    position = targets * CAP + jnp.sum(earlier.astype(jnp.int32), axis=1)
    match = position[:, None] == jnp.arange(GROUPS * CAP, dtype=jnp.int32)[None, :]
    wanted = jnp.sum(jnp.where(match, slots[:, None] + 1, 0), axis=0) - 1
    source = jnp.sum(jnp.where(match, order[:, None], 0), axis=0)
    wanted = jnp.pad(wanted.reshape(GROUPS, 1, CAP), ((0, 0), (0, 7), (0, 128 - CAP)))

    encoded = encode(neighbours, up_weight, down_weight)
    picked, served = fetch(encoded, wanted, position)
    feat = picked.shape[-1]
    context, grad_query, part, gw = attend(
        picked.reshape(-1, feat), key_weight, value_weight, queries, grad_ctx
    )
    grad_encoded, grad_key_w, grad_value_w = give(part, gw, served, source)
    return context, grad_query, grad_encoded, grad_key_w, grad_value_w


def solution(mesh):
    return jax.shard_map(
        body,
        mesh=mesh,
        in_specs=(
            P("seq", "ret"),
            P("seq", "ret"),
            P(("seq", "ret"), None, None),
            P(),
            P(),
            P(None, "ret"),
            P(None, "ret"),
            P("seq", None),
            P("seq", None),
        ),
        out_specs=(
            P("seq", "ret"),
            P("seq", "ret"),
            P(("seq", "ret"), None, None),
            P("seq", "ret"),
            P("seq", "ret"),
        ),
        check_vma=False,
    )
```

```python
import functools
import math

import jax
import jax.numpy as jnp
from jax import lax
from jax.experimental import pallas as pl
from jax.experimental.pallas import tpu as pltpu
from jax.sharding import PartitionSpec as P

HD = 128
CAP = 3
MESH = pl.DeviceIdType.MESH
SIDE = 4
GROUPS = 16
RETS = 8
STEPS = 6
BLOCKS = 7
EARLY = 2
MIB = 1024 * 1024


def ahead(seq, d):
    y, x = seq // SIDE, seq % SIDE
    return ((y + d // SIDE) % SIDE) * SIDE + (x + d % SIDE) % SIDE


def behind(seq, d):
    y, x = seq // SIDE, seq % SIDE
    return ((y + SIDE - d // SIDE) % SIDE) * SIDE + (x + SIDE - d % SIDE) % SIDE


def loop(low, high, step):
    def run(i, carry):
        step(i)
        return carry

    lax.fori_loop(low, high, run, 0)


def greet(seq, ret):
    barrier = pltpu.get_barrier_semaphore()

    def to_seq(d):
        pl.semaphore_signal(barrier, inc=1, device_id=(ahead(seq, d), ret), device_id_type=MESH)

    def to_ret(d):
        pl.semaphore_signal(barrier, inc=1, device_id=(seq, (ret + d) % RETS), device_id_type=MESH)

    loop(1, GROUPS, to_seq)
    loop(1, RETS, to_ret)
    pl.semaphore_wait(barrier, GROUPS + RETS - 2)


def remote(src, dst, send, recv, to):
    return pltpu.make_async_remote_copy(
        src_ref=src,
        dst_ref=dst,
        send_sem=send,
        recv_sem=recv,
        device_id=to,
        device_id_type=MESH,
    )


NT = (((1,), (1,)), ((), ()))
TN = (((0,), (0,)), ((), ()))


def dot(a, b, dims=(((1,), (0,)), ((), ()))):
    return lax.dot_general(a, b, dims, preferred_element_type=jnp.float32)


class Refs:
    def __init__(self, names, refs):
        self.__dict__.update(zip(names, refs))


def kernel(names, *refs):
    r = Refs(names, refs)
    seq, ret = lax.axis_index("seq"), lax.axis_index("ret")
    z, core = ret // 2, ret % 2
    above, below, facing = (z + 1) % SIDE, (z + SIDE - 1) % SIDE, (z + 2) % SIDE
    sibling = (seq, 2 * z + 1 - core)
    up_to, down_to = (seq, 2 * above + core), (seq, 2 * below + core)
    requests = r.own.shape[0]
    size = requests // STEPS
    half = size // 2
    feat = r.own.shape[-1]

    def up_load(j):
        width = r.up_w.shape[-1]
        return pltpu.make_async_copy(
            r.up_weight.at[:, pl.ds(j * width, width)], r.up_w.at[j], r.up_sem.at[j]
        )

    def down_load(j):
        depth = r.down_w.shape[1]
        return pltpu.make_async_copy(
            r.down_weight.at[pl.ds(j * depth, depth)], r.down_w.at[j], r.down_sem.at[j]
        )

    loads = [
        pltpu.make_async_copy(a, b, r.load_sem.at[i])
        for i, (a, b) in enumerate(
            (
                (r.key_weight, r.wk),
                (r.value_weight, r.wv),
                (r.queries, r.q),
                (r.grad_ctx, r.go),
                (r.neighbours.at[:, ret], r.raw.at[pl.ds(2 * ret, 2)]),
            )
        )
    ]
    loads[4].start()
    for j in range(BLOCKS):
        up_load(j).start()
        down_load(j).start()
    for i in range(4):
        loads[i].start()

    greet(seq, ret)

    def id_copy(d, dest, slot):
        return remote(
            r.wanted.at[dest], r.served.at[slot], r.id_send.at[d], r.id_recv.at[d], (dest, ret)
        )

    def raw_copy(d, dest, slot):
        return remote(
            r.neighbours.at[:, dest],
            r.raw.at[pl.ds(2 * slot, 2)],
            r.raw_send.at[d],
            r.raw_recv.at[d],
            (seq, dest),
        )

    loop(1, RETS, lambda d: raw_copy(d, (ret + d) % RETS, ret).start())
    loop(1, GROUPS, lambda d: id_copy(d, ahead(seq, d), seq).start())
    r.served[seq] = r.wanted[seq]
    loads[4].wait()
    loop(1, RETS, lambda d: raw_copy(d, (ret + d) % RETS, (ret + RETS - d) % RETS).wait())

    inputs = r.raw[...].reshape(-1, feat).astype(jnp.float32)
    normed = inputs * lax.rsqrt(jnp.mean(inputs * inputs, axis=-1, keepdims=True) + 1e-06)
    r.normed[...] = normed.astype(jnp.bfloat16)
    r.encoding[...] = inputs

    def feed(j):
        up_load(j).wait()
        hidden = jax.nn.gelu(dot(r.normed[...], r.up_w[j])).astype(jnp.bfloat16)
        down_load(j).wait()
        r.encoding[...] += dot(hidden, r.down_w[j])

    loop(0, BLOCKS, feed)
    r.table[...] = r.encoding[...].astype(jnp.bfloat16).reshape(r.table.shape)

    loop(1, GROUPS, lambda d: id_copy(d, ahead(seq, d), behind(seq, d)).wait())
    to_scalar = pltpu.make_async_copy(r.served, r.served_s, r.scalar_sem)
    to_scalar.start()
    to_scalar.wait()

    def seq_copy(d, dest, slot):
        return remote(
            r.leaving.at[dest], r.arrived.at[slot], r.seq_send.at[d], r.seq_recv.at[d], (dest, ret)
        )

    def serve(d):
        dest = ahead(seq, d)
        for k in range(CAP):
            r.leaving[dest, k] = r.table[jnp.maximum(r.served_s[dest, 0, k], 0)]
        seq_copy(d, dest, seq).start()

    loop(1, GROUPS, serve)
    for k in range(CAP):
        r.arrived[seq, k] = r.table[jnp.maximum(r.served_s[seq, 0, k], 0)]
    loop(1, GROUPS, lambda d: seq_copy(d, ahead(seq, d), behind(seq, d)).wait())

    def compact(i):
        at = r.position[i]
        r.own[i] = r.arrived[at // CAP, at % CAP]

    loop(0, requests, compact)
    for i in range(4):
        loads[i].wait()

    def rows(g, h):
        return pl.ds(g * size + h * half, half)

    def own_up(g, h, held):
        return remote(
            r.own.at[rows(g, h)],
            r.picked.at[rows(g, h), 2 * held + core],
            r.up_send.at[g, h],
            r.up_recv.at[g, h],
            up_to,
        )

    def own_down(g, h, held):
        return remote(
            r.own.at[rows(g, h)],
            r.picked.at[rows(g, h), 2 * held + core],
            r.dn_send.at[g, h],
            r.dn_recv.at[g, h],
            down_to,
        )

    def relay(g, h, held):
        return remote(
            r.picked.at[rows(g, h), 2 * held + core],
            r.picked.at[rows(g, h), 2 * held + core],
            r.far_send.at[g, h],
            r.far_recv.at[g, h],
            down_to if h else up_to,
        )

    def across(g, o, held, side):
        whole = pl.ds(g * size, size)
        source = r.picked.at[whole, 2 * held + side]
        return remote(
            r.own.at[whole] if o == 0 else source,
            source,
            r.sib_send.at[g, o],
            r.sib_recv.at[g, o],
            sibling,
        )

    def keep(g):
        whole = pl.ds(g * size, size)
        return pltpu.make_async_copy(
            r.own.at[whole], r.picked.at[whole, ret], r.keep_sem.at[g]
        )

    def send_own(g):
        own_up(g, 0, z).start()
        own_down(g, 1, z).start()
        own_up(g, 1, z).start()
        own_down(g, 0, z).start()
        across(g, 0, z, core).start()
        keep(g).start()

    def pass_on(g):
        own_up(g, 0, below).wait_recv()
        relay(g, 0, below).start()
        own_down(g, 1, above).wait_recv()
        relay(g, 1, above).start()
        own_up(g, 1, below).wait_recv()
        across(g, 1, below, core).start()
        own_down(g, 0, above).wait_recv()
        across(g, 2, above, core).start()

    def pass_far(g):
        relay(g, 0, facing).wait_recv()
        relay(g, 1, facing).wait_recv()
        across(g, 3, facing, core).start()

    def settle(g):
        for h in range(2):
            own_up(g, h, z).wait_send()
            own_down(g, h, z).wait_send()
            relay(g, h, above if h else below).wait_send()
        keep(g).wait()
        across(g, 0, z, 1 - core).wait()
        across(g, 1, below, 1 - core).wait()
        across(g, 2, above, 1 - core).wait()
        across(g, 3, facing, 1 - core).wait()

    def swap(g, o):
        whole = pl.ds(g * size, size)
        return remote(
            r.part.at[whole, (z + o) % SIDE, 1 - core],
            r.sib.at[o, whole],
            r.swap_send.at[g, o],
            r.swap_recv.at[g, o],
            sibling,
        )

    def far_copy(g, h):
        return remote(
            r.part.at[rows(g, h), facing, core],
            r.far.at[rows(g, h)],
            r.rfar_send.at[g, h],
            r.rfar_recv.at[g, h],
            down_to if h else up_to,
        )

    def up_copy(g, h):
        return remote(
            r.part.at[rows(g, h), above, core],
            r.near_up.at[rows(g, h)],
            r.rup_send.at[g, h],
            r.rup_recv.at[g, h],
            up_to,
        )

    def down_copy(g, h):
        return remote(
            r.part.at[rows(g, h), below, core],
            r.near_down.at[rows(g, h)],
            r.rdn_send.at[g, h],
            r.rdn_recv.at[g, h],
            down_to,
        )

    def merge(g, o):
        swap(g, o).wait_recv()
        at = (z + o) % SIDE

        def one(i):
            r.part[i, at, core] = (
                r.part[i, at, core].astype(jnp.float32) + r.sib[o, i].astype(jnp.float32)
            ).astype(jnp.bfloat16)

        loop(g * size, g * size + size, one)

    def merge_all(g):
        merge(g, 2)
        far_copy(g, 0).start()
        far_copy(g, 1).start()
        merge(g, 1)
        up_copy(g, 1).start()
        merge(g, 3)
        down_copy(g, 0).start()
        merge(g, 0)

    def add_far(g, h):
        far_copy(g, h).wait_recv()
        at = below if h else above

        def one(i):
            r.part[i, at, core] = (
                r.part[i, at, core].astype(jnp.float32) + r.far[i].astype(jnp.float32)
            ).astype(jnp.bfloat16)

        loop(g * size + h * half, g * size + h * half + half, one)
        (down_copy if h else up_copy)(g, h).start()

    def finish(g):
        for h in range(2):
            up_copy(g, h).wait_recv()
            down_copy(g, h).wait_recv()

        def one(i):
            r.total[i] = (
                r.part[i, z, core].astype(jnp.float32)
                + r.near_up[i].astype(jnp.float32)
                + r.near_down[i].astype(jnp.float32)
            ).astype(jnp.bfloat16)

        loop(g * size, g * size + size, one)
        for o in range(4):
            swap(g, o).wait_send()
        for h in range(2):
            far_copy(g, h).wait_send()
            up_copy(g, h).wait_send()
            down_copy(g, h).wait_send()

    def result_copies(g):
        tokens = pl.ds(g * (size * 32), size * 32)
        return (
            pltpu.make_async_copy(r.ctx.at[tokens], r.context.at[tokens], r.out_sem.at[g, 0]),
            pltpu.make_async_copy(r.gq.at[tokens], r.grad_query.at[tokens], r.out_sem.at[g, 1]),
        )

    def compute(g):
        attend(r, g, size)
        for o in (2, 1, 3, 0):
            swap(g, o).start()
        for copy in result_copies(g):
            copy.start()

    def at_step(g, step):
        @pl.when((g >= 0) & (g < STEPS))
        def _():
            step(g)

    for g in range(EARLY):
        send_own(g)

    def tick(t):
        at_step(t + EARLY, send_own)
        at_step(t, pass_on)
        at_step(t - 1, pass_far)
        at_step(t - 4, lambda g: (add_far(g, 0), add_far(g, 1)))
        at_step(t - 5, finish)
        at_step(t - 3, merge_all)
        at_step(t - 2, settle)
        at_step(t - 2, compute)

    loop(0, STEPS + 2, tick)

    for j in range(GROUPS):
        each = r.acc_k.shape[0] // GROUPS
        block = slice(each * j, each * j + each)
        r.gw[j] = jnp.concatenate([r.acc_k[block], r.acc_v[block]], axis=0).astype(jnp.bfloat16)

    def w_copy(d, dest):
        return remote(r.gw.at[dest], r.wsum.at[d], r.w_send.at[d], r.w_recv.at[d], (dest, ret))

    loop(1, GROUPS, lambda d: w_copy(d, ahead(seq, d)).start())
    r.wsum[0] = r.gw[seq]
    loop(STEPS + 2, STEPS + 5, tick)

    def back_copy(d, dest, slot):
        return remote(
            r.leaving_b.at[dest],
            r.arrived_b.at[slot],
            r.back_send.at[d],
            r.back_recv.at[d],
            (dest, ret),
        )

    def give_back(d):
        dest = ahead(seq, d)
        for k in range(CAP):
            r.leaving_b[dest, k] = r.total[r.source[dest * CAP + k]]
        back_copy(d, dest, seq).start()

    loop(1, GROUPS, give_back)
    for k in range(CAP):
        r.arrived_b[seq, k] = r.total[r.source[seq * CAP + k]]

    loop(1, GROUPS, lambda d: w_copy(d, ahead(seq, d)).wait())
    rows_w = r.gk_out.shape[0]
    for c in range(0, r.gk_out.shape[1], 128):
        col = pl.ds(c, 128)
        w_total = r.wsum[0, :, col].astype(jnp.float32)
        for d in range(1, GROUPS):
            w_total = w_total + r.wsum[d, :, col].astype(jnp.float32)
        r.gk_out[:, col] = w_total[:rows_w]
        r.gv_out[:, col] = w_total[rows_w:]

    loop(1, GROUPS, lambda d: back_copy(d, ahead(seq, d), behind(seq, d)).wait())

    def home_copy(d, dest, slot):
        return remote(
            r.table.at[pl.ds(2 * dest, 2)],
            r.home.at[:, slot],
            r.home_send.at[d],
            r.home_recv.at[d],
            (seq, dest),
        )

    def sum_slot(slot):
        def add(s, carry):
            for k in range(CAP):
                here = r.served_s[s, 0, k] == slot
                carry = carry + jnp.where(here, r.arrived_b[s, k].astype(jnp.float32), 0.0)
            return carry

        r.table[slot] = lax.fori_loop(0, GROUPS, add, jnp.zeros((16, feat), jnp.float32)).astype(
            jnp.bfloat16
        )

    def send_home(d):
        dest = (ret + d) % RETS
        sum_slot(2 * dest)
        sum_slot(2 * dest + 1)
        home_copy(d, dest, ret).start()

    loop(1, RETS, send_home)
    sum_slot(2 * ret)
    sum_slot(2 * ret + 1)
    for k in range(2):
        r.home[k, ret] = r.table[2 * ret + k]
    loop(1, RETS, lambda d: home_copy(d, (ret + d) % RETS, (ret + RETS - d) % RETS).wait())
    for g in range(STEPS):
        for copy in result_copies(g):
            copy.wait()


def attend(r, g, size):
    feat, width = r.wk.shape
    heads = width // HD
    spans = size // 2
    scale = 1.0 / math.sqrt(HD)
    rows = r.picked[pl.ds(g * size, size)].reshape(size * 128, feat)
    r.keys[...] = dot(rows, r.wk[...]).astype(jnp.bfloat16)
    r.values[...] = dot(rows, r.wv[...]).astype(jnp.bfloat16)
    for c in range(spans):
        tok = pl.ds(pl.multiple_of((g * spans + c) * 64, 64), 64)
        row = slice(256 * c, 256 * c + 256)
        for h in range(heads):
            col = slice(HD * h, HD * h + HD)
            qh, gh = r.q[tok, col], r.go[tok, col]
            kh, vh = r.keys[row, col], r.values[row, col]
            weights = jnp.exp(dot(qh, kh, NT) * scale)
            weights = weights / jnp.sum(weights, axis=-1, keepdims=True)
            probs = weights.astype(jnp.bfloat16)
            r.ctx[tok, col] = dot(probs, vh).astype(jnp.bfloat16)
            gp = dot(gh, vh, NT)
            mixed = (
                weights * (gp - jnp.sum(weights * gp, axis=-1, keepdims=True)) * scale
            ).astype(jnp.bfloat16)
            r.gq[tok, col] = dot(mixed, kh).astype(jnp.bfloat16)
            r.gkeys[row, col] = dot(mixed, qh, TN).astype(jnp.bfloat16)
            r.gvalues[row, col] = dot(probs, gh, TN).astype(jnp.bfloat16)
    part = dot(r.gkeys[...], r.wk[...], NT) + dot(r.gvalues[...], r.wv[...], NT)
    r.part[pl.ds(g * size, size)] = part.astype(jnp.bfloat16).reshape(size, SIDE, 2, 16, feat)
    add_k = dot(rows, r.gkeys[...], TN)
    add_v = dot(rows, r.gvalues[...], TN)

    @pl.when(g == 0)
    def _():
        r.acc_k[...] = add_k
        r.acc_v[...] = add_v

    @pl.when(g > 0)
    def _():
        r.acc_k[...] += add_k
        r.acc_v[...] += add_v


def fused(
    queries,
    grad_ctx,
    neighbours,
    up_weight,
    down_weight,
    key_weight,
    value_weight,
    wanted,
    position,
    source,
):
    feat, ffe = up_weight.shape
    requests = position.shape[0]
    tokens, width = queries.shape
    size = requests // STEPS
    bf, f32 = jnp.bfloat16, jnp.float32
    dma = pltpu.SemaphoreType.DMA
    slots = (GROUPS, CAP, 16, feat)
    chunk = (requests, 16, feat)
    any_, vmem, smem = (
        pl.BlockSpec(memory_space=s) for s in (pl.ANY, pltpu.VMEM, pltpu.SMEM)
    )
    ins = dict(
        queries=any_,
        grad_ctx=any_,
        neighbours=any_,
        up_weight=any_,
        down_weight=any_,
        key_weight=any_,
        value_weight=any_,
        wanted=vmem,
        position=smem,
        source=smem,
    )
    outs = dict(
        context=(any_, queries.shape, bf),
        grad_query=(any_, queries.shape, bf),
        home=(vmem, (2, RETS, 16, feat), bf),
        gk_out=(vmem, (feat // GROUPS, width), f32),
        gv_out=(vmem, (feat // GROUPS, width), f32),
    )
    scratch = dict(
        served=pltpu.VMEM(wanted.shape, jnp.int32),
        served_s=pltpu.SMEM(wanted.shape, jnp.int32),
        raw=pltpu.VMEM((2 * RETS, 16, feat), bf),
        normed=pltpu.VMEM((2 * RETS * 16, feat), bf),
        encoding=pltpu.VMEM((2 * RETS * 16, feat), f32),
        up_w=pltpu.VMEM((BLOCKS, feat, ffe // BLOCKS), bf),
        down_w=pltpu.VMEM((BLOCKS, ffe // BLOCKS, feat), bf),
        table=pltpu.VMEM((2 * RETS, 16, feat), bf),
        arrived=pltpu.VMEM(slots, bf),
        leaving=pltpu.VMEM(slots, bf),
        own=pltpu.VMEM(chunk, bf),
        picked=pltpu.VMEM((requests, RETS, 16, feat), bf),
        wk=pltpu.VMEM((feat, width), bf),
        wv=pltpu.VMEM((feat, width), bf),
        q=pltpu.VMEM(queries.shape, bf),
        go=pltpu.VMEM(queries.shape, bf),
        ctx=pltpu.VMEM(queries.shape, bf),
        gq=pltpu.VMEM(queries.shape, bf),
        keys=pltpu.VMEM((size * 128, width), bf),
        values=pltpu.VMEM((size * 128, width), bf),
        gkeys=pltpu.VMEM((size * 128, width), bf),
        gvalues=pltpu.VMEM((size * 128, width), bf),
        acc_k=pltpu.VMEM((feat, width), f32),
        acc_v=pltpu.VMEM((feat, width), f32),
        part=pltpu.VMEM((requests, SIDE, 2, 16, feat), bf),
        sib=pltpu.VMEM((SIDE,) + chunk, bf),
        far=pltpu.VMEM(chunk, bf),
        near_up=pltpu.VMEM(chunk, bf),
        near_down=pltpu.VMEM(chunk, bf),
        total=pltpu.VMEM(chunk, bf),
        leaving_b=pltpu.VMEM(slots, bf),
        arrived_b=pltpu.VMEM(slots, bf),
        gw=pltpu.VMEM((GROUPS, 2 * feat // GROUPS, width), bf),
        wsum=pltpu.VMEM((GROUPS, 2 * feat // GROUPS, width), bf),
        up_sem=dma((BLOCKS,)),
        down_sem=dma((BLOCKS,)),
        load_sem=dma((5,)),
        scalar_sem=dma,
        keep_sem=dma((STEPS,)),
        out_sem=dma((STEPS, 2)),
    )
    for name, shape in dict(
        id=(GROUPS,),
        raw=(RETS,),
        seq=(GROUPS,),
        up=(STEPS, 2),
        dn=(STEPS, 2),
        far=(STEPS, 2),
        sib=(STEPS, 4),
        swap=(STEPS, 4),
        rfar=(STEPS, 2),
        rup=(STEPS, 2),
        rdn=(STEPS, 2),
        w=(GROUPS,),
        back=(GROUPS,),
        home=(RETS,),
    ).items():
        scratch[name + "_send"] = dma(shape)
        scratch[name + "_recv"] = dma(shape)
    names = tuple(ins) + tuple(outs) + tuple(scratch)
    return pl.pallas_call(
        functools.partial(kernel, names),
        out_shape=tuple(jax.ShapeDtypeStruct(s, t) for _, s, t in outs.values()),
        in_specs=list(ins.values()),
        out_specs=tuple(s for s, _, _ in outs.values()),
        scratch_shapes=list(scratch.values()),
        compiler_params=pltpu.CompilerParams(
            collective_id=0, has_side_effects=True, vmem_limit_bytes=60 * MIB
        ),
        name="fused",
    )(
        queries,
        grad_ctx,
        neighbours.reshape(2, RETS, 16, feat),
        up_weight,
        down_weight,
        key_weight,
        value_weight,
        wanted,
        position,
        source,
    )


def body(
    queries,
    grad_ctx,
    neighbours,
    up_weight,
    down_weight,
    key_weight,
    value_weight,
    group_ids,
    slot_ids,
):
    targets, slots = group_ids.reshape(-1), slot_ids.reshape(-1)
    requests = targets.shape[0]
    order = jnp.arange(requests, dtype=jnp.int32)
    earlier = (targets[:, None] == targets[None, :]) & (order[None, :] < order[:, None])
    position = targets * CAP + jnp.sum(earlier.astype(jnp.int32), axis=1)
    match = position[:, None] == jnp.arange(GROUPS * CAP, dtype=jnp.int32)[None, :]
    wanted = jnp.sum(jnp.where(match, slots[:, None] + 1, 0), axis=0) - 1
    source = jnp.sum(jnp.where(match, order[:, None], 0), axis=0)
    wanted = jnp.pad(wanted.reshape(GROUPS, 1, CAP), ((0, 0), (0, 7), (0, 128 - CAP)))
    context, grad_query, home, grad_key_w, grad_value_w = fused(
        queries,
        grad_ctx,
        neighbours,
        up_weight,
        down_weight,
        key_weight,
        value_weight,
        wanted,
        position,
        source,
    )
    return context, grad_query, home.reshape(neighbours.shape), grad_key_w, grad_value_w


def solution(mesh):
    return jax.shard_map(
        body,
        mesh=mesh,
        in_specs=(
            P("seq", "ret"),
            P("seq", "ret"),
            P(("seq", "ret"), None, None),
            P(),
            P(),
            P(None, "ret"),
            P(None, "ret"),
            P("seq", None),
            P("seq", None),
        ),
        out_specs=(
            P("seq", "ret"),
            P("seq", "ret"),
            P(("seq", "ret"), None, None),
            P("seq", "ret"),
            P("seq", "ret"),
        ),
        check_vma=False,
    )
```

```python
import functools
import math

import jax
import jax.numpy as jnp
from jax import lax
from jax.experimental import pallas as pl
from jax.experimental.pallas import tpu as pltpu
from jax.sharding import PartitionSpec as P

HD = 128
CAP = 3
MESH = pl.DeviceIdType.MESH
SIDE = 4
GROUPS = 16
RETS = 8
STEPS = 6
BLOCKS = 7
CUT = 512
EARLY = 2
MIB = 1024 * 1024


def ahead(seq, d):
    y, x = seq // SIDE, seq % SIDE
    return ((y + d // SIDE) % SIDE) * SIDE + (x + d % SIDE) % SIDE


def behind(seq, d):
    y, x = seq // SIDE, seq % SIDE
    return ((y + SIDE - d // SIDE) % SIDE) * SIDE + (x + SIDE - d % SIDE) % SIDE


def loop(low, high, step):
    def run(i, carry):
        step(i)
        return carry

    lax.fori_loop(low, high, run, 0)


def greet(seq, ret):
    barrier = pltpu.get_barrier_semaphore()

    def to_seq(d):
        pl.semaphore_signal(barrier, inc=1, device_id=(ahead(seq, d), ret), device_id_type=MESH)

    def to_ret(d):
        pl.semaphore_signal(barrier, inc=1, device_id=(seq, (ret + d) % RETS), device_id_type=MESH)

    loop(1, GROUPS, to_seq)
    loop(1, RETS, to_ret)
    return lambda: pl.semaphore_wait(barrier, GROUPS + RETS - 2)


def remote(src, dst, send, recv, to):
    return pltpu.make_async_remote_copy(
        src_ref=src,
        dst_ref=dst,
        send_sem=send,
        recv_sem=recv,
        device_id=to,
        device_id_type=MESH,
    )


NT = (((1,), (1,)), ((), ()))
TN = (((0,), (0,)), ((), ()))


def dot(a, b, dims=(((1,), (0,)), ((), ()))):
    return lax.dot_general(a, b, dims, preferred_element_type=jnp.float32)


class Refs:
    def __init__(self, names, refs):
        self.__dict__.update(zip(names, refs))


def kernel(names, *refs):
    r = Refs(names, refs)
    seq, ret = lax.axis_index("seq"), lax.axis_index("ret")
    z, core = ret // 2, ret % 2
    above, below, facing = (z + 1) % SIDE, (z + SIDE - 1) % SIDE, (z + 2) % SIDE
    sibling = (seq, 2 * z + 1 - core)
    up_to, down_to = (seq, 2 * above + core), (seq, 2 * below + core)
    requests = r.own.shape[0]
    size = requests // STEPS
    half = size // 2
    feat = r.own.shape[-1]

    def up_load(j):
        width = r.up_w.shape[-1]
        return pltpu.make_async_copy(
            r.up_weight.at[:, pl.ds(j * width, width)], r.up_w.at[j], r.up_sem.at[j]
        )

    def down_load(j):
        depth = r.down_w.shape[1]
        return pltpu.make_async_copy(
            r.down_weight.at[pl.ds(j * depth, depth)], r.down_w.at[j], r.down_sem.at[j]
        )

    loads = [
        pltpu.make_async_copy(a, b, r.load_sem.at[i])
        for i, (a, b) in enumerate(
            (
                (r.key_weight, r.wk),
                (r.value_weight, r.wv),
                (r.queries, r.q),
                (r.grad_ctx, r.go),
                (r.neighbours, r.raw),
            )
        )
    ]
    loads[4].start()
    for j in range(BLOCKS):
        up_load(j).start()
        down_load(j).start()
    for i in range(4):
        loads[i].start()

    greeted = greet(seq, ret)

    targets = [r.group_ids[i % 2, i // 2] for i in range(requests)]
    slots = [r.slot_ids[i % 2, i // 2] for i in range(requests)]
    lane = lax.broadcasted_iota(jnp.int32, (8, 128), 1)
    wanted = jnp.full((8, 128), -1, jnp.int32)
    source = jnp.zeros((8, 128), jnp.int32)
    for i in range(requests):
        count = jnp.int32(0)
        for j in range(i):
            count += (targets[j] == targets[i]).astype(jnp.int32)
        at = targets[i] * CAP + count
        r.position[i] = at
        wanted = jnp.where(lane == at, slots[i], wanted)
        source = jnp.where(lane == at, i, source)
    r.wanted[...] = wanted
    r.source_v[...] = source
    to_source = pltpu.make_async_copy(r.source_v, r.source, r.scalar_sem.at[1])
    to_source.start()

    loads[4].wait()
    inputs = r.raw[...].reshape(-1, feat).astype(jnp.float32)
    normed = inputs * lax.rsqrt(jnp.mean(inputs * inputs, axis=-1, keepdims=True) + 1e-06)
    r.normed[...] = normed.astype(jnp.bfloat16)
    r.encoding[...] = inputs

    def feed(j):
        up_load(j).wait()
        hidden = jax.nn.gelu(dot(r.normed[...], r.up_w[j])).astype(jnp.bfloat16)
        down_load(j).wait()
        r.encoding[...] += dot(hidden, r.down_w[j])

    loop(0, BLOCKS, feed)
    r.enc[...] = r.encoding[...].astype(jnp.bfloat16).reshape(r.enc.shape)
    to_source.wait()
    greeted()

    def id_copy(d, dest, slot):
        return remote(r.wanted, r.served.at[slot], r.id_send.at[d], r.id_recv.at[d], (dest, ret))

    def slice_copy(d, dest, slot):
        return remote(
            r.enc.at[:, dest],
            r.table.at[pl.ds(2 * slot, 2)],
            r.raw_send.at[d],
            r.raw_recv.at[d],
            (seq, dest),
        )

    loop(1, RETS, lambda d: slice_copy(d, (ret + d) % RETS, ret).start())
    loop(1, GROUPS, lambda d: id_copy(d, ahead(seq, d), seq).start())
    r.served[seq] = wanted
    for k in range(2):
        r.table[2 * ret + k] = r.enc[k, ret]
    loop(1, GROUPS, lambda d: id_copy(d, ahead(seq, d), behind(seq, d)).wait())
    to_scalar = pltpu.make_async_copy(r.served, r.served_s, r.scalar_sem.at[0])
    to_scalar.start()
    to_scalar.wait()
    loop(1, RETS, lambda d: slice_copy(d, (ret + d) % RETS, (ret + RETS - d) % RETS).wait())

    def asked(s, k):
        return r.served_s[s, 0, seq * CAP + k]

    def seq_copy(d, dest, slot):
        return remote(
            r.leaving.at[dest], r.arrived.at[slot], r.seq_send.at[d], r.seq_recv.at[d], (dest, ret)
        )

    def serve(d):
        dest = ahead(seq, d)
        for k in range(CAP):
            r.leaving[dest, k] = r.table[jnp.maximum(asked(dest, k), 0)]
        seq_copy(d, dest, seq).start()

    loop(1, GROUPS, serve)
    for k in range(CAP):
        r.arrived[seq, k] = r.table[jnp.maximum(asked(seq, k), 0)]
    loop(1, GROUPS, lambda d: seq_copy(d, ahead(seq, d), behind(seq, d)).wait())

    def compact(i):
        at = r.position[i]
        r.own[i] = r.arrived[at // CAP, at % CAP]

    loop(0, requests, compact)
    for i in range(4):
        loads[i].wait()

    def rows(g, h):
        return pl.ds(g * size + h * half, half)

    def own_up(g, h, held):
        return remote(
            r.own.at[rows(g, h)],
            r.picked.at[rows(g, h), 2 * held + core],
            r.up_send.at[g, h],
            r.up_recv.at[g, h],
            up_to,
        )

    def own_down(g, h, held):
        return remote(
            r.own.at[rows(g, h)],
            r.picked.at[rows(g, h), 2 * held + core],
            r.dn_send.at[g, h],
            r.dn_recv.at[g, h],
            down_to,
        )

    def relay(g, h, held):
        return remote(
            r.picked.at[rows(g, h), 2 * held + core],
            r.picked.at[rows(g, h), 2 * held + core],
            r.far_send.at[g, h],
            r.far_recv.at[g, h],
            down_to if h else up_to,
        )

    def across(g, o, held, side):
        whole = pl.ds(g * size, size)
        source = r.picked.at[whole, 2 * held + side]
        return remote(
            r.own.at[whole] if o == 0 else source,
            source,
            r.sib_send.at[g, o],
            r.sib_recv.at[g, o],
            sibling,
        )

    def keep(g):
        whole = pl.ds(g * size, size)
        return pltpu.make_async_copy(
            r.own.at[whole], r.picked.at[whole, ret], r.keep_sem.at[g]
        )

    def send_own(g):
        own_up(g, 0, z).start()
        own_down(g, 1, z).start()
        own_up(g, 1, z).start()
        own_down(g, 0, z).start()
        across(g, 0, z, core).start()
        keep(g).start()

    def pass_on(g):
        own_up(g, 0, below).wait_recv()
        relay(g, 0, below).start()
        own_down(g, 1, above).wait_recv()
        relay(g, 1, above).start()
        own_up(g, 1, below).wait_recv()
        across(g, 1, below, core).start()
        own_down(g, 0, above).wait_recv()
        across(g, 2, above, core).start()

    def pass_far(g):
        relay(g, 0, facing).wait_recv()
        relay(g, 1, facing).wait_recv()
        across(g, 3, facing, core).start()

    def settle(g):
        for h in range(2):
            own_up(g, h, z).wait_send()
            own_down(g, h, z).wait_send()
            relay(g, h, above if h else below).wait_send()
        keep(g).wait()
        across(g, 0, z, 1 - core).wait()
        across(g, 1, below, 1 - core).wait()
        across(g, 2, above, 1 - core).wait()
        across(g, 3, facing, 1 - core).wait()

    cols = (pl.ds(0, CUT), pl.ds(CUT, feat - CUT))

    def swap(p, g, o):
        whole = pl.ds(g * size, size)
        return remote(
            r.part.at[whole, (z + o) % SIDE, 1 - core, :, cols[p]],
            r.sib.at[o, whole, :, cols[p]],
            r.swap_send.at[p, g, o],
            r.swap_recv.at[p, g, o],
            sibling,
        )

    def ring_copy(name, dst, at, to):
        send, recv = getattr(r, name + "_send"), getattr(r, name + "_recv")

        def copy(p, g, h):
            return remote(
                r.part.at[rows(g, h), at, core, :, cols[p]],
                dst.at[rows(g, h), :, cols[p]],
                send.at[p, g, h],
                recv.at[p, g, h],
                to(h),
            )

        return copy

    far_copy = ring_copy("rfar", r.far, facing, lambda h: down_to if h else up_to)
    up_copy = ring_copy("rup", r.near_up, above, lambda h: up_to)
    down_copy = ring_copy("rdn", r.near_down, below, lambda h: down_to)

    def merge(p, g, o):
        swap(p, g, o).wait_recv()
        at = (z + o) % SIDE
        whole = pl.ds(g * size, size)
        mine = r.part[whole, at, core, :, cols[p]].astype(jnp.float32)
        other = r.sib[o, whole, :, cols[p]].astype(jnp.float32)
        r.part[whole, at, core, :, cols[p]] = (mine + other).astype(jnp.bfloat16)

    def merge_all(p, g):
        merge(p, g, 2)
        far_copy(p, g, 0).start()
        far_copy(p, g, 1).start()
        merge(p, g, 1)
        up_copy(p, g, 1).start()
        merge(p, g, 3)
        down_copy(p, g, 0).start()
        merge(p, g, 0)

    def add_far(p, g):
        for h in range(2):
            far_copy(p, g, h).wait_recv()
            at = below if h else above
            mine = r.part[rows(g, h), at, core, :, cols[p]].astype(jnp.float32)
            other = r.far[rows(g, h), :, cols[p]].astype(jnp.float32)
            r.part[rows(g, h), at, core, :, cols[p]] = (mine + other).astype(jnp.bfloat16)
            (down_copy if h else up_copy)(p, g, h).start()

    def finish(p, g):
        for h in range(2):
            up_copy(p, g, h).wait_recv()
            down_copy(p, g, h).wait_recv()
        whole = pl.ds(g * size, size)
        r.total[whole, :, cols[p]] = (
            r.part[whole, z, core, :, cols[p]].astype(jnp.float32)
            + r.near_up[whole, :, cols[p]].astype(jnp.float32)
            + r.near_down[whole, :, cols[p]].astype(jnp.float32)
        ).astype(jnp.bfloat16)
        for o in range(4):
            swap(p, g, o).wait_send()
        for h in range(2):
            far_copy(p, g, h).wait_send()
            up_copy(p, g, h).wait_send()
            down_copy(p, g, h).wait_send()

    def project(p, g):
        gk, gv = r.up_w[g, : size * 128, :], r.down_w[g, :, : r.wk.shape[1]]
        part = dot(gk, r.wk[cols[p], :], NT) + dot(gv, r.wv[cols[p], :], NT)
        r.part[pl.ds(g * size, size), :, :, :, cols[p]] = part.astype(jnp.bfloat16).reshape(
            size, SIDE, 2, 16, part.shape[1]
        )
        for o in (2, 1, 3, 0):
            swap(p, g, o).start()

    def result_copies(g):
        tokens = pl.ds(g * (size * 32), size * 32)
        return (
            pltpu.make_async_copy(r.ctx.at[tokens], r.context.at[tokens], r.out_sem.at[g, 0]),
            pltpu.make_async_copy(r.gq.at[tokens], r.grad_query.at[tokens], r.out_sem.at[g, 1]),
        )

    def compute(g):
        attend(r, g, size)
        for copy in result_copies(g):
            copy.start()

    def at_step(g, step):
        @pl.when((g >= 0) & (g < STEPS))
        def _():
            step(g)

    for g in range(EARLY):
        send_own(g)

    def tick(t):
        at_step(t + EARLY, send_own)
        at_step(t, pass_on)
        at_step(t - 1, pass_far)
        at_step(t - 2, settle)
        at_step(t - 2, compute)

    loop(0, STEPS + 2, tick)

    y, x = seq // SIDE, seq % SIDE
    each = feat // GROUPS
    wide = r.acc_k.shape[1] // 2
    for j in range(GROUPS):
        block = slice(each * j, each * j + each)
        for h in range(2):
            col = slice(wide * h, wide * h + wide)
            r.gw[j // SIDE, j % SIDE, h] = jnp.concatenate(
                [r.acc_k[block, col], r.acc_v[block, col]], axis=0
            ).astype(jnp.bfloat16)

    def along_x(d):
        return (y * SIDE + (x + d) % SIDE, ret)

    def along_y(d):
        return (((y + d) % SIDE) * SIDE + x, ret)

    def w_copy(h, d):
        return remote(
            r.gw.at[(y + d) % SIDE, :, 1] if h else r.gw.at[:, (x + d) % SIDE, 0],
            r.w_in.at[h, d],
            r.w_send.at[h, d],
            r.w_recv.at[h, d],
            along_y(d) if h else along_x(d),
        )

    def w_last(h, d):
        return remote(
            r.w_half.at[h, (x + d) % SIDE if h else (y + d) % SIDE],
            r.w_end.at[h, d],
            r.w2_send.at[h, d],
            r.w2_recv.at[h, d],
            along_x(d) if h else along_y(d),
        )

    def w_middle():
        for h in range(2):
            for d in range(1, SIDE):
                w_copy(h, d).wait()
            for j in range(SIDE):
                mine = r.gw[y, j, 1] if h else r.gw[j, x, 0]
                summed = mine.astype(jnp.float32)
                for d in range(1, SIDE):
                    summed = summed + r.w_in[h, d, j].astype(jnp.float32)
                r.w_half[h, j] = summed.astype(jnp.bfloat16)
            for d in range(1, SIDE):
                w_last(h, d).start()

    for d in range(1, SIDE):
        for h in range(2):
            w_copy(h, d).start()

    def back_copy(p, d, dest, slot):
        return remote(
            r.leaving.at[dest, :, :, cols[p]],
            r.arrived_b.at[slot, :, :, cols[p]],
            r.back_send.at[p, d],
            r.back_recv.at[p, d],
            (dest, ret),
        )

    def give_back(p):
        def give(d):
            dest = ahead(seq, d)
            for k in range(CAP):
                r.leaving[dest, k, :, cols[p]] = r.total[r.source[0, dest * CAP + k], :, cols[p]]
            back_copy(p, d, dest, seq).start()

        loop(1, GROUPS, give)
        for k in range(CAP):
            r.arrived_b[seq, k, :, cols[p]] = r.total[r.source[0, seq * CAP + k], :, cols[p]]

    def tock(t):
        for p in range(2):
            begin = p * STEPS
            at_step(t - begin - 5, lambda g: finish(p, g))
            at_step(t - begin - 3, lambda g: add_far(p, g))
            at_step(t - begin - 1, lambda g: merge_all(p, g))
            at_step(t - begin, lambda g: project(p, g))
        pl.when(t == STEPS)(w_middle)
        pl.when(t == STEPS + 4)(lambda: give_back(0))

    loop(0, 2 * STEPS + 5, tock)
    give_back(1)

    row = lax.broadcasted_iota(jnp.int32, r.pick.shape, 0)
    col = lax.broadcasted_iota(jnp.int32, r.pick.shape, 1)
    place = lax.broadcasted_iota(jnp.int32, (1, r.pick.shape[1]), 1) // 16
    owner = jnp.full(place.shape, -1, jnp.int32)
    for s in range(GROUPS):
        for k in range(CAP):
            owner = jnp.where(place == s * CAP + k, asked(s, k), owner)
    r.pick[...] = jnp.where((row // 16 == owner) & (row % 16 == col % 16), 1.0, 0.0).astype(
        jnp.bfloat16
    )

    def home_copy(p, d, dest, slot):
        return remote(
            r.table.at[pl.ds(2 * dest, 2), :, cols[p]],
            r.home.at[:, slot, :, cols[p]],
            r.home_send.at[p, d],
            r.home_recv.at[p, d],
            (seq, dest),
        )

    def go_home(p):
        loop(1, GROUPS, lambda d: back_copy(p, d, ahead(seq, d), behind(seq, d)).wait())
        arrived = r.arrived_b[:, :, :, cols[p]]
        summed = dot(r.pick[...], arrived.reshape(r.pick.shape[1], arrived.shape[-1]))
        r.table[:, :, cols[p]] = summed.astype(jnp.bfloat16).reshape(
            2 * RETS, 16, arrived.shape[-1]
        )
        loop(1, RETS, lambda d: home_copy(p, d, (ret + d) % RETS, ret).start())
        for k in range(2):
            r.home[k, ret, :, cols[p]] = r.table[2 * ret + k, :, cols[p]]

    go_home(0)
    for h in range(2):
        summed = r.w_half[h, x if h else y].astype(jnp.float32)
        for d in range(1, SIDE):
            w_last(h, d).wait()
            summed = summed + r.w_end[h, d].astype(jnp.float32)
        r.gk_out[:, wide * h : wide * h + wide] = summed[:each]
        r.gv_out[:, wide * h : wide * h + wide] = summed[each:]
    go_home(1)
    for p in range(2):
        loop(
            1,
            RETS,
            lambda d: home_copy(p, d, (ret + d) % RETS, (ret + RETS - d) % RETS).wait(),
        )
    for g in range(STEPS):
        for copy in result_copies(g):
            copy.wait()


def attend(r, g, size):
    feat, width = r.wk.shape
    heads = width // HD
    spans = size // 2
    scale = 1.0 / math.sqrt(HD)
    rows = r.picked[pl.ds(g * size, size)].reshape(size * 128, feat)
    r.keys[...] = dot(rows, r.wk[...]).astype(jnp.bfloat16)
    r.values[...] = dot(rows, r.wv[...]).astype(jnp.bfloat16)
    gkeys, gvalues = r.up_w.at[g, : size * 128], r.down_w.at[g, :, :width]
    for c in range(spans):
        tok = pl.ds(pl.multiple_of((g * spans + c) * 64, 64), 64)
        row = slice(256 * c, 256 * c + 256)
        cols = [slice(HD * h, HD * h + HD) for h in range(heads)]
        scores = [dot(r.q[tok, col], r.keys[row, col], NT) for col in cols]
        gps = [dot(r.go[tok, col], r.values[row, col], NT) for col in cols]
        weights = [jnp.exp(s * scale) for s in scores]
        weights = [w / jnp.sum(w, axis=-1, keepdims=True) for w in weights]
        probs = [w.astype(jnp.bfloat16) for w in weights]
        mixed = [
            (w * (gp - jnp.sum(w * gp, axis=-1, keepdims=True)) * scale).astype(jnp.bfloat16)
            for w, gp in zip(weights, gps)
        ]
        for col, p, m in zip(cols, probs, mixed):
            r.ctx[tok, col] = dot(p, r.values[row, col]).astype(jnp.bfloat16)
            r.gq[tok, col] = dot(m, r.keys[row, col]).astype(jnp.bfloat16)
            gkeys[row, col] = dot(m, r.q[tok, col], TN).astype(jnp.bfloat16)
            gvalues[row, col] = dot(p, r.go[tok, col], TN).astype(jnp.bfloat16)
    add_k = dot(rows, gkeys[...], TN)
    add_v = dot(rows, gvalues[...], TN)

    @pl.when(g == 0)
    def _():
        r.acc_k[...] = add_k
        r.acc_v[...] = add_v

    @pl.when(g > 0)
    def _():
        r.acc_k[...] += add_k
        r.acc_v[...] += add_v


def fused(
    queries,
    grad_ctx,
    neighbours,
    up_weight,
    down_weight,
    key_weight,
    value_weight,
    group_ids,
    slot_ids,
):
    feat, ffe = up_weight.shape
    requests = group_ids.shape[0] * group_ids.shape[1]
    tokens, width = queries.shape
    size = requests // STEPS
    bf, f32 = jnp.bfloat16, jnp.float32
    dma = pltpu.SemaphoreType.DMA
    slots = (GROUPS, CAP, 16, feat)
    chunk = (requests, 16, feat)
    block = (2 * feat // GROUPS, width // 2)
    any_, vmem, smem = (
        pl.BlockSpec(memory_space=s) for s in (pl.ANY, pltpu.VMEM, pltpu.SMEM)
    )
    ins = dict(
        queries=any_,
        grad_ctx=any_,
        neighbours=any_,
        up_weight=any_,
        down_weight=any_,
        key_weight=any_,
        value_weight=any_,
        group_ids=smem,
        slot_ids=smem,
    )
    outs = dict(
        context=(any_, queries.shape, bf),
        grad_query=(any_, queries.shape, bf),
        home=(vmem, (2, RETS, 16, feat), bf),
        gk_out=(vmem, (feat // GROUPS, width), f32),
        gv_out=(vmem, (feat // GROUPS, width), f32),
    )
    scratch = dict(
        wanted=pltpu.VMEM((8, 128), jnp.int32),
        source_v=pltpu.VMEM((8, 128), jnp.int32),
        source=pltpu.SMEM((8, 128), jnp.int32),
        position=pltpu.SMEM((requests,), jnp.int32),
        served=pltpu.VMEM((GROUPS, 8, 128), jnp.int32),
        served_s=pltpu.SMEM((GROUPS, 8, 128), jnp.int32),
        raw=pltpu.VMEM((2, RETS, 16, feat), bf),
        enc=pltpu.VMEM((2, RETS, 16, feat), bf),
        normed=pltpu.VMEM((2 * RETS * 16, feat), bf),
        encoding=pltpu.VMEM((2 * RETS * 16, feat), f32),
        up_w=pltpu.VMEM((BLOCKS, feat, ffe // BLOCKS), bf),
        down_w=pltpu.VMEM((BLOCKS, ffe // BLOCKS, feat), bf),
        table=pltpu.VMEM((2 * RETS, 16, feat), bf),
        arrived=pltpu.VMEM(slots, bf),
        leaving=pltpu.VMEM(slots, bf),
        own=pltpu.VMEM(chunk, bf),
        picked=pltpu.VMEM((requests, RETS, 16, feat), bf),
        wk=pltpu.VMEM((feat, width), bf),
        wv=pltpu.VMEM((feat, width), bf),
        q=pltpu.VMEM(queries.shape, bf),
        go=pltpu.VMEM(queries.shape, bf),
        ctx=pltpu.VMEM(queries.shape, bf),
        gq=pltpu.VMEM(queries.shape, bf),
        keys=pltpu.VMEM((size * 128, width), bf),
        values=pltpu.VMEM((size * 128, width), bf),
        acc_k=pltpu.VMEM((feat, width), f32),
        acc_v=pltpu.VMEM((feat, width), f32),
        part=pltpu.VMEM((requests, SIDE, 2, 16, feat), bf),
        sib=pltpu.VMEM((SIDE,) + chunk, bf),
        far=pltpu.VMEM(chunk, bf),
        near_up=pltpu.VMEM(chunk, bf),
        near_down=pltpu.VMEM(chunk, bf),
        total=pltpu.VMEM(chunk, bf),
        arrived_b=pltpu.VMEM(slots, bf),
        gw=pltpu.VMEM((SIDE, SIDE, 2) + block, bf),
        w_in=pltpu.VMEM((2, SIDE, SIDE) + block, bf),
        w_half=pltpu.VMEM((2, SIDE) + block, bf),
        w_end=pltpu.VMEM((2, SIDE) + block, bf),
        pick=pltpu.VMEM((2 * RETS * 16, GROUPS * CAP * 16), bf),
        up_sem=dma((BLOCKS,)),
        down_sem=dma((BLOCKS,)),
        load_sem=dma((5,)),
        scalar_sem=dma((2,)),
        keep_sem=dma((STEPS,)),
        out_sem=dma((STEPS, 2)),
    )
    for name, shape in dict(
        id=(GROUPS,),
        raw=(RETS,),
        seq=(GROUPS,),
        up=(STEPS, 2),
        dn=(STEPS, 2),
        far=(STEPS, 2),
        sib=(STEPS, 4),
        swap=(2, STEPS, 4),
        rfar=(2, STEPS, 2),
        rup=(2, STEPS, 2),
        rdn=(2, STEPS, 2),
        w=(2, SIDE),
        w2=(2, SIDE),
        back=(2, GROUPS),
        home=(2, RETS),
    ).items():
        scratch[name + "_send"] = dma(shape)
        scratch[name + "_recv"] = dma(shape)
    names = tuple(ins) + tuple(outs) + tuple(scratch)
    return pl.pallas_call(
        functools.partial(kernel, names),
        out_shape=tuple(jax.ShapeDtypeStruct(s, t) for _, s, t in outs.values()),
        in_specs=list(ins.values()),
        out_specs=tuple(s for s, _, _ in outs.values()),
        scratch_shapes=list(scratch.values()),
        compiler_params=pltpu.CompilerParams(
            collective_id=0, has_side_effects=True, vmem_limit_bytes=60 * MIB
        ),
        name="fused",
    )(
        queries,
        grad_ctx,
        neighbours.reshape(2, RETS, 16, feat),
        up_weight,
        down_weight,
        key_weight,
        value_weight,
        group_ids,
        slot_ids,
    )


def deliver_kernel(*refs):
    count = len(refs) // 3
    sems = refs[-1]
    incoming = [
        pltpu.make_async_copy(refs[i], refs[2 * count + i], sems.at[0, i]) for i in range(count)
    ]
    outgoing = [
        pltpu.make_async_copy(refs[2 * count + i], refs[count + i], sems.at[1, i])
        for i in range(count)
    ]
    for copy in incoming:
        copy.start()
    for i in range(count):
        incoming[i].wait()
        outgoing[i].start()
    for copy in outgoing:
        copy.wait()


def deliver(arrays):
    any_ = pl.BlockSpec(memory_space=pl.ANY)
    return pl.pallas_call(
        deliver_kernel,
        out_shape=tuple(jax.ShapeDtypeStruct(a.shape, a.dtype) for a in arrays),
        in_specs=[any_] * len(arrays),
        out_specs=(any_,) * len(arrays),
        scratch_shapes=[pltpu.VMEM(a.shape, a.dtype) for a in arrays]
        + [pltpu.SemaphoreType.DMA((2, len(arrays)))],
        name="deliver",
    )(*arrays)


def body(
    queries,
    grad_ctx,
    neighbours,
    up_weight,
    down_weight,
    key_weight,
    value_weight,
    group_ids,
    slot_ids,
):
    context, grad_query, home, grad_key_w, grad_value_w = deliver(
        fused(
            queries,
            grad_ctx,
            neighbours,
            up_weight,
            down_weight,
            key_weight,
            value_weight,
            group_ids.T,
            slot_ids.T,
        )
    )
    return context, grad_query, home.reshape(neighbours.shape), grad_key_w, grad_value_w


def solution(mesh):
    return jax.shard_map(
        body,
        mesh=mesh,
        in_specs=(
            P("seq", "ret"),
            P("seq", "ret"),
            P(("seq", "ret"), None, None),
            P(),
            P(),
            P(None, "ret"),
            P(None, "ret"),
            P("seq", None),
            P("seq", None),
        ),
        out_specs=(
            P("seq", "ret"),
            P("seq", "ret"),
            P(("seq", "ret"), None, None),
            P("seq", "ret"),
            P("seq", "ret"),
        ),
        check_vma=False,
    )
```

```python
import functools
import math

import jax
import jax.numpy as jnp
from jax import lax
from jax.experimental import pallas as pl
from jax.experimental.pallas import tpu as pltpu
from jax.sharding import PartitionSpec as P

HD = 128
CAP = 3
MESH = pl.DeviceIdType.MESH
SIDE = 4
GROUPS = 16
RETS = 8
STEPS = 6
BLOCKS = 7
CUT = 512
EARLY = 3
LAG_FAR = 1
LAG_USE = 2
MIX = 3
MIB = 1024 * 1024


def ahead(seq, d):
    y, x = seq // SIDE, seq % SIDE
    return ((y + d // SIDE) % SIDE) * SIDE + (x + d % SIDE) % SIDE


def behind(seq, d):
    y, x = seq // SIDE, seq % SIDE
    return ((y + SIDE - d // SIDE) % SIDE) * SIDE + (x + SIDE - d % SIDE) % SIDE


def each_group(step):
    loop(1, GROUPS, lambda d: step(d * MIX % GROUPS))


def loop(low, high, step):
    def run(i, carry):
        step(i)
        return carry

    lax.fori_loop(low, high, run, 0)


def greet(seq, ret):
    barrier = pltpu.get_barrier_semaphore()

    def to_seq(d):
        pl.semaphore_signal(barrier, inc=1, device_id=(ahead(seq, d), ret), device_id_type=MESH)

    def to_ret(d):
        pl.semaphore_signal(barrier, inc=1, device_id=(seq, (ret + d) % RETS), device_id_type=MESH)

    loop(1, GROUPS, to_seq)
    loop(1, RETS, to_ret)
    return lambda: pl.semaphore_wait(barrier, GROUPS + RETS - 2)


def remote(src, dst, send, recv, to):
    return pltpu.make_async_remote_copy(
        src_ref=src,
        dst_ref=dst,
        send_sem=send,
        recv_sem=recv,
        device_id=to,
        device_id_type=MESH,
    )


NT = (((1,), (1,)), ((), ()))
TN = (((0,), (0,)), ((), ()))


def dot(a, b, dims=(((1,), (0,)), ((), ()))):
    return lax.dot_general(a, b, dims, preferred_element_type=jnp.float32)


class Refs:
    def __init__(self, names, refs):
        self.__dict__.update(zip(names, refs))


def kernel(names, *refs):
    r = Refs(names, refs)
    seq, ret = lax.axis_index("seq"), lax.axis_index("ret")
    z, core = ret // 2, ret % 2
    above, below, facing = (z + 1) % SIDE, (z + SIDE - 1) % SIDE, (z + 2) % SIDE
    sibling = (seq, 2 * z + 1 - core)
    up_to, down_to = (seq, 2 * above + core), (seq, 2 * below + core)
    requests = r.own.shape[0]
    size = requests // STEPS
    half = size // 2
    feat = r.own.shape[-1]

    def up_load(j):
        width = r.up_w.shape[-1]
        return pltpu.make_async_copy(
            r.up_weight.at[:, pl.ds(j * width, width)], r.up_w.at[j], r.up_sem.at[j]
        )

    def down_load(j):
        depth = r.down_w.shape[1]
        return pltpu.make_async_copy(
            r.down_weight.at[pl.ds(j * depth, depth)], r.down_w.at[j], r.down_sem.at[j]
        )

    loads = [
        pltpu.make_async_copy(a, b, r.load_sem.at[i])
        for i, (a, b) in enumerate(
            (
                (r.key_weight, r.wk),
                (r.value_weight, r.wv),
                (r.queries, r.q),
                (r.grad_ctx, r.go),
                (r.neighbours.at[:, ret], r.raw.at[pl.ds(2 * ret, 2)]),
            )
        )
    ]
    loads[4].start()
    for j in range(BLOCKS):
        up_load(j).start()
        down_load(j).start()
    for i in range(4):
        loads[i].start()

    greeted = greet(seq, ret)

    targets = [r.group_ids[i % 2, i // 2] for i in range(requests)]
    slots = [r.slot_ids[i % 2, i // 2] for i in range(requests)]
    lane = lax.broadcasted_iota(jnp.int32, (8, 128), 1)
    wanted = jnp.full((8, 128), -1, jnp.int32)
    source = jnp.zeros((8, 128), jnp.int32)
    for i in range(requests):
        count = jnp.int32(0)
        for j in range(i):
            count += (targets[j] == targets[i]).astype(jnp.int32)
        at = targets[i] * CAP + count
        r.position[i] = at
        wanted = jnp.where(lane == at, slots[i], wanted)
        source = jnp.where(lane == at, i, source)
    r.wanted[...] = wanted
    r.source_v[...] = source
    to_source = pltpu.make_async_copy(r.source_v, r.source, r.scalar_sem.at[1])
    to_source.start()

    def id_copy(d, dest, slot):
        return remote(r.wanted, r.served.at[slot], r.id_send.at[d], r.id_recv.at[d], (dest, ret))

    def raw_copy(d, dest, slot):
        return remote(
            r.neighbours.at[:, dest],
            r.raw.at[pl.ds(2 * slot, 2)],
            r.raw_send.at[d],
            r.raw_recv.at[d],
            (seq, dest),
        )

    greeted()
    loop(1, RETS, lambda d: raw_copy(d, (ret + d) % RETS, ret).start())
    loop(1, GROUPS, lambda d: id_copy(d, ahead(seq, d), seq).start())
    r.served[seq] = wanted
    for j in range(BLOCKS):
        up_load(j).wait()
        down_load(j).wait()
    loop(1, GROUPS, lambda d: id_copy(d, ahead(seq, d), behind(seq, d)).wait())
    to_scalar = pltpu.make_async_copy(r.served, r.served_s, r.scalar_sem.at[0])
    to_scalar.start()
    loads[4].wait()
    loop(1, RETS, lambda d: raw_copy(d, (ret + d) % RETS, (ret + RETS - d) % RETS).wait())

    inputs = r.raw[...].reshape(-1, feat).astype(jnp.float32)
    normed = inputs * lax.rsqrt(jnp.mean(inputs * inputs, axis=-1, keepdims=True) + 1e-06)
    r.normed[...] = normed.astype(jnp.bfloat16)
    before = dot(r.normed[...], r.up_w[0])
    encoding = None
    for j in range(BLOCKS):
        following = dot(r.normed[...], r.up_w[j + 1]) if j < BLOCKS - 1 else None
        added = dot(jax.nn.gelu(before).astype(jnp.bfloat16), r.down_w[j])
        encoding = added if encoding is None else encoding + added
        before = following
    encoding = r.raw[...].reshape(-1, feat).astype(jnp.float32) + encoding
    r.table[...] = encoding.astype(jnp.bfloat16).reshape(r.table.shape)
    to_source.wait()
    to_scalar.wait()

    def asked(s, k):
        return r.served_s[s, 0, seq * CAP + k]

    def seq_copy(e, d, dest, slot):
        places = pl.ds(0, 2) if e == 0 else pl.ds(2, CAP - 2)
        return remote(
            r.leaving.at[dest, places],
            (r.arrived if e == 0 else r.arrived_third).at[slot],
            r.seq_send.at[e, d],
            r.seq_recv.at[e, d],
            (dest, ret),
        )

    def serve(e):
        def one(d):
            dest = ahead(seq, d)
            for k in ((0, 1), range(2, CAP))[e]:
                r.leaving[dest, k] = r.table[jnp.maximum(asked(dest, k), 0)]
            seq_copy(e, d, dest, seq).start()

        each_group(one)

    serve(0)
    serve(1)
    for k in range(CAP):
        mine = r.table[jnp.maximum(asked(seq, k), 0)]
        if k < 2:
            r.arrived[seq, k] = mine
        else:
            r.arrived_third[seq, k - 2] = mine

    def first(i):
        at = r.position[i]
        r.own[i] = r.arrived[at // CAP, jnp.minimum(at % CAP, 1)]

    def compact(i):
        at = r.position[i]
        group, place = at // CAP, at % CAP
        r.own[i] = jnp.where(
            place < 2, r.arrived[group, jnp.minimum(place, 1)], r.arrived_third[group, 0]
        )

    def rows(g, h):
        return pl.ds(g * size + h * half, half)

    def own_up(g, h, held):
        return remote(
            r.own.at[rows(g, h)],
            r.picked.at[rows(g, h), 2 * held + core],
            r.up_send.at[g, h],
            r.up_recv.at[g, h],
            up_to,
        )

    def own_down(g, h, held):
        return remote(
            r.own.at[rows(g, h)],
            r.picked.at[rows(g, h), 2 * held + core],
            r.dn_send.at[g, h],
            r.dn_recv.at[g, h],
            down_to,
        )

    def relay(g, h, held):
        return remote(
            r.picked.at[rows(g, h), 2 * held + core],
            r.picked.at[rows(g, h), 2 * held + core],
            r.far_send.at[g, h],
            r.far_recv.at[g, h],
            down_to if h else up_to,
        )

    def across(g, o, held, side):
        whole = pl.ds(g * size, size)
        source = r.picked.at[whole, 2 * held + side]
        return remote(
            r.own.at[whole] if o == 0 else source,
            source,
            r.sib_send.at[g, o],
            r.sib_recv.at[g, o],
            sibling,
        )

    def keep(g):
        whole = pl.ds(g * size, size)
        return pltpu.make_async_copy(
            r.own.at[whole], r.picked.at[whole, ret], r.keep_sem.at[g]
        )

    def send_own(g):
        own_up(g, 0, z).start()
        own_down(g, 1, z).start()
        own_up(g, 1, z).start()
        own_down(g, 0, z).start()
        across(g, 0, z, core).start()
        keep(g).start()

    def pass_on(g):
        own_up(g, 0, below).wait_recv()
        relay(g, 0, below).start()
        own_down(g, 1, above).wait_recv()
        relay(g, 1, above).start()
        own_up(g, 1, below).wait_recv()
        across(g, 1, below, core).start()
        own_down(g, 0, above).wait_recv()
        across(g, 2, above, core).start()

    def pass_far(g):
        relay(g, 0, facing).wait_recv()
        relay(g, 1, facing).wait_recv()
        across(g, 3, facing, core).start()

    def settle(g):
        for h in range(2):
            own_up(g, h, z).wait_send()
            own_down(g, h, z).wait_send()
            relay(g, h, above if h else below).wait_send()
        keep(g).wait()
        across(g, 0, z, 1 - core).wait()
        across(g, 1, below, 1 - core).wait()
        across(g, 2, above, 1 - core).wait()
        across(g, 3, facing, 1 - core).wait()

    cols = (pl.ds(0, CUT), pl.ds(CUT, feat - CUT))

    def swap(p, g, o):
        whole = pl.ds(g * size, size)
        return remote(
            r.part.at[whole, (z + o) % SIDE, 1 - core, :, cols[p]],
            r.sib.at[o, whole, :, cols[p]],
            r.swap_send.at[p, g, o],
            r.swap_recv.at[p, g, o],
            sibling,
        )

    def ring_copy(name, dst, at, to):
        send, recv = getattr(r, name + "_send"), getattr(r, name + "_recv")

        def copy(p, g, h):
            return remote(
                r.part.at[rows(g, h), at, core, :, cols[p]],
                dst.at[rows(g, h), :, cols[p]],
                send.at[p, g, h],
                recv.at[p, g, h],
                to(h),
            )

        return copy

    far_copy = ring_copy("rfar", r.far, facing, lambda h: down_to if h else up_to)
    up_copy = ring_copy("rup", r.near_up, above, lambda h: up_to)
    down_copy = ring_copy("rdn", r.near_down, below, lambda h: down_to)

    def merge(p, g, o):
        swap(p, g, o).wait_recv()
        at = (z + o) % SIDE
        whole = pl.ds(g * size, size)
        mine = r.part[whole, at, core, :, cols[p]].astype(jnp.float32)
        other = r.sib[o, whole, :, cols[p]].astype(jnp.float32)
        r.part[whole, at, core, :, cols[p]] = (mine + other).astype(jnp.bfloat16)

    def merge_all(p, g):
        merge(p, g, 2)
        far_copy(p, g, 0).start()
        far_copy(p, g, 1).start()
        merge(p, g, 1)
        up_copy(p, g, 1).start()
        merge(p, g, 3)
        down_copy(p, g, 0).start()
        merge(p, g, 0)

    def add_far(p, g):
        for h in range(2):
            far_copy(p, g, h).wait_recv()
            at = below if h else above
            mine = r.part[rows(g, h), at, core, :, cols[p]].astype(jnp.float32)
            other = r.far[rows(g, h), :, cols[p]].astype(jnp.float32)
            r.part[rows(g, h), at, core, :, cols[p]] = (mine + other).astype(jnp.bfloat16)
            (down_copy if h else up_copy)(p, g, h).start()

    def finish(p, g):
        for h in range(2):
            up_copy(p, g, h).wait_recv()
            down_copy(p, g, h).wait_recv()
        whole = pl.ds(g * size, size)
        r.total[whole, :, cols[p]] = (
            r.part[whole, z, core, :, cols[p]].astype(jnp.float32)
            + r.near_up[whole, :, cols[p]].astype(jnp.float32)
            + r.near_down[whole, :, cols[p]].astype(jnp.float32)
        ).astype(jnp.bfloat16)
        for o in range(4):
            swap(p, g, o).wait_send()
        for h in range(2):
            far_copy(p, g, h).wait_send()
            up_copy(p, g, h).wait_send()
            down_copy(p, g, h).wait_send()

    def project(p, g):
        gk, gv = r.up_w[g, : size * 128, :], r.down_w[g, :, : r.wk.shape[1]]
        part = dot(gk, r.wk[cols[p], :], NT) + dot(gv, r.wv[cols[p], :], NT)
        r.part[pl.ds(g * size, size), :, :, :, cols[p]] = part.astype(jnp.bfloat16).reshape(
            size, SIDE, 2, 16, part.shape[1]
        )
        for o in (2, 1, 3, 0):
            swap(p, g, o).start()

    def result_copies(g):
        tokens = pl.ds(g * (size * 32), size * 32)
        return (
            pltpu.make_async_copy(r.ctx.at[tokens], r.context.at[tokens], r.out_sem.at[g, 0]),
            pltpu.make_async_copy(r.gq.at[tokens], r.grad_query.at[tokens], r.out_sem.at[g, 1]),
        )

    def compute(g):
        attend(r, g, size)
        for copy in result_copies(g):
            copy.start()

    def at_step(g, step):
        @pl.when((g >= 0) & (g < STEPS))
        def _():
            step(g)

    each_group(lambda d: seq_copy(0, d, ahead(seq, d), behind(seq, d)).wait())
    loop(0, size, first)
    send_own(0)
    for i in range(4):
        loads[i].wait()
    each_group(lambda d: seq_copy(1, d, ahead(seq, d), behind(seq, d)).wait())
    loop(size, requests, compact)
    for g in range(1, EARLY):
        send_own(g)

    def tock(t):
        for p in range(2):
            begin = 4 + p * STEPS
            at_step(t - begin - 5, lambda g: finish(p, g))
            at_step(t - begin - 3, lambda g: add_far(p, g))
            at_step(t - begin - 1, lambda g: merge_all(p, g))
            at_step(t - begin, lambda g: project(p, g))

    def tick(t):
        at_step(t, pass_on)
        at_step(t + EARLY, send_own)
        at_step(t - LAG_FAR, pass_far)
        at_step(t - LAG_USE, settle)
        at_step(t - LAG_USE, compute)
        tock(t)

    phase = STEPS + LAG_USE
    loop(0, phase, tick)

    y, x = seq // SIDE, seq % SIDE
    each = feat // GROUPS
    wide = r.acc_k.shape[1] // 2
    for j in range(GROUPS):
        block = slice(each * j, each * j + each)
        for h in range(2):
            col = slice(wide * h, wide * h + wide)
            r.gw[j // SIDE, j % SIDE, h] = jnp.concatenate(
                [r.acc_k[block, col], r.acc_v[block, col]], axis=0
            ).astype(jnp.bfloat16)

    def along_x(d):
        return (y * SIDE + (x + d) % SIDE, ret)

    def along_y(d):
        return (((y + d) % SIDE) * SIDE + x, ret)

    def w_copy(h, d):
        return remote(
            r.gw.at[(y + d) % SIDE, :, 1] if h else r.gw.at[:, (x + d) % SIDE, 0],
            r.w_in.at[h, d],
            r.w_send.at[h, d],
            r.w_recv.at[h, d],
            along_y(d) if h else along_x(d),
        )

    def w_last(h, d):
        return remote(
            r.w_half.at[h, (x + d) % SIDE if h else (y + d) % SIDE],
            r.w_end.at[h, d],
            r.w2_send.at[h, d],
            r.w2_recv.at[h, d],
            along_x(d) if h else along_y(d),
        )

    def w_middle():
        for h in range(2):
            for d in range(1, SIDE):
                w_copy(h, d).wait()
            for j in range(SIDE):
                mine = r.gw[y, j, 1] if h else r.gw[j, x, 0]
                summed = mine.astype(jnp.float32)
                for d in range(1, SIDE):
                    summed = summed + r.w_in[h, d, j].astype(jnp.float32)
                r.w_half[h, j] = summed.astype(jnp.bfloat16)
            for d in range(1, SIDE):
                w_last(h, d).start()

    for d in range(1, SIDE):
        for h in range(2):
            w_copy(h, d).start()

    def back_copy(p, d, dest, slot):
        return remote(
            r.leaving.at[dest, :, :, cols[p]],
            r.arrived_b.at[slot, :, :, cols[p]],
            r.back_send.at[p, d],
            r.back_recv.at[p, d],
            (dest, ret),
        )

    def give_back(p):
        def give(d):
            dest = ahead(seq, d)
            for k in range(CAP):
                r.leaving[dest, k, :, cols[p]] = r.total[r.source[0, dest * CAP + k], :, cols[p]]
            back_copy(p, d, dest, seq).start()

        each_group(give)
        for k in range(CAP):
            r.arrived_b[seq, k, :, cols[p]] = r.total[r.source[0, seq * CAP + k], :, cols[p]]

    def last_tick(t):
        tock(t)
        pl.when(t == 4 + STEPS + 4)(w_middle)
        pl.when(t == 4 + STEPS + 5)(lambda: give_back(0))

    loop(phase, 4 + 2 * STEPS + 5, last_tick)
    give_back(1)

    row = lax.broadcasted_iota(jnp.int32, r.pick.shape, 0)
    col = lax.broadcasted_iota(jnp.int32, r.pick.shape, 1)
    place = lax.broadcasted_iota(jnp.int32, (1, r.pick.shape[1]), 1) // 16
    owner = jnp.full(place.shape, -1, jnp.int32)
    for s in range(GROUPS):
        for k in range(CAP):
            owner = jnp.where(place == s * CAP + k, asked(s, k), owner)
    r.pick[...] = jnp.where((row // 16 == owner) & (row % 16 == col % 16), 1.0, 0.0).astype(
        jnp.bfloat16
    )

    def home_copy(p, d, dest, slot):
        return remote(
            r.table.at[pl.ds(2 * dest, 2), :, cols[p]],
            r.home.at[:, slot, :, cols[p]],
            r.home_send.at[p, d],
            r.home_recv.at[p, d],
            (seq, dest),
        )

    def go_home(p):
        each_group(lambda d: back_copy(p, d, ahead(seq, d), behind(seq, d)).wait())
        arrived = r.arrived_b[:, :, :, cols[p]]
        summed = dot(r.pick[...], arrived.reshape(r.pick.shape[1], arrived.shape[-1]))
        r.table[:, :, cols[p]] = summed.astype(jnp.bfloat16).reshape(
            2 * RETS, 16, arrived.shape[-1]
        )
        loop(1, RETS, lambda d: home_copy(p, d, (ret + d) % RETS, ret).start())
        for k in range(2):
            r.home[k, ret, :, cols[p]] = r.table[2 * ret + k, :, cols[p]]

    go_home(0)
    for h in range(2):
        summed = r.w_half[h, x if h else y].astype(jnp.float32)
        for d in range(1, SIDE):
            w_last(h, d).wait()
            summed = summed + r.w_end[h, d].astype(jnp.float32)
        r.gk_out[:, wide * h : wide * h + wide] = summed[:each]
        r.gv_out[:, wide * h : wide * h + wide] = summed[each:]
    go_home(1)
    for p in range(2):
        loop(
            1,
            RETS,
            lambda d: home_copy(p, d, (ret + d) % RETS, (ret + RETS - d) % RETS).wait(),
        )
    for g in range(STEPS):
        for copy in result_copies(g):
            copy.wait()


def picked_rows(r, g, count):
    first = g * (r.own.shape[0] // STEPS)
    return r.picked[pl.ds(first, count)].reshape(count * 128, r.wk.shape[0])


def attend(r, g, size):
    feat, width = r.wk.shape
    heads = width // HD
    spans = size // 2
    scale = 1.0 / math.sqrt(HD)
    rows = picked_rows(r, g, size)
    r.keys[...] = dot(rows, r.wk[...]).astype(jnp.bfloat16)
    r.values[...] = dot(rows, r.wv[...]).astype(jnp.bfloat16)
    gkeys, gvalues = r.up_w.at[g, : size * 128], r.down_w.at[g, :, :width]
    for c in range(spans):
        tok = pl.ds(pl.multiple_of((g * spans + c) * 64, 64), 64)
        row = slice(256 * c, 256 * c + 256)
        cols = [slice(HD * h, HD * h + HD) for h in range(heads)]
        scores = [dot(r.q[tok, col], r.keys[row, col], NT) for col in cols]
        gps = [dot(r.go[tok, col], r.values[row, col], NT) for col in cols]
        weights = [jnp.exp(s * scale) for s in scores]
        weights = [w / jnp.sum(w, axis=-1, keepdims=True) for w in weights]
        probs = [w.astype(jnp.bfloat16) for w in weights]
        mixed = [
            (w * (gp - jnp.sum(w * gp, axis=-1, keepdims=True)) * scale).astype(jnp.bfloat16)
            for w, gp in zip(weights, gps)
        ]
        for col, p, m in zip(cols, probs, mixed):
            r.ctx[tok, col] = dot(p, r.values[row, col]).astype(jnp.bfloat16)
            r.gq[tok, col] = dot(m, r.keys[row, col]).astype(jnp.bfloat16)
            gkeys[row, col] = dot(m, r.q[tok, col], TN).astype(jnp.bfloat16)
            gvalues[row, col] = dot(p, r.go[tok, col], TN).astype(jnp.bfloat16)

    @pl.when(g % 2 == 1)
    def _():
        pair = picked_rows(r, g - 1, 2 * size)
        gk = r.up_w[pl.ds(g - 1, 2), : size * 128].reshape(-1, width)
        gv = r.down_w[pl.ds(g - 1, 2), :, :width].reshape(-1, width)
        add_k = dot(pair, gk, TN)
        add_v = dot(pair, gv, TN)

        @pl.when(g == 1)
        def _():
            r.acc_k[...] = add_k
            r.acc_v[...] = add_v

        @pl.when(g > 1)
        def _():
            r.acc_k[...] += add_k
            r.acc_v[...] += add_v


def fused(
    queries,
    grad_ctx,
    neighbours,
    up_weight,
    down_weight,
    key_weight,
    value_weight,
    group_ids,
    slot_ids,
):
    feat, ffe = up_weight.shape
    requests = group_ids.shape[0] * group_ids.shape[1]
    tokens, width = queries.shape
    size = requests // STEPS
    bf, f32 = jnp.bfloat16, jnp.float32
    dma = pltpu.SemaphoreType.DMA
    slots = (GROUPS, CAP, 16, feat)
    chunk = (requests, 16, feat)
    block = (2 * feat // GROUPS, width // 2)
    any_, vmem, smem = (
        pl.BlockSpec(memory_space=s) for s in (pl.ANY, pltpu.VMEM, pltpu.SMEM)
    )
    ins = dict(
        queries=any_,
        grad_ctx=any_,
        neighbours=any_,
        up_weight=any_,
        down_weight=any_,
        key_weight=any_,
        value_weight=any_,
        group_ids=smem,
        slot_ids=smem,
    )
    outs = dict(
        context=(any_, queries.shape, bf),
        grad_query=(any_, queries.shape, bf),
        home=(vmem, (2, RETS, 16, feat), bf),
        gk_out=(vmem, (feat // GROUPS, width), f32),
        gv_out=(vmem, (feat // GROUPS, width), f32),
    )
    scratch = dict(
        wanted=pltpu.VMEM((8, 128), jnp.int32),
        source_v=pltpu.VMEM((8, 128), jnp.int32),
        source=pltpu.SMEM((8, 128), jnp.int32),
        position=pltpu.SMEM((requests,), jnp.int32),
        served=pltpu.VMEM((GROUPS, 8, 128), jnp.int32),
        served_s=pltpu.SMEM((GROUPS, 8, 128), jnp.int32),
        raw=pltpu.VMEM((2 * RETS, 16, feat), bf),
        normed=pltpu.VMEM((2 * RETS * 16, feat), bf),
        up_w=pltpu.VMEM((BLOCKS, feat, ffe // BLOCKS), bf),
        down_w=pltpu.VMEM((BLOCKS, ffe // BLOCKS, feat), bf),
        table=pltpu.VMEM((2 * RETS, 16, feat), bf),
        arrived=pltpu.VMEM((GROUPS, 2, 16, feat), bf),
        arrived_third=pltpu.VMEM((GROUPS, CAP - 2, 16, feat), bf),
        leaving=pltpu.VMEM(slots, bf),
        own=pltpu.VMEM(chunk, bf),
        picked=pltpu.VMEM((requests, RETS, 16, feat), bf),
        wk=pltpu.VMEM((feat, width), bf),
        wv=pltpu.VMEM((feat, width), bf),
        q=pltpu.VMEM(queries.shape, bf),
        go=pltpu.VMEM(queries.shape, bf),
        ctx=pltpu.VMEM(queries.shape, bf),
        gq=pltpu.VMEM(queries.shape, bf),
        keys=pltpu.VMEM((size * 128, width), bf),
        values=pltpu.VMEM((size * 128, width), bf),
        acc_k=pltpu.VMEM((feat, width), f32),
        acc_v=pltpu.VMEM((feat, width), f32),
        part=pltpu.VMEM((requests, SIDE, 2, 16, feat), bf),
        sib=pltpu.VMEM((SIDE,) + chunk, bf),
        far=pltpu.VMEM(chunk, bf),
        near_up=pltpu.VMEM(chunk, bf),
        near_down=pltpu.VMEM(chunk, bf),
        total=pltpu.VMEM(chunk, bf),
        arrived_b=pltpu.VMEM(slots, bf),
        gw=pltpu.VMEM((SIDE, SIDE, 2) + block, bf),
        w_in=pltpu.VMEM((2, SIDE, SIDE) + block, bf),
        w_half=pltpu.VMEM((2, SIDE) + block, bf),
        w_end=pltpu.VMEM((2, SIDE) + block, bf),
        pick=pltpu.VMEM((2 * RETS * 16, GROUPS * CAP * 16), bf),
        up_sem=dma((BLOCKS,)),
        down_sem=dma((BLOCKS,)),
        load_sem=dma((5,)),
        scalar_sem=dma((2,)),
        keep_sem=dma((STEPS,)),
        out_sem=dma((STEPS, 2)),
    )
    for name, shape in dict(
        id=(GROUPS,),
        raw=(RETS,),
        seq=(2, GROUPS),
        up=(STEPS, 2),
        dn=(STEPS, 2),
        far=(STEPS, 2),
        sib=(STEPS, 4),
        swap=(2, STEPS, 4),
        rfar=(2, STEPS, 2),
        rup=(2, STEPS, 2),
        rdn=(2, STEPS, 2),
        w=(2, SIDE),
        w2=(2, SIDE),
        back=(2, GROUPS),
        home=(2, RETS),
    ).items():
        scratch[name + "_send"] = dma(shape)
        scratch[name + "_recv"] = dma(shape)
    names = tuple(ins) + tuple(outs) + tuple(scratch)
    return pl.pallas_call(
        functools.partial(kernel, names),
        out_shape=tuple(jax.ShapeDtypeStruct(s, t) for _, s, t in outs.values()),
        in_specs=list(ins.values()),
        out_specs=tuple(s for s, _, _ in outs.values()),
        scratch_shapes=list(scratch.values()),
        compiler_params=pltpu.CompilerParams(
            collective_id=0, has_side_effects=True, vmem_limit_bytes=60 * MIB
        ),
        name="fused",
    )(
        queries,
        grad_ctx,
        neighbours.reshape(2, RETS, 16, feat),
        up_weight,
        down_weight,
        key_weight,
        value_weight,
        group_ids,
        slot_ids,
    )


def deliver_kernel(*refs):
    count = len(refs) // 3
    sems = refs[-1]
    incoming = [
        pltpu.make_async_copy(refs[i], refs[2 * count + i], sems.at[0, i]) for i in range(count)
    ]
    outgoing = [
        pltpu.make_async_copy(refs[2 * count + i], refs[count + i], sems.at[1, i])
        for i in range(count)
    ]
    for copy in incoming:
        copy.start()
    for i in range(count):
        incoming[i].wait()
        outgoing[i].start()
    for copy in outgoing:
        copy.wait()


def deliver(arrays):
    any_ = pl.BlockSpec(memory_space=pl.ANY)
    return pl.pallas_call(
        deliver_kernel,
        out_shape=tuple(jax.ShapeDtypeStruct(a.shape, a.dtype) for a in arrays),
        in_specs=[any_] * len(arrays),
        out_specs=(any_,) * len(arrays),
        scratch_shapes=[pltpu.VMEM(a.shape, a.dtype) for a in arrays]
        + [pltpu.SemaphoreType.DMA((2, len(arrays)))],
        name="deliver",
    )(*arrays)


def body(
    queries,
    grad_ctx,
    neighbours,
    up_weight,
    down_weight,
    key_weight,
    value_weight,
    group_ids,
    slot_ids,
):
    context, grad_query, home, grad_key_w, grad_value_w = deliver(
        fused(
            queries,
            grad_ctx,
            neighbours,
            up_weight,
            down_weight,
            key_weight,
            value_weight,
            group_ids.T,
            slot_ids.T,
        )
    )
    return context, grad_query, home.reshape(neighbours.shape), grad_key_w, grad_value_w


def solution(mesh):
    return jax.shard_map(
        body,
        mesh=mesh,
        in_specs=(
            P("seq", "ret"),
            P("seq", "ret"),
            P(("seq", "ret"), None, None),
            P(),
            P(),
            P(None, "ret"),
            P(None, "ret"),
            P("seq", None),
            P("seq", None),
        ),
        out_specs=(
            P("seq", "ret"),
            P("seq", "ret"),
            P(("seq", "ret"), None, None),
            P("seq", "ret"),
            P("seq", "ret"),
        ),
        check_vma=False,
    )
```

```python
import functools
import math

import jax
import jax.numpy as jnp
from jax import lax
from jax.experimental import pallas as pl
from jax.experimental.pallas import tpu as pltpu
from jax.sharding import PartitionSpec as P

HD = 128
CAP = 3
MESH = pl.DeviceIdType.MESH
SIDE = 4
GROUPS = 16
RETS = 8
STEPS = 6
BLOCKS = 7
CUT = 512
EARLY = 3
LAG_PART = 1
MIX = 3
MIB = 1024 * 1024


def ahead(seq, d):
    y, x = seq // SIDE, seq % SIDE
    return ((y + d // SIDE) % SIDE) * SIDE + (x + d % SIDE) % SIDE


def behind(seq, d):
    y, x = seq // SIDE, seq % SIDE
    return ((y + SIDE - d // SIDE) % SIDE) * SIDE + (x + SIDE - d % SIDE) % SIDE


def each_group(step):
    loop(1, GROUPS, lambda d: step(d * MIX % GROUPS))


def loop(low, high, step):
    def run(i, carry):
        step(i)
        return carry

    lax.fori_loop(low, high, run, 0)


def greet(seq, ret):
    barrier = pltpu.get_barrier_semaphore()

    def to_seq(d):
        pl.semaphore_signal(barrier, inc=1, device_id=(ahead(seq, d), ret), device_id_type=MESH)

    def to_ret(d):
        pl.semaphore_signal(barrier, inc=1, device_id=(seq, (ret + d) % RETS), device_id_type=MESH)

    loop(1, GROUPS, to_seq)
    loop(1, RETS, to_ret)
    return lambda: pl.semaphore_wait(barrier, GROUPS + RETS - 2)


def drain(like, sem):
    pltpu.make_async_copy(like, like, sem).wait()


def remote(src, dst, send, recv, to):
    return pltpu.make_async_remote_copy(
        src_ref=src,
        dst_ref=dst,
        send_sem=send,
        recv_sem=recv,
        device_id=to,
        device_id_type=MESH,
    )


NT = (((1,), (1,)), ((), ()))
TN = (((0,), (0,)), ((), ()))


def dot(a, b, dims=(((1,), (0,)), ((), ()))):
    return lax.dot_general(a, b, dims, preferred_element_type=jnp.float32)


class Refs:
    def __init__(self, names, refs):
        self.__dict__.update(zip(names, refs))


def kernel(names, *refs):
    r = Refs(names, refs)
    seq, ret = lax.axis_index("seq"), lax.axis_index("ret")
    z, core = ret // 2, ret % 2
    above, below, facing = (z + 1) % SIDE, (z + SIDE - 1) % SIDE, (z + 2) % SIDE
    sibling = (seq, 2 * z + 1 - core)
    up_to, down_to = (seq, 2 * above + core), (seq, 2 * below + core)
    requests = r.own.shape[0]
    size = requests // STEPS
    half = size // 2
    feat = r.own.shape[-1]

    def up_load(j):
        width = r.up_w.shape[-1]
        return pltpu.make_async_copy(
            r.up_weight.at[:, pl.ds(j * width, width)], r.up_w.at[j], r.up_sem
        )

    def down_load(j):
        depth = r.down_w.shape[1]
        return pltpu.make_async_copy(
            r.down_weight.at[pl.ds(j * depth, depth)], r.down_w.at[j], r.down_sem
        )

    loads = [
        pltpu.make_async_copy(a, b, r.load_sem.at[i])
        for i, (a, b) in enumerate(
            (
                (r.key_weight, r.wk),
                (r.value_weight, r.wv),
                (r.queries, r.q),
                (r.grad_ctx, r.go),
                (r.neighbours.at[:, ret], r.raw.at[pl.ds(2 * ret, 2)]),
            )
        )
    ]
    loads[4].start()

    greeted = greet(seq, ret)

    targets = [r.group_ids[i % 2, i // 2] for i in range(requests)]
    slots = [r.slot_ids[i % 2, i // 2] for i in range(requests)]
    lane = lax.broadcasted_iota(jnp.int32, (8, 128), 1)
    wanted = jnp.full((8, 128), -1, jnp.int32)
    source = jnp.zeros((8, 128), jnp.int32)
    for i in range(requests):
        count = jnp.int32(0)
        for j in range(i):
            count += (targets[j] == targets[i]).astype(jnp.int32)
        at = targets[i] * CAP + count
        r.position[i] = at
        wanted = jnp.where(lane == at, slots[i], wanted)
        source = jnp.where(lane == at, i, source)
    r.wanted[...] = wanted
    r.source_v[...] = source
    to_source = pltpu.make_async_copy(r.source_v, r.source, r.scalar_sem.at[1])
    to_source.start()

    def id_copy(d, dest, slot):
        return remote(r.wanted, r.served.at[slot], r.id_send, r.id_recv, (dest, ret))

    def raw_copy(d, dest, slot):
        return remote(
            r.neighbours.at[:, dest],
            r.raw.at[pl.ds(2 * slot, 2)],
            r.raw_send,
            r.raw_recv,
            (seq, dest),
        )

    greeted()
    loop(1, RETS, lambda d: raw_copy(d, (ret + d) % RETS, ret).start())
    loop(1, GROUPS, lambda d: id_copy(d, ahead(seq, d), seq).start())
    for j in range(BLOCKS):
        up_load(j).start()
        down_load(j).start()
    r.served[seq] = wanted
    drain(r.served.at[pl.ds(0, GROUPS - 1)], r.id_recv)
    drain(r.served.at[pl.ds(0, GROUPS - 1)], r.id_send)
    to_scalar = pltpu.make_async_copy(r.served, r.served_s, r.scalar_sem.at[0])
    to_scalar.start()
    loads[4].wait()
    drain(r.raw.at[pl.ds(0, 2 * (RETS - 1))], r.raw_recv)
    drain(r.raw.at[pl.ds(0, 2 * (RETS - 1))], r.raw_send)

    drain(r.up_w, r.up_sem)
    drain(r.down_w, r.down_sem)
    for i in range(4):
        loads[i].start()

    inputs = r.raw[...].reshape(-1, feat).astype(jnp.float32)
    normed = inputs * lax.rsqrt(jnp.mean(inputs * inputs, axis=-1, keepdims=True) + 1e-06)
    r.normed[...] = normed.astype(jnp.bfloat16)
    before = dot(r.normed[...], r.up_w[0])
    encoding = None
    for j in range(BLOCKS):
        following = dot(r.normed[...], r.up_w[j + 1]) if j < BLOCKS - 1 else None
        added = dot(jax.nn.gelu(before).astype(jnp.bfloat16), r.down_w[j])
        encoding = added if encoding is None else encoding + added
        before = following
    encoding = r.raw[...].reshape(-1, feat).astype(jnp.float32) + encoding
    r.table[...] = encoding.astype(jnp.bfloat16).reshape(r.table.shape)
    to_source.wait()
    to_scalar.wait()

    def asked(s, k):
        return r.served_s[s, 0, seq * CAP + k]

    def seq_copy(e, d, dest, slot):
        places = pl.ds(0, 2) if e == 0 else pl.ds(2, CAP - 2)
        return remote(
            r.leaving.at[dest, places],
            (r.arrived if e == 0 else r.arrived_third).at[slot],
            r.seq_send.at[e],
            r.seq_recv.at[e],
            (dest, ret),
        )

    def serve(e):
        def one(d):
            dest = ahead(seq, d)
            for k in ((0, 1), range(2, CAP))[e]:
                r.leaving[dest, k] = r.table[jnp.maximum(asked(dest, k), 0)]
            seq_copy(e, d, dest, seq).start()

        each_group(one)

    serve(0)
    serve(1)
    for k in range(CAP):
        mine = r.table[jnp.maximum(asked(seq, k), 0)]
        if k < 2:
            r.arrived[seq, k] = mine
        else:
            r.arrived_third[seq, k - 2] = mine

    def first(i):
        at = r.position[i]
        r.own[i] = r.arrived[at // CAP, jnp.minimum(at % CAP, 1)]

    def compact(i):
        at = r.position[i]
        group, place = at // CAP, at % CAP
        r.own[i] = jnp.where(
            place < 2, r.arrived[group, jnp.minimum(place, 1)], r.arrived_third[group, 0]
        )

    def rows(g, h):
        return pl.ds(g * size + h * half, half)

    def own_up(g, h, held):
        return remote(
            r.own.at[rows(g, h)],
            r.picked.at[rows(g, h), 2 * held + core],
            r.up_send,
            r.up_recv.at[g, h],
            up_to,
        )

    def own_down(g, h, held):
        return remote(
            r.own.at[rows(g, h)],
            r.picked.at[rows(g, h), 2 * held + core],
            r.dn_send,
            r.dn_recv.at[g, h],
            down_to,
        )

    def relay(g, h, held):
        return remote(
            r.picked.at[rows(g, h), 2 * held + core],
            r.picked.at[rows(g, h), 2 * held + core],
            r.far_send,
            r.far_recv.at[g],
            down_to if h else up_to,
        )

    def across(g, o, held, side):
        whole = pl.ds(g * size, size)
        source = r.picked.at[whole, 2 * held + side]
        return remote(
            r.own.at[whole] if o == 0 else source,
            source,
            r.sib_send,
            r.sib_recv.at[g],
            sibling,
        )

    def keep(g):
        whole = pl.ds(g * size, size)
        return pltpu.make_async_copy(
            r.own.at[whole], r.picked.at[whole, ret], r.keep_sem.at[g]
        )

    def send_own(g):
        own_up(g, 0, z).start()
        own_down(g, 1, z).start()
        own_up(g, 1, z).start()
        own_down(g, 0, z).start()
        across(g, 0, z, core).start()
        keep(g).start()

    def pass_on(g):
        own_up(g, 0, below).wait_recv()
        relay(g, 0, below).start()
        own_down(g, 1, above).wait_recv()
        relay(g, 1, above).start()
        own_up(g, 1, below).wait_recv()
        across(g, 1, below, core).start()
        own_down(g, 0, above).wait_recv()
        across(g, 2, above, core).start()

    def pass_far(g):
        drain(r.own.at[pl.ds(0, size)], r.far_recv.at[g])
        across(g, 3, facing, core).start()

    def settle(g):
        keep(g).wait()
        drain(r.picked.at[pl.ds(0, size), pl.ds(0, SIDE)], r.sib_recv.at[g])

    cols = (pl.ds(0, CUT), pl.ds(CUT, feat - CUT))

    def swap(p, g, o):
        whole = pl.ds(g * size, size)
        return remote(
            r.part.at[whole, (z + o) % SIDE, 1 - core, :, cols[p]],
            r.sib.at[o, whole, :, cols[p]],
            r.swap_send.at[p],
            r.swap_recv.at[p, g],
            sibling,
        )

    def ring_copy(send, recv, dst, at, to):

        def copy(p, g, h):
            return remote(
                r.part.at[rows(g, h), at, core, :, cols[p]],
                dst.at[rows(g, h), :, cols[p]],
                send.at[p],
                recv.at[p, g],
                to(h),
            )

        return copy

    far_copy = ring_copy(r.rfar_send, r.rfar_recv, r.far, facing, lambda h: down_to if h else up_to)
    up_copy = ring_copy(r.near_send, r.near_recv, r.near_up, above, lambda h: up_to)
    down_copy = ring_copy(r.near_send, r.near_recv, r.near_down, below, lambda h: down_to)

    def merge(p, g, o):
        at = (z + o) % SIDE
        whole = pl.ds(g * size, size)
        mine = r.part[whole, at, core, :, cols[p]].astype(jnp.float32)
        other = r.sib[o, whole, :, cols[p]].astype(jnp.float32)
        r.part[whole, at, core, :, cols[p]] = (mine + other).astype(jnp.bfloat16)

    def merge_all(p, g):
        drain(r.sib.at[:, pl.ds(0, size), :, cols[p]], r.swap_recv.at[p, g])
        merge(p, g, 2)
        far_copy(p, g, 0).start()
        far_copy(p, g, 1).start()
        merge(p, g, 1)
        up_copy(p, g, 1).start()
        merge(p, g, 3)
        down_copy(p, g, 0).start()
        merge(p, g, 0)

    def add_far(p, g):
        drain(r.far.at[pl.ds(0, size), :, cols[p]], r.rfar_recv.at[p, g])
        for h in range(2):
            at = below if h else above
            mine = r.part[rows(g, h), at, core, :, cols[p]].astype(jnp.float32)
            other = r.far[rows(g, h), :, cols[p]].astype(jnp.float32)
            r.part[rows(g, h), at, core, :, cols[p]] = (mine + other).astype(jnp.bfloat16)
            (down_copy if h else up_copy)(p, g, h).start()

    def finish(p, g):
        drain(r.sib.at[pl.ds(0, 2), pl.ds(0, size), :, cols[p]], r.near_recv.at[p, g])
        whole = pl.ds(g * size, size)
        r.total[whole, :, cols[p]] = (
            r.part[whole, z, core, :, cols[p]].astype(jnp.float32)
            + r.near_up[whole, :, cols[p]].astype(jnp.float32)
            + r.near_down[whole, :, cols[p]].astype(jnp.float32)
        ).astype(jnp.bfloat16)

    def project(p, g):
        gk, gv = r.up_w[g, : size * 128, :], r.down_w[g, :, : r.wk.shape[1]]
        part = dot(gk, r.wk[cols[p], :], NT) + dot(gv, r.wv[cols[p], :], NT)
        r.part[pl.ds(g * size, size), :, :, :, cols[p]] = part.astype(jnp.bfloat16).reshape(
            size, SIDE, 2, 16, part.shape[1]
        )
        for o in (2, 1, 3, 0):
            swap(p, g, o).start()

    def result_copies(g):
        tokens = pl.ds(g * (size * 32), size * 32)
        return (
            pltpu.make_async_copy(r.ctx.at[tokens], r.context.at[tokens], r.out_sem.at[0]),
            pltpu.make_async_copy(r.gq.at[tokens], r.grad_query.at[tokens], r.out_sem.at[1]),
        )

    def compute(g):
        weight_grads(r, g, size)
        for copy in result_copies(g):
            copy.start()

    def at_step(g, step):
        @pl.when((g >= 0) & (g < STEPS))
        def _():
            step(g)

    drain(r.arrived.at[pl.ds(0, GROUPS - 1)], r.seq_recv.at[0])
    drain(r.arrived.at[pl.ds(0, GROUPS - 1)], r.seq_send.at[0])
    loop(0, size, first)
    send_own(0)
    pass_on(0)
    for i in range(4):
        loads[i].wait()
    drain(r.arrived_third.at[pl.ds(0, GROUPS - 1)], r.seq_recv.at[1])
    drain(r.arrived_third.at[pl.ds(0, GROUPS - 1)], r.seq_send.at[1])
    loop(size, requests, compact)

    def tock(t):
        for p in range(2):
            begin = LAG_PART + p * STEPS
            at_step(t - begin - 5, lambda g: finish(p, g))
            at_step(t - begin - 3, lambda g: add_far(p, g))
            at_step(t - begin - 1, lambda g: merge_all(p, g))
            at_step(t - begin, lambda g: project(p, g))

    def tick(t):
        at_step(t + 1, pass_on)
        at_step(t + EARLY, send_own)
        settle(t)
        attend(r, t, size)
        at_step(t + 1, pass_far)
        compute(t)
        tock(t)

    for g in range(1, EARLY):
        send_own(g)
    pass_far(0)
    loop(0, STEPS, tick)

    y, x = seq // SIDE, seq % SIDE
    each = feat // GROUPS
    wide = r.acc_k.shape[1] // 2
    for j in range(GROUPS):
        block = slice(each * j, each * j + each)
        for h in range(2):
            col = slice(wide * h, wide * h + wide)
            r.gw[j // SIDE, j % SIDE, h] = jnp.concatenate(
                [r.acc_k[block, col], r.acc_v[block, col]], axis=0
            ).astype(jnp.bfloat16)

    def along_x(d):
        return (y * SIDE + (x + d) % SIDE, ret)

    def along_y(d):
        return (((y + d) % SIDE) * SIDE + x, ret)

    def w_copy(h, d):
        return remote(
            r.gw.at[(y + d) % SIDE, :, 1] if h else r.gw.at[:, (x + d) % SIDE, 0],
            r.w_in.at[h, d],
            r.w_send.at[h, d],
            r.w_recv.at[h, d],
            along_y(d) if h else along_x(d),
        )

    def w_last(h, d):
        return remote(
            r.w_half.at[h, (x + d) % SIDE if h else (y + d) % SIDE],
            r.w_end.at[h, d],
            r.w2_send.at[h, d],
            r.w2_recv.at[h, d],
            along_x(d) if h else along_y(d),
        )

    def w_middle():
        for h in range(2):
            for d in range(1, SIDE):
                w_copy(h, d).wait()
            for j in range(SIDE):
                mine = r.gw[y, j, 1] if h else r.gw[j, x, 0]
                summed = mine.astype(jnp.float32)
                for d in range(1, SIDE):
                    summed = summed + r.w_in[h, d, j].astype(jnp.float32)
                r.w_half[h, j] = summed.astype(jnp.bfloat16)
            for d in range(1, SIDE):
                w_last(h, d).start()

    for d in range(1, SIDE):
        for h in range(2):
            w_copy(h, d).start()

    def back_copy(p, d, dest, slot):
        return remote(
            r.leaving.at[dest, :, :, cols[p]],
            r.arrived_b.at[slot, :, :, cols[p]],
            r.back_send.at[p],
            r.back_recv.at[p],
            (dest, ret),
        )

    def give_back(p):
        def give(d):
            dest = ahead(seq, d)
            for k in range(CAP):
                r.leaving[dest, k, :, cols[p]] = r.total[r.source[0, dest * CAP + k], :, cols[p]]
            back_copy(p, d, dest, seq).start()

        each_group(give)
        for k in range(CAP):
            r.arrived_b[seq, k, :, cols[p]] = r.total[r.source[0, seq * CAP + k], :, cols[p]]

    def last_tick(t):
        tock(t)
        pl.when(t == LAG_PART + STEPS + 5)(w_middle)
        pl.when(t == LAG_PART + STEPS + 5)(lambda: give_back(0))

    loop(STEPS, LAG_PART + 2 * STEPS + 5, last_tick)
    give_back(1)

    row = lax.broadcasted_iota(jnp.int32, r.pick.shape, 0)
    col = lax.broadcasted_iota(jnp.int32, r.pick.shape, 1)
    place = lax.broadcasted_iota(jnp.int32, (1, r.pick.shape[1]), 1) // 16
    owner = jnp.full(place.shape, -1, jnp.int32)
    for s in range(GROUPS):
        for k in range(CAP):
            owner = jnp.where(place == s * CAP + k, asked(s, k), owner)
    r.pick[...] = jnp.where((row // 16 == owner) & (row % 16 == col % 16), 1.0, 0.0).astype(
        jnp.bfloat16
    )

    def home_copy(p, d, dest, slot):
        return remote(
            r.table.at[pl.ds(2 * dest, 2), :, cols[p]],
            r.home.at[:, slot, :, cols[p]],
            r.home_send.at[p],
            r.home_recv.at[p],
            (seq, dest),
        )

    def go_home(p):
        drain(r.arrived_b.at[pl.ds(0, GROUPS - 1), :, :, cols[p]], r.back_recv.at[p])
        arrived = r.arrived_b[:, :, :, cols[p]]
        summed = dot(r.pick[...], arrived.reshape(r.pick.shape[1], arrived.shape[-1]))
        r.table[:, :, cols[p]] = summed.astype(jnp.bfloat16).reshape(
            2 * RETS, 16, arrived.shape[-1]
        )
        loop(1, RETS, lambda d: home_copy(p, d, (ret + d) % RETS, ret).start())
        for k in range(2):
            r.home[k, ret, :, cols[p]] = r.table[2 * ret + k, :, cols[p]]

    go_home(0)
    for h in range(2):
        summed = r.w_half[h, x if h else y].astype(jnp.float32)
        for d in range(1, SIDE):
            w_last(h, d).wait()
            summed = summed + r.w_end[h, d].astype(jnp.float32)
        r.gk_out[:, wide * h : wide * h + wide] = summed[:each]
        r.gv_out[:, wide * h : wide * h + wide] = summed[each:]
    go_home(1)
    for p in range(2):
        sent_home = r.home.at[:, pl.ds(0, RETS - 1), :, cols[p]]
        drain(sent_home, r.home_recv.at[p])
        drain(sent_home, r.home_send.at[p])
        drain(r.arrived_b.at[pl.ds(0, GROUPS - 1), :, :, cols[p]], r.back_send.at[p])
        drain(r.sib.at[:, :, :, cols[p]], r.swap_send.at[p])
        drain(r.far.at[:, :, cols[p]], r.rfar_send.at[p])
        drain(r.sib.at[pl.ds(0, 2), :, :, cols[p]], r.near_send.at[p])
    drain(r.own, r.up_send)
    drain(r.own, r.dn_send)
    drain(r.own, r.far_send)
    drain(r.picked.at[:, pl.ds(0, SIDE)], r.sib_send)
    drain(r.ctx, r.out_sem.at[0])
    drain(r.gq, r.out_sem.at[1])


def picked_rows(r, g, count):
    first = g * (r.own.shape[0] // STEPS)
    return r.picked[pl.ds(first, count)].reshape(count * 128, r.wk.shape[0])


def attend(r, g, size):
    feat, width = r.wk.shape
    heads = width // HD
    spans = size // 2
    scale = 1.0 / math.sqrt(HD)
    rows = picked_rows(r, g, size)
    r.keys[...] = dot(rows, r.wk[...]).astype(jnp.bfloat16)
    r.values[...] = dot(rows, r.wv[...]).astype(jnp.bfloat16)
    gkeys, gvalues = r.up_w.at[g, : size * 128], r.down_w.at[g, :, :width]
    for c in range(spans):
        tok = pl.ds(pl.multiple_of((g * spans + c) * 64, 64), 64)
        row = slice(256 * c, 256 * c + 256)
        cols = [slice(HD * h, HD * h + HD) for h in range(heads)]
        scores = [dot(r.q[tok, col], r.keys[row, col], NT) for col in cols]
        gps = [dot(r.go[tok, col], r.values[row, col], NT) for col in cols]
        weights = [jnp.exp(s * scale) for s in scores]
        weights = [w / jnp.sum(w, axis=-1, keepdims=True) for w in weights]
        probs = [w.astype(jnp.bfloat16) for w in weights]
        mixed = [
            (w * (gp - jnp.sum(w * gp, axis=-1, keepdims=True)) * scale).astype(jnp.bfloat16)
            for w, gp in zip(weights, gps)
        ]
        for col, p, m in zip(cols, probs, mixed):
            r.ctx[tok, col] = dot(p, r.values[row, col]).astype(jnp.bfloat16)
            r.gq[tok, col] = dot(m, r.keys[row, col]).astype(jnp.bfloat16)
            gkeys[row, col] = dot(m, r.q[tok, col], TN).astype(jnp.bfloat16)
            gvalues[row, col] = dot(p, r.go[tok, col], TN).astype(jnp.bfloat16)


def weight_grads(r, g, size):
    width = r.wk.shape[1]

    @pl.when(g % 2 == 1)
    def _():
        pair = picked_rows(r, g - 1, 2 * size)
        gk = r.up_w[pl.ds(g - 1, 2), : size * 128].reshape(-1, width)
        gv = r.down_w[pl.ds(g - 1, 2), :, :width].reshape(-1, width)
        add_k = dot(pair, gk, TN)
        add_v = dot(pair, gv, TN)

        @pl.when(g == 1)
        def _():
            r.acc_k[...] = add_k
            r.acc_v[...] = add_v

        @pl.when(g > 1)
        def _():
            r.acc_k[...] += add_k
            r.acc_v[...] += add_v


def fused(
    queries,
    grad_ctx,
    neighbours,
    up_weight,
    down_weight,
    key_weight,
    value_weight,
    group_ids,
    slot_ids,
):
    feat, ffe = up_weight.shape
    requests = group_ids.shape[0] * group_ids.shape[1]
    tokens, width = queries.shape
    size = requests // STEPS
    bf, f32 = jnp.bfloat16, jnp.float32
    dma = pltpu.SemaphoreType.DMA
    slots = (GROUPS, CAP, 16, feat)
    chunk = (requests, 16, feat)
    block = (2 * feat // GROUPS, width // 2)
    any_, vmem, smem = (
        pl.BlockSpec(memory_space=s) for s in (pl.ANY, pltpu.VMEM, pltpu.SMEM)
    )
    ins = dict(
        queries=any_,
        grad_ctx=any_,
        neighbours=any_,
        up_weight=any_,
        down_weight=any_,
        key_weight=any_,
        value_weight=any_,
        group_ids=smem,
        slot_ids=smem,
    )
    outs = dict(
        context=(any_, queries.shape, bf),
        grad_query=(any_, queries.shape, bf),
        home=(vmem, (2, RETS, 16, feat), bf),
        gk_out=(vmem, (feat // GROUPS, width), f32),
        gv_out=(vmem, (feat // GROUPS, width), f32),
    )
    scratch = dict(
        wanted=pltpu.VMEM((8, 128), jnp.int32),
        source_v=pltpu.VMEM((8, 128), jnp.int32),
        source=pltpu.SMEM((8, 128), jnp.int32),
        position=pltpu.SMEM((requests,), jnp.int32),
        served=pltpu.VMEM((GROUPS, 8, 128), jnp.int32),
        served_s=pltpu.SMEM((GROUPS, 8, 128), jnp.int32),
        raw=pltpu.VMEM((2 * RETS, 16, feat), bf),
        normed=pltpu.VMEM((2 * RETS * 16, feat), bf),
        up_w=pltpu.VMEM((BLOCKS, feat, ffe // BLOCKS), bf),
        down_w=pltpu.VMEM((BLOCKS, ffe // BLOCKS, feat), bf),
        table=pltpu.VMEM((2 * RETS, 16, feat), bf),
        arrived=pltpu.VMEM((GROUPS, 2, 16, feat), bf),
        arrived_third=pltpu.VMEM((GROUPS, CAP - 2, 16, feat), bf),
        leaving=pltpu.VMEM(slots, bf),
        own=pltpu.VMEM(chunk, bf),
        picked=pltpu.VMEM((requests, RETS, 16, feat), bf),
        wk=pltpu.VMEM((feat, width), bf),
        wv=pltpu.VMEM((feat, width), bf),
        q=pltpu.VMEM(queries.shape, bf),
        go=pltpu.VMEM(queries.shape, bf),
        ctx=pltpu.VMEM(queries.shape, bf),
        gq=pltpu.VMEM(queries.shape, bf),
        keys=pltpu.VMEM((size * 128, width), bf),
        values=pltpu.VMEM((size * 128, width), bf),
        acc_k=pltpu.VMEM((feat, width), f32),
        acc_v=pltpu.VMEM((feat, width), f32),
        part=pltpu.VMEM((requests, SIDE, 2, 16, feat), bf),
        sib=pltpu.VMEM((SIDE,) + chunk, bf),
        far=pltpu.VMEM(chunk, bf),
        near_up=pltpu.VMEM(chunk, bf),
        near_down=pltpu.VMEM(chunk, bf),
        total=pltpu.VMEM(chunk, bf),
        arrived_b=pltpu.VMEM(slots, bf),
        gw=pltpu.VMEM((SIDE, SIDE, 2) + block, bf),
        w_in=pltpu.VMEM((2, SIDE, SIDE) + block, bf),
        w_half=pltpu.VMEM((2, SIDE) + block, bf),
        w_end=pltpu.VMEM((2, SIDE) + block, bf),
        pick=pltpu.VMEM((2 * RETS * 16, GROUPS * CAP * 16), bf),
        up_sem=dma,
        down_sem=dma,
        load_sem=dma((5,)),
        scalar_sem=dma((2,)),
        keep_sem=dma((STEPS,)),
        out_sem=dma((2,)),
    )
    for name, (send, recv) in dict(
        id=((), ()),
        raw=((), ()),
        seq=((2,), (2,)),
        up=((), (STEPS, 2)),
        dn=((), (STEPS, 2)),
        far=((), (STEPS,)),
        sib=((), (STEPS,)),
        swap=((2,), (2, STEPS)),
        rfar=((2,), (2, STEPS)),
        near=((2,), (2, STEPS)),
        w=((2, SIDE), (2, SIDE)),
        w2=((2, SIDE), (2, SIDE)),
        back=((2,), (2,)),
        home=((2,), (2,)),
    ).items():
        scratch[name + "_send"] = dma(send) if send else dma
        scratch[name + "_recv"] = dma(recv) if recv else dma
    names = tuple(ins) + tuple(outs) + tuple(scratch)
    return pl.pallas_call(
        functools.partial(kernel, names),
        out_shape=tuple(jax.ShapeDtypeStruct(s, t) for _, s, t in outs.values()),
        in_specs=list(ins.values()),
        out_specs=tuple(s for s, _, _ in outs.values()),
        scratch_shapes=list(scratch.values()),
        compiler_params=pltpu.CompilerParams(
            collective_id=0, has_side_effects=True, vmem_limit_bytes=60 * MIB
        ),
        name="fused",
    )(
        queries,
        grad_ctx,
        neighbours.reshape(2, RETS, 16, feat),
        up_weight,
        down_weight,
        key_weight,
        value_weight,
        group_ids,
        slot_ids,
    )


def deliver_kernel(*refs):
    count = len(refs) // 3
    sems = refs[-1]
    incoming = [
        pltpu.make_async_copy(refs[i], refs[2 * count + i], sems.at[0, i]) for i in range(count)
    ]
    outgoing = [
        pltpu.make_async_copy(refs[2 * count + i], refs[count + i], sems.at[1, i])
        for i in range(count)
    ]
    for copy in incoming:
        copy.start()
    for i in range(count):
        incoming[i].wait()
        outgoing[i].start()
    for copy in outgoing:
        copy.wait()


def deliver(arrays):
    any_ = pl.BlockSpec(memory_space=pl.ANY)
    return pl.pallas_call(
        deliver_kernel,
        out_shape=tuple(jax.ShapeDtypeStruct(a.shape, a.dtype) for a in arrays),
        in_specs=[any_] * len(arrays),
        out_specs=(any_,) * len(arrays),
        scratch_shapes=[pltpu.VMEM(a.shape, a.dtype) for a in arrays]
        + [pltpu.SemaphoreType.DMA((2, len(arrays)))],
        name="deliver",
    )(*arrays)


def body(
    queries,
    grad_ctx,
    neighbours,
    up_weight,
    down_weight,
    key_weight,
    value_weight,
    group_ids,
    slot_ids,
):
    context, grad_query, home, grad_key_w, grad_value_w = deliver(
        fused(
            queries,
            grad_ctx,
            neighbours,
            up_weight,
            down_weight,
            key_weight,
            value_weight,
            group_ids.T,
            slot_ids.T,
        )
    )
    return context, grad_query, home.reshape(neighbours.shape), grad_key_w, grad_value_w


def solution(mesh):
    return jax.shard_map(
        body,
        mesh=mesh,
        in_specs=(
            P("seq", "ret"),
            P("seq", "ret"),
            P(("seq", "ret"), None, None),
            P(),
            P(),
            P(None, "ret"),
            P(None, "ret"),
            P("seq", None),
            P("seq", None),
        ),
        out_specs=(
            P("seq", "ret"),
            P("seq", "ret"),
            P(("seq", "ret"), None, None),
            P("seq", "ret"),
            P("seq", "ret"),
        ),
        check_vma=False,
    )
```

```python
import functools
import math

import jax
import jax.numpy as jnp
from jax import lax
from jax.experimental import pallas as pl
from jax.experimental.pallas import tpu as pltpu
from jax.sharding import PartitionSpec as P

HD = 128
CAP = 3
MESH = pl.DeviceIdType.MESH
SIDE = 4
GROUPS = 16
RETS = 8
STEPS = 6
BLOCKS = 7
CUT = 512
EARLY = 3
LAG_PART = 1
MIX = 3
MIB = 1024 * 1024


def ahead(seq, d):
    y, x = seq // SIDE, seq % SIDE
    return ((y + d // SIDE) % SIDE) * SIDE + (x + d % SIDE) % SIDE


def behind(seq, d):
    y, x = seq // SIDE, seq % SIDE
    return ((y + SIDE - d // SIDE) % SIDE) * SIDE + (x + SIDE - d % SIDE) % SIDE


def each_group(step):
    loop(1, GROUPS, lambda d: step(d * MIX % GROUPS))


def loop(low, high, step):
    def run(i, carry):
        step(i)
        return carry

    lax.fori_loop(low, high, run, 0)


def greet(seq, ret):
    barrier = pltpu.get_barrier_semaphore()

    def to_seq(d):
        pl.semaphore_signal(barrier, inc=1, device_id=(ahead(seq, d), ret), device_id_type=MESH)

    def to_ret(d):
        pl.semaphore_signal(barrier, inc=1, device_id=(seq, (ret + d) % RETS), device_id_type=MESH)

    loop(1, GROUPS, to_seq)
    loop(1, RETS, to_ret)
    return lambda: pl.semaphore_wait(barrier, GROUPS + RETS - 2)


def drain(like, sem):
    pltpu.make_async_copy(like, like, sem).wait()


def remote(src, dst, send, recv, to):
    return pltpu.make_async_remote_copy(
        src_ref=src,
        dst_ref=dst,
        send_sem=send,
        recv_sem=recv,
        device_id=to,
        device_id_type=MESH,
    )


NT = (((1,), (1,)), ((), ()))
TN = (((0,), (0,)), ((), ()))


def dot(a, b, dims=(((1,), (0,)), ((), ()))):
    return lax.dot_general(a, b, dims, preferred_element_type=jnp.float32)


class Refs:
    def __init__(self, names, refs):
        self.__dict__.update(zip(names, refs))


def kernel(names, *refs):
    r = Refs(names, refs)
    seq, ret = lax.axis_index("seq"), lax.axis_index("ret")
    z, core = ret // 2, ret % 2
    above, below, facing = (z + 1) % SIDE, (z + SIDE - 1) % SIDE, (z + 2) % SIDE
    sibling = (seq, 2 * z + 1 - core)
    up_to, down_to = (seq, 2 * above + core), (seq, 2 * below + core)
    requests = r.own.shape[0]
    size = requests // STEPS
    half = size // 2
    feat = r.own.shape[-1]

    def up_load(j):
        width = r.up_w.shape[-1]
        return pltpu.make_async_copy(
            r.up_weight.at[:, pl.ds(j * width, width)], r.up_w.at[j], r.up_sem
        )

    def down_load(j):
        depth = r.down_w.shape[1]
        return pltpu.make_async_copy(
            r.down_weight.at[pl.ds(j * depth, depth)], r.down_w.at[j], r.down_sem
        )

    loads = [
        pltpu.make_async_copy(a, b, r.load_sem.at[i])
        for i, (a, b) in enumerate(
            (
                (r.key_weight, r.wk),
                (r.value_weight, r.wv),
                (r.queries, r.q),
                (r.grad_ctx, r.go),
                (r.neighbours.at[:, ret], r.raw.at[pl.ds(2 * ret, 2)]),
            )
        )
    ]
    loads[4].start()

    greeted = greet(seq, ret)

    targets = [r.group_ids[i % 2, i // 2] for i in range(requests)]
    slots = [r.slot_ids[i % 2, i // 2] for i in range(requests)]
    lane = lax.broadcasted_iota(jnp.int32, (8, 128), 1)
    wanted = jnp.full((8, 128), -1, jnp.int32)
    source = jnp.zeros((8, 128), jnp.int32)
    for i in range(requests):
        count = jnp.int32(0)
        for j in range(i):
            count += (targets[j] == targets[i]).astype(jnp.int32)
        at = targets[i] * CAP + count
        r.position[i] = at
        wanted = jnp.where(lane == at, slots[i], wanted)
        source = jnp.where(lane == at, i, source)
    r.wanted[...] = wanted
    r.source_v[...] = source
    to_source = pltpu.make_async_copy(r.source_v, r.source, r.scalar_sem.at[1])
    to_source.start()

    def id_copy(d, dest, slot):
        return remote(r.wanted, r.served.at[slot], r.id_send, r.id_recv, (dest, ret))

    def raw_copy(d, dest, slot):
        return remote(
            r.neighbours.at[:, dest],
            r.raw.at[pl.ds(2 * slot, 2)],
            r.raw_send,
            r.raw_recv,
            (seq, dest),
        )

    greeted()
    loop(1, RETS, lambda d: raw_copy(d, (ret + d) % RETS, ret).start())
    loop(1, GROUPS, lambda d: id_copy(d, ahead(seq, d), seq).start())
    for j in range(BLOCKS):
        up_load(j).start()
        down_load(j).start()
    r.served[seq] = wanted
    drain(r.served.at[pl.ds(0, GROUPS - 1)], r.id_recv)
    drain(r.served.at[pl.ds(0, GROUPS - 1)], r.id_send)
    to_scalar = pltpu.make_async_copy(r.served, r.served_s, r.scalar_sem.at[0])
    to_scalar.start()
    loads[4].wait()
    drain(r.raw.at[pl.ds(0, 2 * (RETS - 1))], r.raw_recv)
    drain(r.raw.at[pl.ds(0, 2 * (RETS - 1))], r.raw_send)

    drain(r.up_w, r.up_sem)
    drain(r.down_w, r.down_sem)
    for i in range(4):
        loads[i].start()

    inputs = r.raw[...].reshape(-1, feat).astype(jnp.float32)
    normed = inputs * lax.rsqrt(jnp.mean(inputs * inputs, axis=-1, keepdims=True) + 1e-06)
    r.normed[...] = normed.astype(jnp.bfloat16)
    before = dot(r.normed[...], r.up_w[0])
    encoding = None
    for j in range(BLOCKS):
        following = dot(r.normed[...], r.up_w[j + 1]) if j < BLOCKS - 1 else None
        added = dot(jax.nn.gelu(before).astype(jnp.bfloat16), r.down_w[j])
        encoding = added if encoding is None else encoding + added
        before = following
    encoding = r.raw[...].reshape(-1, feat).astype(jnp.float32) + encoding
    r.table[...] = encoding.astype(jnp.bfloat16).reshape(r.table.shape)
    to_source.wait()
    to_scalar.wait()

    def asked(s, k):
        return r.served_s[s, 0, seq * CAP + k]

    def seq_copy(e, d, dest, slot):
        places = pl.ds(0, 2) if e == 0 else pl.ds(2, CAP - 2)
        return remote(
            r.leaving.at[dest, places],
            (r.arrived if e == 0 else r.arrived_third).at[slot],
            r.seq_send.at[e],
            r.seq_recv.at[e],
            (dest, ret),
        )

    def serve(e):
        def one(d):
            dest = ahead(seq, d)
            for k in ((0, 1), range(2, CAP))[e]:
                r.leaving[dest, k] = r.table[jnp.maximum(asked(dest, k), 0)]
            seq_copy(e, d, dest, seq).start()

        each_group(one)

    serve(0)
    serve(1)
    for k in range(CAP):
        mine = r.table[jnp.maximum(asked(seq, k), 0)]
        if k < 2:
            r.arrived[seq, k] = mine
        else:
            r.arrived_third[seq, k - 2] = mine

    def first(i):
        at = r.position[i]
        r.own[i] = r.arrived[at // CAP, jnp.minimum(at % CAP, 1)]

    def compact(i):
        at = r.position[i]
        group, place = at // CAP, at % CAP
        r.own[i] = jnp.where(
            place < 2, r.arrived[group, jnp.minimum(place, 1)], r.arrived_third[group, 0]
        )

    def rows(g, h):
        return pl.ds(g * size + h * half, half)

    def own_up(g, h, held):
        return remote(
            r.own.at[rows(g, h)],
            r.picked.at[rows(g, h), 2 * held + core],
            r.up_send,
            r.up_recv.at[g, h],
            up_to,
        )

    def own_down(g, h, held):
        return remote(
            r.own.at[rows(g, h)],
            r.picked.at[rows(g, h), 2 * held + core],
            r.dn_send,
            r.dn_recv.at[g, h],
            down_to,
        )

    def relay(g, h, held):
        return remote(
            r.picked.at[rows(g, h), 2 * held + core],
            r.picked.at[rows(g, h), 2 * held + core],
            r.far_send,
            r.far_recv.at[g],
            down_to if h else up_to,
        )

    def across(g, o, held, side):
        whole = pl.ds(g * size, size)
        source = r.picked.at[whole, 2 * held + side]
        return remote(
            r.own.at[whole] if o == 0 else source,
            source,
            r.sib_send,
            r.sib_recv.at[g],
            sibling,
        )

    def keep(g):
        whole = pl.ds(g * size, size)
        return pltpu.make_async_copy(
            r.own.at[whole], r.picked.at[whole, ret], r.keep_sem.at[g]
        )

    def send_own(g):
        own_up(g, 0, z).start()
        own_down(g, 1, z).start()
        own_up(g, 1, z).start()
        own_down(g, 0, z).start()
        across(g, 0, z, core).start()
        keep(g).start()

    def pass_on(g):
        own_up(g, 0, below).wait_recv()
        relay(g, 0, below).start()
        own_down(g, 1, above).wait_recv()
        relay(g, 1, above).start()
        own_up(g, 1, below).wait_recv()
        across(g, 1, below, core).start()
        own_down(g, 0, above).wait_recv()
        across(g, 2, above, core).start()

    def pass_far(g):
        drain(r.own.at[pl.ds(0, size)], r.far_recv.at[g])
        across(g, 3, facing, core).start()

    def settle(g):
        keep(g).wait()
        drain(r.picked.at[pl.ds(0, size), pl.ds(0, SIDE)], r.sib_recv.at[g])

    cols = (pl.ds(0, CUT), pl.ds(CUT, feat - CUT))

    def swap(p, g, o):
        whole = pl.ds(g * size, size)
        return remote(
            r.part.at[whole, (z + o) % SIDE, 1 - core, :, cols[p]],
            r.sib.at[o, whole, :, cols[p]],
            r.swap_send.at[p],
            r.swap_recv.at[p, g],
            sibling,
        )

    def ring_copy(send, recv, dst, at, to):

        def copy(p, g, h):
            return remote(
                r.part.at[rows(g, h), at, core, :, cols[p]],
                dst.at[rows(g, h), :, cols[p]],
                send.at[p],
                recv.at[p, g],
                to(h),
            )

        return copy

    far_copy = ring_copy(r.rfar_send, r.rfar_recv, r.far, facing, lambda h: down_to if h else up_to)
    up_copy = ring_copy(r.near_send, r.near_recv, r.near_up, above, lambda h: up_to)
    down_copy = ring_copy(r.near_send, r.near_recv, r.near_down, below, lambda h: down_to)

    def merge(p, g, o):
        at = (z + o) % SIDE
        whole = pl.ds(g * size, size)
        mine = r.part[whole, at, core, :, cols[p]].astype(jnp.float32)
        other = r.sib[o, whole, :, cols[p]].astype(jnp.float32)
        r.part[whole, at, core, :, cols[p]] = (mine + other).astype(jnp.bfloat16)

    def merge_all(p, g):
        drain(r.sib.at[:, pl.ds(0, size), :, cols[p]], r.swap_recv.at[p, g])
        merge(p, g, 2)
        far_copy(p, g, 0).start()
        far_copy(p, g, 1).start()
        merge(p, g, 1)
        up_copy(p, g, 1).start()
        merge(p, g, 3)
        down_copy(p, g, 0).start()
        merge(p, g, 0)

    def add_far(p, g):
        drain(r.far.at[pl.ds(0, size), :, cols[p]], r.rfar_recv.at[p, g])
        for h in range(2):
            at = below if h else above
            mine = r.part[rows(g, h), at, core, :, cols[p]].astype(jnp.float32)
            other = r.far[rows(g, h), :, cols[p]].astype(jnp.float32)
            r.part[rows(g, h), at, core, :, cols[p]] = (mine + other).astype(jnp.bfloat16)
            (down_copy if h else up_copy)(p, g, h).start()

    def finish(p, g):
        drain(r.sib.at[pl.ds(0, 2), pl.ds(0, size), :, cols[p]], r.near_recv.at[p, g])
        whole = pl.ds(g * size, size)
        r.total[whole, :, cols[p]] = (
            r.part[whole, z, core, :, cols[p]].astype(jnp.float32)
            + r.near_up[whole, :, cols[p]].astype(jnp.float32)
            + r.near_down[whole, :, cols[p]].astype(jnp.float32)
        ).astype(jnp.bfloat16)

    def project(p, g):
        gk, gv = r.up_w[g, : size * 128, :], r.down_w[g, :, : r.wk.shape[1]]
        part = dot(gk, r.wk[cols[p], :], NT) + dot(gv, r.wv[cols[p], :], NT)
        r.part[pl.ds(g * size, size), :, :, :, cols[p]] = part.astype(jnp.bfloat16).reshape(
            size, SIDE, 2, 16, part.shape[1]
        )
        for o in (2, 1, 3, 0):
            swap(p, g, o).start()

    def result_copies(g):
        tokens = pl.ds(g * (size * 32), size * 32)
        return (
            pltpu.make_async_copy(r.ctx.at[tokens], r.context.at[tokens], r.out_sem.at[0]),
            pltpu.make_async_copy(r.gq.at[tokens], r.grad_query.at[tokens], r.out_sem.at[1]),
        )

    def compute(g):
        weight_grads(r, g, size)
        for copy in result_copies(g):
            copy.start()

    def at_step(g, step):
        @pl.when((g >= 0) & (g < STEPS))
        def _():
            step(g)

    drain(r.arrived.at[pl.ds(0, GROUPS - 1)], r.seq_recv.at[0])
    drain(r.arrived.at[pl.ds(0, GROUPS - 1)], r.seq_send.at[0])
    loop(0, size, first)
    send_own(0)
    pass_on(0)
    for i in range(4):
        loads[i].wait()
    drain(r.arrived_third.at[pl.ds(0, GROUPS - 1)], r.seq_recv.at[1])
    drain(r.arrived_third.at[pl.ds(0, GROUPS - 1)], r.seq_send.at[1])
    loop(size, requests, compact)

    def tock(t):
        for p in range(2):
            begin = LAG_PART + p * STEPS
            at_step(t - begin - 6, lambda g: finish(p, g))
            at_step(t - begin - 4, lambda g: add_far(p, g))
            at_step(t - begin - 2, lambda g: merge_all(p, g))
            at_step(t - begin, lambda g: project(p, g))

    def tick(t):
        at_step(t + 1, pass_on)
        at_step(t + EARLY, send_own)
        settle(t)
        tock(t)
        attend(r, t, size)
        at_step(t + 1, pass_far)
        compute(t)

    for g in range(1, EARLY):
        send_own(g)
    pass_far(0)
    loop(0, STEPS, tick)

    y, x = seq // SIDE, seq % SIDE
    each = feat // GROUPS
    wide = r.acc_k.shape[1] // 2
    for j in range(GROUPS):
        block = slice(each * j, each * j + each)
        for h in range(2):
            col = slice(wide * h, wide * h + wide)
            r.gw[j // SIDE, j % SIDE, h] = jnp.concatenate(
                [r.acc_k[block, col], r.acc_v[block, col]], axis=0
            ).astype(jnp.bfloat16)

    def along_x(d):
        return (y * SIDE + (x + d) % SIDE, ret)

    def along_y(d):
        return (((y + d) % SIDE) * SIDE + x, ret)

    def w_copy(h, d):
        return remote(
            r.gw.at[(y + d) % SIDE, :, 1] if h else r.gw.at[:, (x + d) % SIDE, 0],
            r.w_in.at[h, d],
            r.w_send.at[h, d],
            r.w_recv.at[h, d],
            along_y(d) if h else along_x(d),
        )

    def w_last(h, d):
        return remote(
            r.w_half.at[h, (x + d) % SIDE if h else (y + d) % SIDE],
            r.w_end.at[h, d],
            r.w2_send.at[h, d],
            r.w2_recv.at[h, d],
            along_x(d) if h else along_y(d),
        )

    def w_middle():
        for h in range(2):
            for d in range(1, SIDE):
                w_copy(h, d).wait()
            for j in range(SIDE):
                mine = r.gw[y, j, 1] if h else r.gw[j, x, 0]
                summed = mine.astype(jnp.float32)
                for d in range(1, SIDE):
                    summed = summed + r.w_in[h, d, j].astype(jnp.float32)
                r.w_half[h, j] = summed.astype(jnp.bfloat16)
            for d in range(1, SIDE):
                w_last(h, d).start()

    for d in range(1, SIDE):
        for h in range(2):
            w_copy(h, d).start()

    def back_copy(p, d, dest, slot):
        return remote(
            r.leaving.at[dest, :, :, cols[p]],
            r.arrived_b.at[slot, :, :, cols[p]],
            r.back_send.at[p],
            r.back_recv.at[p],
            (dest, ret),
        )

    def give_back(p):
        def give(d):
            dest = ahead(seq, d)
            for k in range(CAP):
                r.leaving[dest, k, :, cols[p]] = r.total[r.source[0, dest * CAP + k], :, cols[p]]
            back_copy(p, d, dest, seq).start()

        each_group(give)
        for k in range(CAP):
            r.arrived_b[seq, k, :, cols[p]] = r.total[r.source[0, seq * CAP + k], :, cols[p]]

    def last_tick(t):
        tock(t)
        pl.when(t == LAG_PART + STEPS + 6)(w_middle)
        pl.when(t == LAG_PART + STEPS + 6)(lambda: give_back(0))

    loop(STEPS, LAG_PART + 2 * STEPS + 6, last_tick)
    give_back(1)

    row = lax.broadcasted_iota(jnp.int32, r.pick.shape, 0)
    col = lax.broadcasted_iota(jnp.int32, r.pick.shape, 1)
    place = lax.broadcasted_iota(jnp.int32, (1, r.pick.shape[1]), 1) // 16
    owner = jnp.full(place.shape, -1, jnp.int32)
    for s in range(GROUPS):
        for k in range(CAP):
            owner = jnp.where(place == s * CAP + k, asked(s, k), owner)
    r.pick[...] = jnp.where((row // 16 == owner) & (row % 16 == col % 16), 1.0, 0.0).astype(
        jnp.bfloat16
    )

    def home_copy(p, d, dest, slot):
        return remote(
            r.table.at[pl.ds(2 * dest, 2), :, cols[p]],
            r.home.at[:, slot, :, cols[p]],
            r.home_send.at[p],
            r.home_recv.at[p],
            (seq, dest),
        )

    def go_home(p):
        drain(r.arrived_b.at[pl.ds(0, GROUPS - 1), :, :, cols[p]], r.back_recv.at[p])
        arrived = r.arrived_b[:, :, :, cols[p]]
        summed = dot(r.pick[...], arrived.reshape(r.pick.shape[1], arrived.shape[-1]))
        r.table[:, :, cols[p]] = summed.astype(jnp.bfloat16).reshape(
            2 * RETS, 16, arrived.shape[-1]
        )
        loop(1, RETS, lambda d: home_copy(p, d, (ret + d) % RETS, ret).start())
        for k in range(2):
            r.home[k, ret, :, cols[p]] = r.table[2 * ret + k, :, cols[p]]

    go_home(0)
    for h in range(2):
        summed = r.w_half[h, x if h else y].astype(jnp.float32)
        for d in range(1, SIDE):
            w_last(h, d).wait()
            summed = summed + r.w_end[h, d].astype(jnp.float32)
        r.gk_out[:, wide * h : wide * h + wide] = summed[:each]
        r.gv_out[:, wide * h : wide * h + wide] = summed[each:]
    go_home(1)
    for p in range(2):
        sent_home = r.home.at[:, pl.ds(0, RETS - 1), :, cols[p]]
        drain(sent_home, r.home_recv.at[p])
        drain(sent_home, r.home_send.at[p])
        drain(r.arrived_b.at[pl.ds(0, GROUPS - 1), :, :, cols[p]], r.back_send.at[p])
        drain(r.sib.at[:, :, :, cols[p]], r.swap_send.at[p])
        drain(r.far.at[:, :, cols[p]], r.rfar_send.at[p])
        drain(r.sib.at[pl.ds(0, 2), :, :, cols[p]], r.near_send.at[p])
    drain(r.own, r.up_send)
    drain(r.own, r.dn_send)
    drain(r.own, r.far_send)
    drain(r.picked.at[:, pl.ds(0, SIDE)], r.sib_send)
    drain(r.ctx, r.out_sem.at[0])
    drain(r.gq, r.out_sem.at[1])


def picked_rows(r, g, count):
    first = g * (r.own.shape[0] // STEPS)
    return r.picked[pl.ds(first, count)].reshape(count * 128, r.wk.shape[0])


def attend(r, g, size):
    feat, width = r.wk.shape
    heads = width // HD
    spans = size // 2
    scale = 1.0 / math.sqrt(HD)
    rows = picked_rows(r, g, size)
    r.keys[...] = dot(rows, r.wk[...]).astype(jnp.bfloat16)
    r.values[...] = dot(rows, r.wv[...]).astype(jnp.bfloat16)
    gkeys, gvalues = r.up_w.at[g, : size * 128], r.down_w.at[g, :, :width]
    for c in range(spans):
        tok = pl.ds(pl.multiple_of((g * spans + c) * 64, 64), 64)
        row = slice(256 * c, 256 * c + 256)
        cols = [slice(HD * h, HD * h + HD) for h in range(heads)]
        scores = [dot(r.q[tok, col], r.keys[row, col], NT) for col in cols]
        gps = [dot(r.go[tok, col], r.values[row, col], NT) for col in cols]
        weights = [jnp.exp(s * scale) for s in scores]
        weights = [w / jnp.sum(w, axis=-1, keepdims=True) for w in weights]
        probs = [w.astype(jnp.bfloat16) for w in weights]
        mixed = [
            (w * (gp - jnp.sum(w * gp, axis=-1, keepdims=True)) * scale).astype(jnp.bfloat16)
            for w, gp in zip(weights, gps)
        ]
        for col, p, m in zip(cols, probs, mixed):
            r.ctx[tok, col] = dot(p, r.values[row, col]).astype(jnp.bfloat16)
            r.gq[tok, col] = dot(m, r.keys[row, col]).astype(jnp.bfloat16)
            gkeys[row, col] = dot(m, r.q[tok, col], TN).astype(jnp.bfloat16)
            gvalues[row, col] = dot(p, r.go[tok, col], TN).astype(jnp.bfloat16)


def weight_grads(r, g, size):
    width = r.wk.shape[1]

    @pl.when(g % 2 == 1)
    def _():
        pair = picked_rows(r, g - 1, 2 * size)
        gk = r.up_w[pl.ds(g - 1, 2), : size * 128].reshape(-1, width)
        gv = r.down_w[pl.ds(g - 1, 2), :, :width].reshape(-1, width)
        add_k = dot(pair, gk, TN)
        add_v = dot(pair, gv, TN)

        @pl.when(g == 1)
        def _():
            r.acc_k[...] = add_k
            r.acc_v[...] = add_v

        @pl.when(g > 1)
        def _():
            r.acc_k[...] += add_k
            r.acc_v[...] += add_v


def fused(
    queries,
    grad_ctx,
    neighbours,
    up_weight,
    down_weight,
    key_weight,
    value_weight,
    group_ids,
    slot_ids,
):
    feat, ffe = up_weight.shape
    requests = group_ids.shape[0] * group_ids.shape[1]
    tokens, width = queries.shape
    size = requests // STEPS
    bf, f32 = jnp.bfloat16, jnp.float32
    dma = pltpu.SemaphoreType.DMA
    slots = (GROUPS, CAP, 16, feat)
    chunk = (requests, 16, feat)
    block = (2 * feat // GROUPS, width // 2)
    any_, vmem, smem = (
        pl.BlockSpec(memory_space=s) for s in (pl.ANY, pltpu.VMEM, pltpu.SMEM)
    )
    ins = dict(
        queries=any_,
        grad_ctx=any_,
        neighbours=any_,
        up_weight=any_,
        down_weight=any_,
        key_weight=any_,
        value_weight=any_,
        group_ids=smem,
        slot_ids=smem,
    )
    outs = dict(
        context=(any_, queries.shape, bf),
        grad_query=(any_, queries.shape, bf),
        home=(vmem, (2, RETS, 16, feat), bf),
        gk_out=(vmem, (feat // GROUPS, width), f32),
        gv_out=(vmem, (feat // GROUPS, width), f32),
    )
    scratch = dict(
        wanted=pltpu.VMEM((8, 128), jnp.int32),
        source_v=pltpu.VMEM((8, 128), jnp.int32),
        source=pltpu.SMEM((8, 128), jnp.int32),
        position=pltpu.SMEM((requests,), jnp.int32),
        served=pltpu.VMEM((GROUPS, 8, 128), jnp.int32),
        served_s=pltpu.SMEM((GROUPS, 8, 128), jnp.int32),
        raw=pltpu.VMEM((2 * RETS, 16, feat), bf),
        normed=pltpu.VMEM((2 * RETS * 16, feat), bf),
        up_w=pltpu.VMEM((BLOCKS, feat, ffe // BLOCKS), bf),
        down_w=pltpu.VMEM((BLOCKS, ffe // BLOCKS, feat), bf),
        table=pltpu.VMEM((2 * RETS, 16, feat), bf),
        arrived=pltpu.VMEM((GROUPS, 2, 16, feat), bf),
        arrived_third=pltpu.VMEM((GROUPS, CAP - 2, 16, feat), bf),
        leaving=pltpu.VMEM(slots, bf),
        own=pltpu.VMEM(chunk, bf),
        picked=pltpu.VMEM((requests, RETS, 16, feat), bf),
        wk=pltpu.VMEM((feat, width), bf),
        wv=pltpu.VMEM((feat, width), bf),
        q=pltpu.VMEM(queries.shape, bf),
        go=pltpu.VMEM(queries.shape, bf),
        ctx=pltpu.VMEM(queries.shape, bf),
        gq=pltpu.VMEM(queries.shape, bf),
        keys=pltpu.VMEM((size * 128, width), bf),
        values=pltpu.VMEM((size * 128, width), bf),
        acc_k=pltpu.VMEM((feat, width), f32),
        acc_v=pltpu.VMEM((feat, width), f32),
        part=pltpu.VMEM((requests, SIDE, 2, 16, feat), bf),
        sib=pltpu.VMEM((SIDE,) + chunk, bf),
        far=pltpu.VMEM(chunk, bf),
        near_up=pltpu.VMEM(chunk, bf),
        near_down=pltpu.VMEM(chunk, bf),
        total=pltpu.VMEM(chunk, bf),
        arrived_b=pltpu.VMEM(slots, bf),
        gw=pltpu.VMEM((SIDE, SIDE, 2) + block, bf),
        w_in=pltpu.VMEM((2, SIDE, SIDE) + block, bf),
        w_half=pltpu.VMEM((2, SIDE) + block, bf),
        w_end=pltpu.VMEM((2, SIDE) + block, bf),
        pick=pltpu.VMEM((2 * RETS * 16, GROUPS * CAP * 16), bf),
        up_sem=dma,
        down_sem=dma,
        load_sem=dma((5,)),
        scalar_sem=dma((2,)),
        keep_sem=dma((STEPS,)),
        out_sem=dma((2,)),
    )
    for name, (send, recv) in dict(
        id=((), ()),
        raw=((), ()),
        seq=((2,), (2,)),
        up=((), (STEPS, 2)),
        dn=((), (STEPS, 2)),
        far=((), (STEPS,)),
        sib=((), (STEPS,)),
        swap=((2,), (2, STEPS)),
        rfar=((2,), (2, STEPS)),
        near=((2,), (2, STEPS)),
        w=((2, SIDE), (2, SIDE)),
        w2=((2, SIDE), (2, SIDE)),
        back=((2,), (2,)),
        home=((2,), (2,)),
    ).items():
        scratch[name + "_send"] = dma(send) if send else dma
        scratch[name + "_recv"] = dma(recv) if recv else dma
    names = tuple(ins) + tuple(outs) + tuple(scratch)
    return pl.pallas_call(
        functools.partial(kernel, names),
        out_shape=tuple(jax.ShapeDtypeStruct(s, t) for _, s, t in outs.values()),
        in_specs=list(ins.values()),
        out_specs=tuple(s for s, _, _ in outs.values()),
        scratch_shapes=list(scratch.values()),
        compiler_params=pltpu.CompilerParams(
            collective_id=0, has_side_effects=True, vmem_limit_bytes=60 * MIB
        ),
        name="fused",
    )(
        queries,
        grad_ctx,
        neighbours.reshape(2, RETS, 16, feat),
        up_weight,
        down_weight,
        key_weight,
        value_weight,
        group_ids,
        slot_ids,
    )


def deliver_kernel(*refs):
    count = len(refs) // 3
    sems = refs[-1]
    incoming = [
        pltpu.make_async_copy(refs[i], refs[2 * count + i], sems.at[0, i]) for i in range(count)
    ]
    outgoing = [
        pltpu.make_async_copy(refs[2 * count + i], refs[count + i], sems.at[1, i])
        for i in range(count)
    ]
    for copy in incoming:
        copy.start()
    for i in range(count):
        incoming[i].wait()
        outgoing[i].start()
    for copy in outgoing:
        copy.wait()


def deliver(arrays):
    any_ = pl.BlockSpec(memory_space=pl.ANY)
    return pl.pallas_call(
        deliver_kernel,
        out_shape=tuple(jax.ShapeDtypeStruct(a.shape, a.dtype) for a in arrays),
        in_specs=[any_] * len(arrays),
        out_specs=(any_,) * len(arrays),
        scratch_shapes=[pltpu.VMEM(a.shape, a.dtype) for a in arrays]
        + [pltpu.SemaphoreType.DMA((2, len(arrays)))],
        name="deliver",
    )(*arrays)


def body(
    queries,
    grad_ctx,
    neighbours,
    up_weight,
    down_weight,
    key_weight,
    value_weight,
    group_ids,
    slot_ids,
):
    context, grad_query, home, grad_key_w, grad_value_w = deliver(
        fused(
            queries,
            grad_ctx,
            neighbours,
            up_weight,
            down_weight,
            key_weight,
            value_weight,
            group_ids.T,
            slot_ids.T,
        )
    )
    return context, grad_query, home.reshape(neighbours.shape), grad_key_w, grad_value_w


def solution(mesh):
    return jax.shard_map(
        body,
        mesh=mesh,
        in_specs=(
            P("seq", "ret"),
            P("seq", "ret"),
            P(("seq", "ret"), None, None),
            P(),
            P(),
            P(None, "ret"),
            P(None, "ret"),
            P("seq", None),
            P("seq", None),
        ),
        out_specs=(
            P("seq", "ret"),
            P("seq", "ret"),
            P(("seq", "ret"), None, None),
            P("seq", "ret"),
            P("seq", "ret"),
        ),
        check_vma=False,
    )
```

```python
import functools
import math

import jax
import jax.numpy as jnp
from jax import lax
from jax.experimental import pallas as pl
from jax.experimental.pallas import tpu as pltpu
from jax.sharding import PartitionSpec as P

HD = 128
CAP = 3
MESH = pl.DeviceIdType.MESH
SIDE = 4
GROUPS = 16
RETS = 8
STEPS = 6
BLOCKS = 7
CUT = 512
EARLY = 3
LAG_PART = 1
MIX = 3
MIB = 1024 * 1024


def ahead(seq, d):
    y, x = seq // SIDE, seq % SIDE
    return ((y + d // SIDE) % SIDE) * SIDE + (x + d % SIDE) % SIDE


def behind(seq, d):
    y, x = seq // SIDE, seq % SIDE
    return ((y + SIDE - d // SIDE) % SIDE) * SIDE + (x + SIDE - d % SIDE) % SIDE


def each_group(step):
    loop(1, GROUPS, lambda d: step(d * MIX % GROUPS))


def loop(low, high, step):
    def run(i, carry):
        step(i)
        return carry

    lax.fori_loop(low, high, run, 0)


def greet(seq, ret):
    barrier = pltpu.get_barrier_semaphore()

    def to_seq(d):
        pl.semaphore_signal(barrier, inc=1, device_id=(ahead(seq, d), ret), device_id_type=MESH)

    def to_ret(d):
        pl.semaphore_signal(barrier, inc=1, device_id=(seq, (ret + d) % RETS), device_id_type=MESH)

    loop(1, GROUPS, to_seq)
    loop(1, RETS, to_ret)
    return lambda: pl.semaphore_wait(barrier, GROUPS + RETS - 2)


def drain(like, sem):
    pltpu.make_async_copy(like, like, sem).wait()


def remote(src, dst, send, recv, to):
    return pltpu.make_async_remote_copy(
        src_ref=src,
        dst_ref=dst,
        send_sem=send,
        recv_sem=recv,
        device_id=to,
        device_id_type=MESH,
    )


NT = (((1,), (1,)), ((), ()))
TN = (((0,), (0,)), ((), ()))


def dot(a, b, dims=(((1,), (0,)), ((), ()))):
    return lax.dot_general(a, b, dims, preferred_element_type=jnp.float32)


class Refs:
    def __init__(self, names, refs):
        self.__dict__.update(zip(names, refs))


def kernel(names, *refs):
    r = Refs(names, refs)
    seq, ret = lax.axis_index("seq"), lax.axis_index("ret")
    z, core = ret // 2, ret % 2
    above, below, facing = (z + 1) % SIDE, (z + SIDE - 1) % SIDE, (z + 2) % SIDE
    sibling = (seq, 2 * z + 1 - core)
    up_to, down_to = (seq, 2 * above + core), (seq, 2 * below + core)
    requests = r.own.shape[0]
    size = requests // STEPS
    half = size // 2
    feat = r.own.shape[-1]

    def up_load(j):
        width = r.up_w.shape[-1]
        return pltpu.make_async_copy(
            r.up_weight.at[:, pl.ds(j * width, width)], r.up_w.at[j], r.up_sem
        )

    def down_load(j):
        depth = r.down_w.shape[1]
        return pltpu.make_async_copy(
            r.down_weight.at[pl.ds(j * depth, depth)], r.down_w.at[j], r.down_sem
        )

    loads = [
        pltpu.make_async_copy(a, b, r.load_sem.at[i])
        for i, (a, b) in enumerate(
            (
                (r.key_weight, r.wk),
                (r.value_weight, r.wv),
                (r.queries, r.q),
                (r.grad_ctx, r.go),
                (r.neighbours.at[:, ret], r.raw.at[pl.ds(2 * ret, 2)]),
            )
        )
    ]
    loads[4].start()

    greeted = greet(seq, ret)

    targets = [r.group_ids[i % 2, i // 2] for i in range(requests)]
    slots = [r.slot_ids[i % 2, i // 2] for i in range(requests)]
    lane = lax.broadcasted_iota(jnp.int32, (8, 128), 1)
    wanted = jnp.full((8, 128), -1, jnp.int32)
    source = jnp.zeros((8, 128), jnp.int32)
    for i in range(requests):
        count = jnp.int32(0)
        for j in range(i):
            count += (targets[j] == targets[i]).astype(jnp.int32)
        at = targets[i] * CAP + count
        r.position[i] = at
        wanted = jnp.where(lane == at, slots[i], wanted)
        source = jnp.where(lane == at, i, source)
    r.wanted[...] = wanted
    r.source_v[...] = source
    to_source = pltpu.make_async_copy(r.source_v, r.source, r.scalar_sem.at[1])
    to_source.start()

    def id_copy(d, dest, slot):
        return remote(r.wanted, r.served.at[slot], r.id_send, r.id_recv, (dest, ret))

    def raw_copy(d, dest, slot):
        return remote(
            r.neighbours.at[:, dest],
            r.raw.at[pl.ds(2 * slot, 2)],
            r.raw_send,
            r.raw_recv,
            (seq, dest),
        )

    greeted()
    loop(1, RETS, lambda d: raw_copy(d, (ret + d) % RETS, ret).start())
    loop(1, GROUPS, lambda d: id_copy(d, ahead(seq, d), seq).start())
    for j in range(BLOCKS):
        up_load(j).start()
        down_load(j).start()
    r.served[seq] = wanted
    drain(r.served.at[pl.ds(0, GROUPS - 1)], r.id_recv)
    drain(r.served.at[pl.ds(0, GROUPS - 1)], r.id_send)
    to_scalar = pltpu.make_async_copy(r.served, r.served_s, r.scalar_sem.at[0])
    to_scalar.start()
    loads[4].wait()
    drain(r.raw.at[pl.ds(0, 2 * (RETS - 1))], r.raw_recv)
    drain(r.raw.at[pl.ds(0, 2 * (RETS - 1))], r.raw_send)

    drain(r.up_w, r.up_sem)
    drain(r.down_w, r.down_sem)
    for i in range(4):
        loads[i].start()

    inputs = r.raw[...].reshape(-1, feat).astype(jnp.float32)
    normed = inputs * lax.rsqrt(jnp.mean(inputs * inputs, axis=-1, keepdims=True) + 1e-06)
    r.normed[...] = normed.astype(jnp.bfloat16)
    before = dot(r.normed[...], r.up_w[0])
    encoding = None
    for j in range(BLOCKS):
        following = dot(r.normed[...], r.up_w[j + 1]) if j < BLOCKS - 1 else None
        added = dot(jax.nn.gelu(before).astype(jnp.bfloat16), r.down_w[j])
        encoding = added if encoding is None else encoding + added
        before = following
    encoding = r.raw[...].reshape(-1, feat).astype(jnp.float32) + encoding
    r.table[...] = encoding.astype(jnp.bfloat16).reshape(r.table.shape)
    to_source.wait()
    to_scalar.wait()

    def asked(s, k):
        return r.served_s[s, 0, seq * CAP + k]

    def seq_copy(e, d, dest, slot):
        places = pl.ds(0, 2) if e == 0 else pl.ds(2, CAP - 2)
        return remote(
            r.leaving.at[dest, places],
            (r.arrived if e == 0 else r.arrived_third).at[slot],
            r.seq_send.at[e],
            r.seq_recv.at[e],
            (dest, ret),
        )

    def serve(e):
        def one(d):
            dest = ahead(seq, d)
            for k in ((0, 1), range(2, CAP))[e]:
                r.leaving[dest, k] = r.table[jnp.maximum(asked(dest, k), 0)]
            seq_copy(e, d, dest, seq).start()

        each_group(one)

    serve(0)
    serve(1)
    for k in range(CAP):
        mine = r.table[jnp.maximum(asked(seq, k), 0)]
        if k < 2:
            r.arrived[seq, k] = mine
        else:
            r.arrived_third[seq, k - 2] = mine

    def first(i):
        at = r.position[i]
        r.own[i] = r.arrived[at // CAP, jnp.minimum(at % CAP, 1)]

    def compact(i):
        at = r.position[i]
        group, place = at // CAP, at % CAP
        r.own[i] = jnp.where(
            place < 2, r.arrived[group, jnp.minimum(place, 1)], r.arrived_third[group, 0]
        )

    def rows(g, h):
        return pl.ds(g * size + h * half, half)

    def own_up(g, h, held):
        return remote(
            r.own.at[rows(g, h)],
            r.picked.at[rows(g, h), 2 * held + core],
            r.up_send,
            r.up_recv.at[g, h],
            up_to,
        )

    def own_down(g, h, held):
        return remote(
            r.own.at[rows(g, h)],
            r.picked.at[rows(g, h), 2 * held + core],
            r.dn_send,
            r.dn_recv.at[g, h],
            down_to,
        )

    def relay(g, h, held):
        return remote(
            r.picked.at[rows(g, h), 2 * held + core],
            r.picked.at[rows(g, h), 2 * held + core],
            r.far_send,
            r.far_recv.at[g],
            down_to if h else up_to,
        )

    def across(g, o, held, side):
        whole = pl.ds(g * size, size)
        source = r.picked.at[whole, 2 * held + side]
        return remote(
            r.own.at[whole] if o == 0 else source,
            source,
            r.sib_send,
            r.sib_recv.at[g],
            sibling,
        )

    def keep(g):
        whole = pl.ds(g * size, size)
        return pltpu.make_async_copy(
            r.own.at[whole], r.picked.at[whole, ret], r.keep_sem.at[g]
        )

    def send_own(g):
        own_up(g, 0, z).start()
        own_down(g, 1, z).start()
        own_up(g, 1, z).start()
        own_down(g, 0, z).start()
        across(g, 0, z, core).start()
        keep(g).start()

    def pass_on(g):
        own_up(g, 0, below).wait_recv()
        relay(g, 0, below).start()
        own_down(g, 1, above).wait_recv()
        relay(g, 1, above).start()
        own_up(g, 1, below).wait_recv()
        across(g, 1, below, core).start()
        own_down(g, 0, above).wait_recv()
        across(g, 2, above, core).start()

    def pass_far(g):
        drain(r.own.at[pl.ds(0, size)], r.far_recv.at[g])
        across(g, 3, facing, core).start()

    def settle(g):
        keep(g).wait()
        drain(r.picked.at[pl.ds(0, size), pl.ds(0, SIDE)], r.sib_recv.at[g])

    cols = (pl.ds(0, CUT), pl.ds(CUT, feat - CUT))

    def swap(p, g, o):
        whole = pl.ds(g * size, size)
        return remote(
            r.part.at[whole, (z + o) % SIDE, 1 - core, :, cols[p]],
            r.sib.at[o, whole, :, cols[p]],
            r.swap_send.at[p],
            r.swap_recv.at[p, g],
            sibling,
        )

    def ring_copy(send, recv, dst, at, to):

        def copy(p, g, h):
            return remote(
                r.part.at[rows(g, h), at, core, :, cols[p]],
                dst.at[rows(g, h), :, cols[p]],
                send.at[p],
                recv.at[p, g],
                to(h),
            )

        return copy

    far_copy = ring_copy(r.rfar_send, r.rfar_recv, r.far, facing, lambda h: down_to if h else up_to)
    up_copy = ring_copy(r.near_send, r.near_recv, r.near_up, above, lambda h: up_to)
    down_copy = ring_copy(r.near_send, r.near_recv, r.near_down, below, lambda h: down_to)

    def merge(p, g, o):
        at = (z + o) % SIDE
        whole = pl.ds(g * size, size)
        mine = r.part[whole, at, core, :, cols[p]].astype(jnp.float32)
        other = r.sib[o, whole, :, cols[p]].astype(jnp.float32)
        r.part[whole, at, core, :, cols[p]] = (mine + other).astype(jnp.bfloat16)

    def merge_all(p, g):
        drain(r.sib.at[:, pl.ds(0, size), :, cols[p]], r.swap_recv.at[p, g])
        merge(p, g, 2)
        far_copy(p, g, 0).start()
        far_copy(p, g, 1).start()
        merge(p, g, 1)
        up_copy(p, g, 1).start()
        merge(p, g, 3)
        down_copy(p, g, 0).start()
        merge(p, g, 0)

    def add_far(p, g):
        drain(r.far.at[pl.ds(0, size), :, cols[p]], r.rfar_recv.at[p, g])
        for h in range(2):
            at = below if h else above
            mine = r.part[rows(g, h), at, core, :, cols[p]].astype(jnp.float32)
            other = r.far[rows(g, h), :, cols[p]].astype(jnp.float32)
            r.part[rows(g, h), at, core, :, cols[p]] = (mine + other).astype(jnp.bfloat16)
            (down_copy if h else up_copy)(p, g, h).start()

    def finish(p, g):
        drain(r.sib.at[pl.ds(0, 2), pl.ds(0, size), :, cols[p]], r.near_recv.at[p, g])
        whole = pl.ds(g * size, size)
        r.total[whole, :, cols[p]] = (
            r.part[whole, z, core, :, cols[p]].astype(jnp.float32)
            + r.near_up[whole, :, cols[p]].astype(jnp.float32)
            + r.near_down[whole, :, cols[p]].astype(jnp.float32)
        ).astype(jnp.bfloat16)

    def project(p, g):
        gk, gv = r.up_w[g, : size * 128, :], r.down_w[g, :, : r.wk.shape[1]]
        part = dot(gk, r.wk[cols[p], :], NT) + dot(gv, r.wv[cols[p], :], NT)
        r.part[pl.ds(g * size, size), :, :, :, cols[p]] = part.astype(jnp.bfloat16).reshape(
            size, SIDE, 2, 16, part.shape[1]
        )
        for o in (2, 1, 3, 0):
            swap(p, g, o).start()

    def result_copies(g):
        tokens = pl.ds(g * (size * 32), size * 32)
        return (
            pltpu.make_async_copy(r.ctx.at[tokens], r.context.at[tokens], r.out_sem.at[0]),
            pltpu.make_async_copy(r.gq.at[tokens], r.grad_query.at[tokens], r.out_sem.at[1]),
        )

    def compute(g):
        weight_grads(r, g, size)
        for copy in result_copies(g):
            copy.start()

    def at_step(g, step):
        @pl.when((g >= 0) & (g < STEPS))
        def _():
            step(g)

    drain(r.arrived.at[pl.ds(0, GROUPS - 1)], r.seq_recv.at[0])
    drain(r.arrived.at[pl.ds(0, GROUPS - 1)], r.seq_send.at[0])
    loop(0, size, first)
    send_own(0)
    pass_on(0)
    for i in range(4):
        loads[i].wait()
    drain(r.arrived_third.at[pl.ds(0, GROUPS - 1)], r.seq_recv.at[1])
    drain(r.arrived_third.at[pl.ds(0, GROUPS - 1)], r.seq_send.at[1])
    loop(size, requests, compact)

    def tock(t):
        for p in range(2):
            begin = LAG_PART + p * STEPS
            at_step(t - begin - 6, lambda g: finish(p, g))
            at_step(t - begin - 4, lambda g: add_far(p, g))
            at_step(t - begin - 2, lambda g: merge_all(p, g))
            at_step(t - begin, lambda g: project(p, g))

    def tick(t):
        at_step(t + 1, pass_on)
        at_step(t + EARLY, send_own)
        settle(t)
        tock(t)
        attend(r, t, size)
        at_step(t + 1, pass_far)
        compute(t)

    for g in range(1, EARLY):
        send_own(g)
    pass_far(0)
    loop(0, STEPS, tick)

    y, x = seq // SIDE, seq % SIDE
    each = feat // GROUPS
    wide = r.acc_k.shape[1] // 2
    for j in range(GROUPS):
        block = slice(each * j, each * j + each)
        for h in range(2):
            col = slice(wide * h, wide * h + wide)
            r.gw[j // SIDE, j % SIDE, h] = jnp.concatenate(
                [r.acc_k[block, col], r.acc_v[block, col]], axis=0
            ).astype(jnp.bfloat16)

    def along_x(d):
        return (y * SIDE + (x + d) % SIDE, ret)

    def along_y(d):
        return (((y + d) % SIDE) * SIDE + x, ret)

    def w_copy(h, d):
        return remote(
            r.gw.at[(y + d) % SIDE, :, 1] if h else r.gw.at[:, (x + d) % SIDE, 0],
            r.w_in.at[h, d],
            r.w_send.at[h, d],
            r.w_recv.at[h, d],
            along_y(d) if h else along_x(d),
        )

    def w_last(h, d):
        return remote(
            r.w_half.at[h, (x + d) % SIDE if h else (y + d) % SIDE],
            r.w_end.at[h, d],
            r.w2_send.at[h, d],
            r.w2_recv.at[h, d],
            along_x(d) if h else along_y(d),
        )

    def w_middle():
        for h in range(2):
            for d in range(1, SIDE):
                w_copy(h, d).wait()
            for j in range(SIDE):
                mine = r.gw[y, j, 1] if h else r.gw[j, x, 0]
                summed = mine.astype(jnp.float32)
                for d in range(1, SIDE):
                    summed = summed + r.w_in[h, d, j].astype(jnp.float32)
                r.w_half[h, j] = summed.astype(jnp.bfloat16)
            for d in range(1, SIDE):
                w_last(h, d).start()

    for d in range(1, SIDE):
        for h in range(2):
            w_copy(h, d).start()

    def back_copy(p, d, dest, slot):
        return remote(
            r.leaving.at[dest, :, :, cols[p]],
            r.arrived_b.at[slot, :, :, cols[p]],
            r.back_send.at[p],
            r.back_recv.at[p],
            (dest, ret),
        )

    def give_back(p):
        def give(d):
            dest = ahead(seq, d)
            for k in range(CAP):
                r.leaving[dest, k, :, cols[p]] = r.total[r.source[0, dest * CAP + k], :, cols[p]]
            back_copy(p, d, dest, seq).start()

        each_group(give)
        for k in range(CAP):
            r.arrived_b[seq, k, :, cols[p]] = r.total[r.source[0, seq * CAP + k], :, cols[p]]

    def last_tick(t):
        tock(t)
        pl.when(t == LAG_PART + STEPS + 4)(w_middle)
        pl.when(t == LAG_PART + STEPS + 6)(lambda: give_back(0))

    loop(STEPS, LAG_PART + 2 * STEPS + 6, last_tick)
    give_back(1)

    row = lax.broadcasted_iota(jnp.int32, r.pick.shape, 0)
    col = lax.broadcasted_iota(jnp.int32, r.pick.shape, 1)
    place = lax.broadcasted_iota(jnp.int32, (1, r.pick.shape[1]), 1) // 16
    owner = jnp.full(place.shape, -1, jnp.int32)
    for s in range(GROUPS):
        for k in range(CAP):
            owner = jnp.where(place == s * CAP + k, asked(s, k), owner)
    r.pick[...] = jnp.where((row // 16 == owner) & (row % 16 == col % 16), 1.0, 0.0).astype(
        jnp.bfloat16
    )

    def home_copy(p, d, dest, slot):
        return remote(
            r.table.at[pl.ds(2 * dest, 2), :, cols[p]],
            r.home.at[:, slot, :, cols[p]],
            r.home_send.at[p],
            r.home_recv.at[p],
            (seq, dest),
        )

    def go_home(p):
        drain(r.arrived_b.at[pl.ds(0, GROUPS - 1), :, :, cols[p]], r.back_recv.at[p])
        arrived = r.arrived_b[:, :, :, cols[p]]
        summed = dot(r.pick[...], arrived.reshape(r.pick.shape[1], arrived.shape[-1]))
        r.table[:, :, cols[p]] = summed.astype(jnp.bfloat16).reshape(
            2 * RETS, 16, arrived.shape[-1]
        )
        loop(1, RETS, lambda d: home_copy(p, d, (ret + d) % RETS, ret).start())
        for k in range(2):
            r.home[k, ret, :, cols[p]] = r.table[2 * ret + k, :, cols[p]]

    go_home(0)
    for h in range(2):
        summed = r.w_half[h, x if h else y].astype(jnp.float32)
        for d in range(1, SIDE):
            w_last(h, d).wait()
            summed = summed + r.w_end[h, d].astype(jnp.float32)
        r.gk_out[:, wide * h : wide * h + wide] = summed[:each]
        r.gv_out[:, wide * h : wide * h + wide] = summed[each:]
    go_home(1)
    for p in range(2):
        sent_home = r.home.at[:, pl.ds(0, RETS - 1), :, cols[p]]
        drain(sent_home, r.home_recv.at[p])
        drain(sent_home, r.home_send.at[p])
        drain(r.arrived_b.at[pl.ds(0, GROUPS - 1), :, :, cols[p]], r.back_send.at[p])
        drain(r.sib.at[:, :, :, cols[p]], r.swap_send.at[p])
        drain(r.far.at[:, :, cols[p]], r.rfar_send.at[p])
        drain(r.sib.at[pl.ds(0, 2), :, :, cols[p]], r.near_send.at[p])
    drain(r.own, r.up_send)
    drain(r.own, r.dn_send)
    drain(r.own, r.far_send)
    drain(r.picked.at[:, pl.ds(0, SIDE)], r.sib_send)
    drain(r.ctx, r.out_sem.at[0])
    drain(r.gq, r.out_sem.at[1])


def picked_rows(r, g, count):
    first = g * (r.own.shape[0] // STEPS)
    return r.picked[pl.ds(first, count)].reshape(count * 128, r.wk.shape[0])


def attend(r, g, size):
    feat, width = r.wk.shape
    heads = width // HD
    spans = size // 2
    scale = 1.0 / math.sqrt(HD)
    rows = picked_rows(r, g, size)
    r.keys[...] = dot(rows, r.wk[...]).astype(jnp.bfloat16)
    r.values[...] = dot(rows, r.wv[...]).astype(jnp.bfloat16)
    gkeys, gvalues = r.up_w.at[g, : size * 128], r.down_w.at[g, :, :width]
    for c in range(spans):
        tok = pl.ds(pl.multiple_of((g * spans + c) * 64, 64), 64)
        row = slice(256 * c, 256 * c + 256)
        cols = [slice(HD * h, HD * h + HD) for h in range(heads)]
        scores = [dot(r.q[tok, col], r.keys[row, col], NT) for col in cols]
        gps = [dot(r.go[tok, col], r.values[row, col], NT) for col in cols]
        weights = [jnp.exp(s * scale) for s in scores]
        weights = [w / jnp.sum(w, axis=-1, keepdims=True) for w in weights]
        probs = [w.astype(jnp.bfloat16) for w in weights]
        mixed = [
            (w * (gp - jnp.sum(w * gp, axis=-1, keepdims=True)) * scale).astype(jnp.bfloat16)
            for w, gp in zip(weights, gps)
        ]
        for col, p, m in zip(cols, probs, mixed):
            r.ctx[tok, col] = dot(p, r.values[row, col]).astype(jnp.bfloat16)
            r.gq[tok, col] = dot(m, r.keys[row, col]).astype(jnp.bfloat16)
            gkeys[row, col] = dot(m, r.q[tok, col], TN).astype(jnp.bfloat16)
            gvalues[row, col] = dot(p, r.go[tok, col], TN).astype(jnp.bfloat16)


def weight_grads(r, g, size):
    width = r.wk.shape[1]

    @pl.when(g % 2 == 1)
    def _():
        pair = picked_rows(r, g - 1, 2 * size)
        gk = r.up_w[pl.ds(g - 1, 2), : size * 128].reshape(-1, width)
        gv = r.down_w[pl.ds(g - 1, 2), :, :width].reshape(-1, width)
        add_k = dot(pair, gk, TN)
        add_v = dot(pair, gv, TN)

        @pl.when(g == 1)
        def _():
            r.acc_k[...] = add_k
            r.acc_v[...] = add_v

        @pl.when(g > 1)
        def _():
            r.acc_k[...] += add_k
            r.acc_v[...] += add_v


def fused(
    queries,
    grad_ctx,
    neighbours,
    up_weight,
    down_weight,
    key_weight,
    value_weight,
    group_ids,
    slot_ids,
):
    feat, ffe = up_weight.shape
    requests = group_ids.shape[0] * group_ids.shape[1]
    tokens, width = queries.shape
    size = requests // STEPS
    bf, f32 = jnp.bfloat16, jnp.float32
    dma = pltpu.SemaphoreType.DMA
    slots = (GROUPS, CAP, 16, feat)
    chunk = (requests, 16, feat)
    block = (2 * feat // GROUPS, width // 2)
    any_, vmem, smem = (
        pl.BlockSpec(memory_space=s) for s in (pl.ANY, pltpu.VMEM, pltpu.SMEM)
    )
    ins = dict(
        queries=any_,
        grad_ctx=any_,
        neighbours=any_,
        up_weight=any_,
        down_weight=any_,
        key_weight=any_,
        value_weight=any_,
        group_ids=smem,
        slot_ids=smem,
    )
    outs = dict(
        context=(any_, queries.shape, bf),
        grad_query=(any_, queries.shape, bf),
        home=(vmem, (2, RETS, 16, feat), bf),
        gk_out=(vmem, (feat // GROUPS, width), f32),
        gv_out=(vmem, (feat // GROUPS, width), f32),
    )
    scratch = dict(
        wanted=pltpu.VMEM((8, 128), jnp.int32),
        source_v=pltpu.VMEM((8, 128), jnp.int32),
        source=pltpu.SMEM((8, 128), jnp.int32),
        position=pltpu.SMEM((requests,), jnp.int32),
        served=pltpu.VMEM((GROUPS, 8, 128), jnp.int32),
        served_s=pltpu.SMEM((GROUPS, 8, 128), jnp.int32),
        raw=pltpu.VMEM((2 * RETS, 16, feat), bf),
        normed=pltpu.VMEM((2 * RETS * 16, feat), bf),
        up_w=pltpu.VMEM((BLOCKS, feat, ffe // BLOCKS), bf),
        down_w=pltpu.VMEM((BLOCKS, ffe // BLOCKS, feat), bf),
        table=pltpu.VMEM((2 * RETS, 16, feat), bf),
        arrived=pltpu.VMEM((GROUPS, 2, 16, feat), bf),
        arrived_third=pltpu.VMEM((GROUPS, CAP - 2, 16, feat), bf),
        leaving=pltpu.VMEM(slots, bf),
        own=pltpu.VMEM(chunk, bf),
        picked=pltpu.VMEM((requests, RETS, 16, feat), bf),
        wk=pltpu.VMEM((feat, width), bf),
        wv=pltpu.VMEM((feat, width), bf),
        q=pltpu.VMEM(queries.shape, bf),
        go=pltpu.VMEM(queries.shape, bf),
        ctx=pltpu.VMEM(queries.shape, bf),
        gq=pltpu.VMEM(queries.shape, bf),
        keys=pltpu.VMEM((size * 128, width), bf),
        values=pltpu.VMEM((size * 128, width), bf),
        acc_k=pltpu.VMEM((feat, width), f32),
        acc_v=pltpu.VMEM((feat, width), f32),
        part=pltpu.VMEM((requests, SIDE, 2, 16, feat), bf),
        sib=pltpu.VMEM((SIDE,) + chunk, bf),
        far=pltpu.VMEM(chunk, bf),
        near_up=pltpu.VMEM(chunk, bf),
        near_down=pltpu.VMEM(chunk, bf),
        total=pltpu.VMEM(chunk, bf),
        arrived_b=pltpu.VMEM(slots, bf),
        gw=pltpu.VMEM((SIDE, SIDE, 2) + block, bf),
        w_in=pltpu.VMEM((2, SIDE, SIDE) + block, bf),
        w_half=pltpu.VMEM((2, SIDE) + block, bf),
        w_end=pltpu.VMEM((2, SIDE) + block, bf),
        pick=pltpu.VMEM((2 * RETS * 16, GROUPS * CAP * 16), bf),
        up_sem=dma,
        down_sem=dma,
        load_sem=dma((5,)),
        scalar_sem=dma((2,)),
        keep_sem=dma((STEPS,)),
        out_sem=dma((2,)),
    )
    for name, (send, recv) in dict(
        id=((), ()),
        raw=((), ()),
        seq=((2,), (2,)),
        up=((), (STEPS, 2)),
        dn=((), (STEPS, 2)),
        far=((), (STEPS,)),
        sib=((), (STEPS,)),
        swap=((2,), (2, STEPS)),
        rfar=((2,), (2, STEPS)),
        near=((2,), (2, STEPS)),
        w=((2, SIDE), (2, SIDE)),
        w2=((2, SIDE), (2, SIDE)),
        back=((2,), (2,)),
        home=((2,), (2,)),
    ).items():
        scratch[name + "_send"] = dma(send) if send else dma
        scratch[name + "_recv"] = dma(recv) if recv else dma
    names = tuple(ins) + tuple(outs) + tuple(scratch)
    return pl.pallas_call(
        functools.partial(kernel, names),
        out_shape=tuple(jax.ShapeDtypeStruct(s, t) for _, s, t in outs.values()),
        in_specs=list(ins.values()),
        out_specs=tuple(s for s, _, _ in outs.values()),
        scratch_shapes=list(scratch.values()),
        compiler_params=pltpu.CompilerParams(
            collective_id=0, has_side_effects=True, vmem_limit_bytes=60 * MIB
        ),
        name="fused",
    )(
        queries,
        grad_ctx,
        neighbours.reshape(2, RETS, 16, feat),
        up_weight,
        down_weight,
        key_weight,
        value_weight,
        group_ids,
        slot_ids,
    )


def deliver_kernel(*refs):
    count = len(refs) // 3
    sems = refs[-1]
    incoming = [
        pltpu.make_async_copy(refs[i], refs[2 * count + i], sems.at[0, i]) for i in range(count)
    ]
    outgoing = [
        pltpu.make_async_copy(refs[2 * count + i], refs[count + i], sems.at[1, i])
        for i in range(count)
    ]
    for copy in incoming:
        copy.start()
    for i in range(count):
        incoming[i].wait()
        outgoing[i].start()
    for copy in outgoing:
        copy.wait()


def deliver(arrays):
    any_ = pl.BlockSpec(memory_space=pl.ANY)
    return pl.pallas_call(
        deliver_kernel,
        out_shape=tuple(jax.ShapeDtypeStruct(a.shape, a.dtype) for a in arrays),
        in_specs=[any_] * len(arrays),
        out_specs=(any_,) * len(arrays),
        scratch_shapes=[pltpu.VMEM(a.shape, a.dtype) for a in arrays]
        + [pltpu.SemaphoreType.DMA((2, len(arrays)))],
        name="deliver",
    )(*arrays)


def body(
    queries,
    grad_ctx,
    neighbours,
    up_weight,
    down_weight,
    key_weight,
    value_weight,
    group_ids,
    slot_ids,
):
    context, grad_query, home, grad_key_w, grad_value_w = deliver(
        fused(
            queries,
            grad_ctx,
            neighbours,
            up_weight,
            down_weight,
            key_weight,
            value_weight,
            group_ids.T,
            slot_ids.T,
        )
    )
    return context, grad_query, home.reshape(neighbours.shape), grad_key_w, grad_value_w


def solution(mesh):
    return jax.shard_map(
        body,
        mesh=mesh,
        in_specs=(
            P("seq", "ret"),
            P("seq", "ret"),
            P(("seq", "ret"), None, None),
            P(),
            P(),
            P(None, "ret"),
            P(None, "ret"),
            P("seq", None),
            P("seq", None),
        ),
        out_specs=(
            P("seq", "ret"),
            P("seq", "ret"),
            P(("seq", "ret"), None, None),
            P("seq", "ret"),
            P("seq", "ret"),
        ),
        check_vma=False,
    )
```
